32 devices in a mesh: dp: 16 (over z, y, x), tp: 2 (over core).
Axes of the slice: x: 2, y: 2, z: 4, core: 2. Of those that a mesh axis runs over, the one named last changes fastest.
Arguments:
- tokens: bfloat16 [32768, 768], P(('dp', 'tp')), may hold values from -6 to 6
- cotangent: bfloat16 [32768, 768], P(('dp', 'tp')), may hold values from -6 to 6
- lengths: int32 [16, 8], P('dp'), may hold values from 0 to 2048, as said below
- qkv_weight: bfloat16 [768, 2304], P(('dp', 'tp')), may hold values from -0.21875 to 0.21875
- out_weight: bfloat16 [768, 768], P(('dp', 'tp')), may hold values from -0.21875 to 0.21875
- pre_gain: bfloat16 [768], P(('dp', 'tp')), may hold values from 0.25 to 1.75
- pre_shift: bfloat16 [768], P(('dp', 'tp')), may hold values from -2 to 2
- sub_gain: bfloat16 [768], P(('dp', 'tp')), may hold values from 0.25 to 1.75
- sub_shift: bfloat16 [768], P(('dp', 'tp')), may hold values from -2 to 2
- ffn_gain: bfloat16 [768], P(('dp', 'tp')), may hold values from 0.25 to 1.75
- ffn_shift: bfloat16 [768], P(('dp', 'tp')), may hold values from -2 to 2
- fc1_weight: bfloat16 [3072, 768], P(('dp', 'tp')), may hold values from -0.21875 to 0.21875
- mid_gain: bfloat16 [3072], P(('dp', 'tp')), may hold values from 0.25 to 1.75
- mid_shift: bfloat16 [3072], P(('dp', 'tp')), may hold values from -2 to 2
- fc2_weight: bfloat16 [3072, 768], P(('dp', 'tp')), may hold values from -0.109375 to 0.109375
Outputs:
- block_out: bfloat16 [32768, 768], P(('dp', 'tp'))
- grad_tokens: bfloat16 [32768, 768], P(('dp', 'tp'))
- grad_qkv: float32 [768, 2304], P(('dp', 'tp'))
- grad_out: float32 [768, 768], P(('dp', 'tp'))
- grad_pre_gain: float32 [768], P(('dp', 'tp'))
- grad_pre_shift: float32 [768], P(('dp', 'tp'))
- grad_sub_gain: float32 [768], P(('dp', 'tp'))
- grad_sub_shift: float32 [768], P(('dp', 'tp'))
- grad_ffn_gain: float32 [768], P(('dp', 'tp'))
- grad_ffn_shift: float32 [768], P(('dp', 'tp'))
- grad_fc1: float32 [3072, 768], P(('dp', 'tp'))
- grad_mid_gain: float32 [3072], P(('dp', 'tp'))
- grad_mid_shift: float32 [3072], P(('dp', 'tp'))
- grad_fc2: float32 [3072, 768], P(('dp', 'tp'))
The draws below stay inside these ranges and needn't reach their ends.
Inputs may be any that keep to these rules, and one draw needn't show every extreme that they name: `lengths`: each row lists one chip's sequences in the order they are packed; a row sums to 2048. Half of the chips, drawn from the seed, hold sequences of fewer than 512 tokens in which every two slots (0 and 1, 2 and 3, ...) sum to 512; the other half hold one sequence of more than 1024 tokens in slot 0, the rest of the rows in slot 1 (possibly 0), and zeros in the remaining slots.
All inputs are finite; a program needn't handle non-finite values.
Results may differ from the reference program's by a relative error of at most 0.012.
Values may be sent and summed in bfloat16 or wider, within the bound.
A program may use at most 192 MiB of HBM per device.

```python
import jax
import jax.numpy as jnp
from jax import lax

D = 768
HEADS = 12
HEAD_DIM = 64
FF = 3072
TOK_DEV = 1024
SLOTS = 8
CHIPS = 16
TOKENS = 32768


def draw_lengths(key, part):
    key = jax.random.fold_in(key, 11)
    order_key, long_key, cut_key = jax.random.split(key, 3)
    whole = 2 * TOK_DEV
    short = 4 * TOK_DEV // SLOTS
    order = jax.random.permutation(order_key, CHIPS)
    longer = order % 2 == 1
    leading = jax.random.randint(long_key, (CHIPS,), TOK_DEV + 1, whole + 1)
    leading = jnp.where(order == 1, whole, leading).astype(jnp.int32)
    long_rows = jnp.zeros((CHIPS, SLOTS), jnp.int32)
    long_rows = long_rows.at[:, 0].set(leading).at[:, 1].set(whole - leading)
    cuts = jax.random.randint(cut_key, (CHIPS, SLOTS // 2), 1, short).astype(jnp.int32)
    short_rows = jnp.stack([cuts, short - cuts], axis=2).reshape(CHIPS, SLOTS)
    return jnp.where(longer[:, None], long_rows, short_rows).astype(jnp.int32)


def spiked(values, key, source, target, shards_of, factor):
    def block_of(position):
        return (jnp.arange(values.shape[position]) // (values.shape[position] // shards_of)).reshape((-1,) + (1,) * (values.ndim - 1 - position))

    first = jax.random.permutation(key, shards_of)[block_of(target)]
    second = (block_of(target) + shards_of // 2) % shards_of
    return jnp.where((block_of(source) == first) | (block_of(source) == second), factor * values, values)


def steps_of(rng, shape, shards, low, top_value):
    def one(axis_at, shards_of):
        heights = jax.random.uniform(jax.random.fold_in(jax.random.fold_in(rng, 6), axis_at), (shards_of,), jnp.float32, low / len(shards), top_value / len(shards))
        return jnp.repeat(jnp.exp(heights), shape[axis_at] // shards_of).reshape((-1,) + (1,) * (len(shape) - axis_at - 1))

    gain = one(*shards[0])
    for cut in shards[1:]:
        gain = gain * one(*cut)
    return gain


def scatter_about(stream_key, dims, deviation, reach, pieces=(), kind=jnp.bfloat16):
    factor_of = steps_of(stream_key, dims, pieces, -0.22, 0.18) if pieces else 1.0
    values = jax.random.normal(stream_key, dims, jnp.float32) * deviation * factor_of
    return jnp.minimum(jnp.maximum(values, -reach), reach).astype(kind)


def gaussian_with(own_key, dims, width, limit, cuts, heavy, kind=jnp.bfloat16):
    values = width * jax.random.normal(own_key, dims, jnp.float32)
    if cuts:
        values = values * steps_of(own_key, dims, cuts, -0.22, 0.18)
    return jnp.clip(spiked(values, jax.random.fold_in(own_key, 3), *heavy), -limit, limit).astype(kind)


def setup_inputs(seed: int = 0) -> dict:
    splits = jax.random.split(jax.random.key(seed), 16)
    return {
        "tokens": gaussian_with(splits[0], (TOKENS, D), 1.0, 6.0, ((0, 32),), (0, 1, 32, 2.75)),
        "cotangent": scatter_about(splits[1], (TOKENS, D), 1.0, 6.0, ((0, 32),)),
        "lengths": draw_lengths(jax.random.fold_in(splits[15], 71), 0),
        "qkv_weight": scatter_about(splits[3], (D, 3 * D), D ** -0.5, 0.21875, ((0, 32),)),
        "out_weight": scatter_about(splits[4], (D, D), D ** -0.5, 0.21875, ((0, 32),)),
        "pre_gain": jnp.clip(1.0 + 0.15 * jax.random.normal(splits[5], (D,), jnp.float32), 0.25, 1.75).astype(jnp.bfloat16),
        "pre_shift": scatter_about(splits[6], (D,), 0.3, 2.0, ((0, 32),)),
        "sub_gain": jnp.clip(1.0 + 0.15 * jax.random.normal(splits[7], (D,), jnp.float32), 0.25, 1.75).astype(jnp.bfloat16),
        "sub_shift": scatter_about(splits[8], (D,), 0.3, 2.0, ((0, 32),)),
        "ffn_gain": jnp.clip(1.0 + 0.15 * jax.random.normal(splits[9], (D,), jnp.float32), 0.25, 1.75).astype(jnp.bfloat16),
        "ffn_shift": scatter_about(splits[10], (D,), 0.3, 2.0, ((0, 32),)),
        "fc1_weight": scatter_about(splits[11], (FF, D), D ** -0.5, 0.21875, ((0, 32),)),
        "mid_gain": jnp.clip(1.0 + 0.15 * jax.random.normal(splits[12], (FF,), jnp.float32), 0.25, 1.75).astype(jnp.bfloat16),
        "mid_shift": scatter_about(splits[13], (FF,), 0.3, 2.0, ((0, 32),)),
        "fc2_weight": scatter_about(splits[14], (FF, D), FF ** -0.5, 0.109375, ((0, 32),)),
    }


eps = 1e-05

@jax.custom_vjp
def low(v):
    return lax.optimization_barrier(v.astype(jnp.bfloat16)).astype(jnp.float32)

@jax.custom_vjp
def low_back(v):
    return v

def low_keep(v):
    return (low(v), None)

def low_pass(kept, grad):
    return (grad,)

def back_keep(v):
    return (v, None)

def back_low(kept, grad):
    return (low(grad),)
low.defvjp(low_keep, low_pass)
low_back.defvjp(back_keep, back_low)

def layer_norm(values, factor, offset):
    centre = values - lax.optimization_barrier(jnp.mean(values, axis=-1, keepdims=True))
    spread = lax.optimization_barrier(jnp.mean(centre * centre, axis=-1, keepdims=True))
    return centre * lax.rsqrt(spread + eps) * factor + offset

def gelu_exact(values):
    return jax.nn.gelu(values, approximate=False)

def chip_attention(operands):
    queries, keys, values, documents = operands
    highest = lax.Precision.HIGHEST
    scores = jnp.einsum('qhd,khd->hqk', queries, keys, precision=highest) * HEAD_DIM ** (-0.5)
    scores = low_back(scores)
    places = jnp.arange(queries.shape[0], dtype=jnp.int32)
    allowed = (documents[:, None] == documents[None, :]) & (places[None, :] <= places[:, None])
    scores = jnp.where(allowed[None], scores, -1e+30)
    weights = low(jax.nn.softmax(scores, axis=-1))
    return jnp.einsum('hqk,khd->qhd', weights, values, precision=highest)

def forward(inputs, qkv_weight, out_weight, pre_gain, pre_shift, sub_gain, sub_shift, ffn_gain, ffn_shift, fc1_weight, mid_gain, mid_shift, fc2_weight, documents):
    highest = lax.Precision.HIGHEST
    normed = low(layer_norm(inputs, pre_gain, pre_shift))
    projected = low(low_back(jnp.dot(normed, qkv_weight, precision=highest)))
    shaped = projected.reshape(CHIPS, 2 * TOK_DEV, 3, HEADS, HEAD_DIM)
    attended = lax.map(jax.checkpoint(chip_attention), (shaped[:, :, 0], shaped[:, :, 1], shaped[:, :, 2], documents))
    attended = low_back(attended.reshape(TOKENS, D))
    sub_normed = low(layer_norm(attended, sub_gain, sub_shift))
    branch = low_back(jnp.dot(sub_normed, out_weight, precision=highest))
    middle = inputs + branch
    ffn_normed = low(layer_norm(middle, ffn_gain, ffn_shift))
    pre_act = low_back(jnp.dot(ffn_normed, fc1_weight.T, precision=highest))
    activated = gelu_exact(pre_act)
    row_mean = lax.optimization_barrier(jnp.mean(activated, axis=-1, keepdims=True))
    spread = lax.optimization_barrier(jnp.mean(activated * activated, axis=-1, keepdims=True)) - row_mean * row_mean
    mid_out = low((activated - row_mean) * lax.rsqrt(spread + eps) * mid_gain + mid_shift)
    return middle + jnp.dot(mid_out, fc2_weight, precision=highest)

def reference(tokens, cotangent, lengths, qkv_weight, out_weight, pre_gain, pre_shift, sub_gain, sub_shift, ffn_gain, ffn_shift, fc1_weight, mid_gain, mid_shift, fc2_weight):
    bounds = jnp.cumsum(lengths, axis=1, dtype=jnp.int32)
    places = jnp.arange(2 * TOK_DEV, dtype=jnp.int32)
    documents = lax.optimization_barrier(jnp.sum((places[None, :, None] >= bounds[:, None, :]).astype(jnp.int32), axis=2, dtype=jnp.int32))
    floats = jax.tree.map(lambda tensor: tensor.astype(jnp.float32), (tokens, qkv_weight, out_weight, pre_gain, pre_shift, sub_gain, sub_shift, ffn_gain, ffn_shift, fc1_weight, mid_gain, mid_shift, fc2_weight))

    def wrapped(*operands):
        return forward(*operands, documents)
    result, pull = jax.vjp(wrapped, *floats)
    grads = pull(cotangent.astype(jnp.float32))
    return (result.astype(jnp.bfloat16), grads[0].astype(jnp.bfloat16), grads[1], grads[2], grads[3], grads[4], grads[5], grads[6], grads[7], grads[8], grads[9], grads[10], grads[11], grads[12])
```

```python
import functools

import jax
import jax.numpy as jnp
from jax import lax
from jax.experimental import pallas as pl
from jax.experimental.pallas import tpu as pltpu
from jax.sharding import PartitionSpec as P

f32, bf16 = jnp.float32, jnp.bfloat16
EPS = 1e-5
BIG = 1e30


def nt(a, b):
    return lax.dot_general(a, b, (((1,), (1,)), ((), ())), preferred_element_type=f32)


def nn(a, b):
    return lax.dot_general(a, b, (((1,), (0,)), ((), ())), preferred_element_type=f32)


def tn(a, b):
    return lax.dot_general(a, b, (((0,), (0,)), ((), ())), preferred_element_type=f32)

def doc_features(len_ref, rows, fq, fk):
    lane = lax.broadcasted_iota(jnp.int32, (1, 128), 1)
    lo = jnp.zeros((1, 128), jnp.int32); hi = jnp.zeros((1, 128), jnp.int32)
    run = jnp.int32(0)
    for d in range(8):
        nxt = run + len_ref[0, d]
        lo = jnp.where(lane == d, run, lo); hi = jnp.where(lane == d, nxt, hi)
        run = nxt
    def body(r, _):
        place = lax.broadcasted_iota(jnp.int32, (256, 128), 0) + r * 256
        hit = (place >= lo) & (place < hi)
        sl = pl.ds(pl.multiple_of(r * 256, 256), 256)
        fq[sl, :] = jnp.where(hit, 1.0, 0.0).astype(bf16)
        fk[sl, :] = jnp.where(hit | (lane >= 8), 0.0, -BIG).astype(bf16)
        return 0
    lax.fori_loop(0, rows // 256, body, 0)

def fwd_t(len_ref, qkv, o_ref, lse_ref, fq, fk, q2, st_s, m_s, l_s, acc, *, B, pairs, variant):
    rows = qkv.shape[0]; nb = rows // B; W = pairs * 128
    doc_features(len_ref, rows, fq, fk)
    half = lax.broadcasted_iota(jnp.int32, (1, 128), 1) < 64
    causal = lax.broadcasted_iota(jnp.int32, (B, B), 0) <= lax.broadcasted_iota(jnp.int32, (B, B), 1)
    causal = jnp.concatenate([causal, causal], axis=1)
    for p in range(pairs):
        def qstep(i, _, p=p):
            qs = pl.ds(pl.multiple_of(i * B, B), B)
            q = qkv[qs, p * 128:(p + 1) * 128] * bf16(0.125)
            fqb = fq[qs, :]
            z = jnp.zeros_like(q)
            q2[...] = jnp.concatenate([
                jnp.concatenate([jnp.where(half, q, z), fqb], axis=1),
                jnp.concatenate([jnp.where(half, z, q), fqb], axis=1)], axis=0)
            def score(j):
                ks = pl.ds(pl.multiple_of(j * B, B), B)
                k2 = jnp.concatenate([qkv[ks, W + p * 128:W + (p + 1) * 128], fk[ks, :]], axis=1)
                return nt(k2, q2[...])
            def vblk(j):
                ks = pl.ds(pl.multiple_of(j * B, B), B)
                return qkv[ks, 2 * W + p * 128:2 * W + (p + 1) * 128]
            if variant == "online":
                def block(j, masked, first):
                    s = score(j)
                    if masked: s = jnp.where(causal, s, -BIG)
                    mx = jnp.max(s, axis=0, keepdims=True)
                    if first: mn = mx
                    else:
                        mo = m_s[...]
                        mn = jnp.maximum(mo, mx); al = jnp.exp(mo - mn)
                    e = jnp.exp(s - mn)
                    su = jnp.sum(e, axis=0, keepdims=True)
                    pv = tn(vblk(j), e.astype(bf16))
                    if first: l_s[...] = su; acc[...] = pv
                    else: l_s[...] = l_s[...] * al + su; acc[...] = acc[...] * al + pv
                    m_s[...] = mn
                block(i, True, True)
                def kstep(j, _):
                    block(j, False, False); return 0
                lax.fori_loop(0, i, kstep, 0)
                m = m_s[...]; l = l_s[...]
            else:
                def part(s): return jnp.max(s.reshape(B // 8, 8, 2 * B), axis=0)
                s = jnp.where(causal, score(i), -BIG)
                st_s[i] = s
                def pass1(j, m8):
                    s = score(j); st_s[j] = s
                    return jnp.maximum(m8, part(s))
                m8 = lax.fori_loop(0, i, pass1, part(s))
                m = jnp.max(m8, axis=0, keepdims=True)
                acc[...] = jnp.zeros_like(acc)
                def pass2(j, l8):
                    e = jnp.exp(st_s[j] - m)
                    acc[...] += tn(vblk(j), e.astype(bf16))
                    return l8 + jnp.sum(e.reshape(B // 8, 8, 2 * B), axis=0)
                l8 = lax.fori_loop(0, i + 1, pass2, jnp.zeros((8, 2 * B), f32))
                l = jnp.sum(l8, axis=0, keepdims=True)
            r = 1.0 / l
            a = acc[...] * r
            ot = jnp.concatenate([a[:64, :B], a[64:, B:]], axis=0)
            o_ref[qs, p * 128:(p + 1) * 128] = ot.T.astype(o_ref.dtype)
            lse = m + jnp.log(l)
            lse_ref[2 * p:2 * p + 1, qs] = lse[:, :B]
            lse_ref[2 * p + 1:2 * p + 2, qs] = lse[:, B:]
            return 0
        lax.fori_loop(0, nb, qstep, 0)

def attn_fwd(lengths, qkv, B=256, variant="online"):
    rows, w3 = qkv.shape; W = w3 // 3; pairs = W // 128; nb = rows // B
    return pl.pallas_call(functools.partial(fwd_t, B=B, pairs=pairs, variant=variant), name="attn_fwd",
        out_shape=(jax.ShapeDtypeStruct((rows, W), bf16), jax.ShapeDtypeStruct((8, rows), f32)),
        in_specs=[pl.BlockSpec(memory_space=pltpu.SMEM), pl.BlockSpec(memory_space=pltpu.VMEM)],
        out_specs=(pl.BlockSpec(memory_space=pltpu.VMEM),) * 2,
        scratch_shapes=[pltpu.VMEM((rows, 128), bf16), pltpu.VMEM((rows, 128), bf16), pltpu.VMEM((2 * B, 256), bf16),
                        pltpu.VMEM((nb if variant != "online" else 1, B, 2 * B), f32),
                        pltpu.VMEM((1, 2 * B), f32), pltpu.VMEM((1, 2 * B), f32), pltpu.VMEM((128, 2 * B), f32)],
        compiler_params=pltpu.CompilerParams(vmem_limit_bytes=56 << 20))(lengths, qkv)

def bwd_kernel(len_ref, qkv, do_ref, lse_ref, dl_ref, out, fq, fk, q2, do2, dq, dk, dv, *, B, pairs, mode):
    rows = qkv.shape[0]; nb = rows // B; W = pairs * 128
    doc_features(len_ref, rows, fq, fk)
    half = lax.broadcasted_iota(jnp.int32, (1, 128), 1) < 64
    causal = lax.broadcasted_iota(jnp.int32, (B, B), 0) <= lax.broadcasted_iota(jnp.int32, (B, B), 1)
    causal = jnp.concatenate([causal, causal], axis=1)
    for p in range(pairs):
        def prep(i, _, p=p):
            qs = pl.ds(pl.multiple_of(i * B, B), B)
            q = qkv[qs, p * 128:(p + 1) * 128] * bf16(0.125)
            d = do_ref[qs, p * 128:(p + 1) * 128]
            fqb = fq[qs, :]
            z = jnp.zeros_like(q)
            q2[i] = jnp.concatenate([
                jnp.concatenate([jnp.where(half, q, z), fqb], axis=1),
                jnp.concatenate([jnp.where(half, z, q), fqb], axis=1)], axis=0)
            do2[i] = jnp.concatenate([jnp.where(half, d, z), jnp.where(half, z, d)], axis=0)
            dq[i] = jnp.zeros(dq.shape[1:], f32)
            return 0
        lax.fori_loop(0, nb, prep, 0)
        def kstep(j, _, p=p):
            ks = pl.ds(pl.multiple_of(j * B, B), B)
            kt = qkv[ks, W + p * 128:W + (p + 1) * 128]
            v = qkv[ks, 2 * W + p * 128:2 * W + (p + 1) * 128]
            k2 = jnp.concatenate([kt, fk[ks, :]], axis=1)
            def block(i, masked, first):
                qs = pl.ds(pl.multiple_of(i * B, B), B)
                lse = jnp.concatenate([lse_ref[2 * p:2 * p + 1, qs], lse_ref[2 * p + 1:2 * p + 2, qs]], axis=1)
                dl = jnp.concatenate([dl_ref[2 * p:2 * p + 1, qs], dl_ref[2 * p + 1:2 * p + 2, qs]], axis=1)
                qq = q2[i]; dd = do2[i]
                st = nt(k2, qq)
                pt = jnp.exp(st - lse)
                if masked: pt = jnp.where(causal, pt, 0.0)
                dp = nt(v, dd)
                ds = (pt * (dp - dl)).astype(bf16)
                dvp = nn(pt.astype(bf16), dd)
                dkp = nn(ds, qq[:, :128])
                if first: dv[...] = dvp; dk[...] = dkp
                else: dv[...] += dvp; dk[...] += dkp
                if mode == "tn":
                    dq[i] += tn(ds, kt)
                else:
                    dq[i] += tn(kt, ds)
            block(j, True, True)
            def qstep(i, _):
                block(i, False, False); return 0
            lax.fori_loop(j + 1, nb, qstep, 0)
            out[ks, W + p * 128:W + (p + 1) * 128] = dk[...].astype(bf16)
            out[ks, 2 * W + p * 128:2 * W + (p + 1) * 128] = dv[...].astype(bf16)
            return 0
        lax.fori_loop(0, nb, kstep, 0)
        def fin(i, _, p=p):
            qs = pl.ds(pl.multiple_of(i * B, B), B)
            if mode == "tn":
                d = dq[i]
                r = jnp.where(half, d[:B], d[B:])
            else:
                d = dq[i]
                r = jnp.concatenate([d[:64, :B], d[64:, B:]], axis=0).T
            out[qs, p * 128:(p + 1) * 128] = (r * 0.125).astype(bf16)
            return 0
        lax.fori_loop(0, nb, fin, 0)

def attn_bwd(lengths, qkv, do, lse, dl, B=256, mode="tn"):
    rows, w3 = qkv.shape; W = w3 // 3; pairs = W // 128; nb = rows // B
    dqs = (nb, 2 * B, 128) if mode == "tn" else (nb, 128, 2 * B)
    return pl.pallas_call(functools.partial(bwd_kernel, B=B, pairs=pairs, mode=mode), name="attn_bwd",
        out_shape=jax.ShapeDtypeStruct((rows, w3), bf16),
        in_specs=[pl.BlockSpec(memory_space=pltpu.SMEM)] + [pl.BlockSpec(memory_space=pltpu.VMEM)] * 4,
        out_specs=pl.BlockSpec(memory_space=pltpu.VMEM),
        scratch_shapes=[pltpu.VMEM((rows, 128), bf16), pltpu.VMEM((rows, 128), bf16), pltpu.VMEM((nb, 2 * B, 256), bf16),
                        pltpu.VMEM((nb, 2 * B, 128), bf16), pltpu.VMEM(dqs, f32), pltpu.VMEM((B, 128), f32), pltpu.VMEM((B, 128), f32)],
        compiler_params=pltpu.CompilerParams(vmem_limit_bytes=56 << 20))(lengths, qkv, do, lse, dl)

def stats(v):
    n = v.shape[-1]
    m = jnp.sum(v, axis=-1, keepdims=True) * (1.0 / n)
    c = v - m
    s = jnp.sum(c * c, axis=-1, keepdims=True) * (1.0 / n)
    r = lax.rsqrt(s + EPS)
    return c * r, r
def ln_back(w, vh, r, g):
    n = vh.shape[-1]
    wg = w * g
    a = jnp.sum(wg, axis=-1, keepdims=True) * (1.0 / n)
    b = jnp.sum(wg * vh, axis=-1, keepdims=True) * (1.0 / n)
    return r * (wg - a - vh * b)
def gelu_parts(h):
    e = jnp.exp(h * h * -0.5)
    d = 1.0 + jnp.abs(h) * 0.23164189
    t = pl.reciprocal(d, approx=True)
    t = t * (2.0 - d * t)
    y = t * (0.127414796 + t * (-0.142248368 + t * (0.710706870 + t * (-0.726576013 + t * 0.530702714))))
    q = y * e
    return jnp.where(h >= 0, 1.0 - q, q), e * 0.3989422804014327
def colsum(v): return jnp.sum(v, axis=0, keepdims=True)

def ffn_kernel(o_ref, x_ref, g_ref, gall_ref, wo, fc1, fc2, vec, mg, mb, sel,
               out_ref, dy_ref, do_ref, delta_ref, gwo, gfc1, gfc2, gvec, gmg, gmb,
               u_s, d_s, m_s, dh_s, c_s, b_s, db_s, e_s, *, T, NT, NC):
    step = pl.program_id(0)
    K = fc1.shape[1]
    ff = NC * K
    @pl.when(step < NT)
    def _():
        rs = pl.ds(pl.multiple_of(step * T, T), T)
        @pl.when(step == 0)
        def _():
            gvec[...] = jnp.zeros_like(gvec); gmg[...] = jnp.zeros_like(gmg); gmb[...] = jnp.zeros_like(gmb)
        sg, sb, fg, fb = [vec[k:k + 1, :] for k in range(4)]
        o = o_ref[...].astype(f32)
        oh, orr = stats(o)
        b = (oh * sg + sb).astype(bf16)
        b_s[rs, :] = b
        y = x_ref[...].astype(f32) + nn(b, wo[...])
        yh, yr = stats(y)
        cc = (yh * fg + fb).astype(bf16)
        c_s[rs, :] = cc
        g = g_ref[...]
        def pass_a(c, st):
            s1, s2 = st
            h = nt(c_s[rs, :], fc1[c])
            phi, den = gelu_parts(h)
            u = h * phi
            u_s[c] = u
            d_s[c] = phi + h * den
            return s1 + jnp.sum(u, axis=1, keepdims=True), s2 + jnp.sum(u * u, axis=1, keepdims=True)
        z1 = jnp.zeros((T, 1), f32)
        s1, s2 = lax.fori_loop(0, NC, pass_a, (z1, z1))
        mu = s1 * (1.0 / ff)
        R = lax.rsqrt(s2 * (1.0 / ff) - mu * mu + EPS)
        def pass_b(c, st):
            acc, se, seu = st
            uh = (u_s[c] - mu) * R
            u_s[c] = uh
            gain = mg[c]
            m = (uh * gain + mb[c]).astype(bf16)
            m_s[c, rs, :] = m
            acc = acc + nn(m, fc2[c])
            dm = nt(g_ref[...], fc2[c])
            t = dm * uh
            gmg[c] += colsum(t)
            gmb[c] += colsum(dm)
            e = dm * gain
            e_s[c] = e
            return acc, se + jnp.sum(e, axis=1, keepdims=True), seu + jnp.sum(e * uh, axis=1, keepdims=True)
        acc, se, seu = lax.fori_loop(0, NC, pass_b, (y, z1, z1))
        out_ref[...] = acc.astype(bf16)
        se = se * (1.0 / ff); seu = seu * (1.0 / ff)
        def pass_c(c, acc):
            dh = ((e_s[c] - se - u_s[c] * seu) * R * d_s[c]).astype(bf16)
            dh_s[c, rs, :] = dh
            return acc + nn(dh, fc1[c])
        dc = lax.fori_loop(0, NC, pass_c, jnp.zeros((T, fc1.shape[2]), f32))
        gvec[2:3] += colsum(dc * yh)
        gvec[3:4] += colsum(dc)
        dy = g.astype(f32) + ln_back(dc, yh, yr, fg)
        dy_ref[...] = dy
        db = dy.astype(bf16)
        db_s[rs, :] = db
        dbn = nt(db, wo[...])
        gvec[0:1] += colsum(dbn * oh)
        gvec[1:2] += colsum(dbn)
        do = ln_back(dbn, oh, orr, sg).astype(bf16)
        do_ref[...] = do
        pr = do.astype(f32) * o
        hi = pr.astype(bf16)
        lo = (pr - hi.astype(f32)).astype(bf16)
        delta_ref[...] = nt(sel[...], hi) + nt(sel[...], lo)
    @pl.when(step >= NT)
    def _():
        c = step - NT
        gfc2[0] = tn(m_s[c], gall_ref[...]).astype(bf16)
        gfc1[0] = tn(dh_s[c], c_s[...]).astype(bf16)
        @pl.when(step == NT)
        def _():
            gwo[...] = tn(b_s[...], db_s[...]).astype(bf16)

def ffn(o, x, g, wo, fc1, fc2, vec, mg, mb, T=256, K=512):
    rows, D = x.shape; ff = fc1.shape[0]; NC = ff // K; NT = rows // T
    head = jnp.arange(D)[None] // 64
    sel = (jnp.arange(16)[:, None] == head // (D // 128) * 8 + head % (D // 128)).astype(bf16)
    fc1 = fc1.reshape(NC, K, D); fc2 = fc2.reshape(NC, K, D)
    mg = mg.reshape(NC, 1, K); mb = mb.reshape(NC, 1, K)
    row = lambda s: (jnp.minimum(s, NT - 1), 0)
    cst2 = lambda s: (0, 0)
    cst3 = lambda s: (0, 0, 0)
    one = dict(pipeline_mode=pl.Buffered(1))
    chunk = lambda s: (jnp.maximum(s - NT, 0), 0, 0)
    return pl.pallas_call(functools.partial(ffn_kernel, T=T, NT=NT, NC=NC), name="ffn",
        grid=(NT + NC,),
        in_specs=[pl.BlockSpec((T, D), row), pl.BlockSpec((T, D), row), pl.BlockSpec((T, D), row),
                  pl.BlockSpec((rows, D), cst2, **one), pl.BlockSpec((D, D), cst2, **one),
                  pl.BlockSpec((NC, K, D), cst3, **one), pl.BlockSpec((NC, K, D), cst3, **one),
                  pl.BlockSpec((8, D), cst2, **one), pl.BlockSpec((NC, 1, K), cst3, **one), pl.BlockSpec((NC, 1, K), cst3, **one),
                  pl.BlockSpec((16, D), cst2, **one)],
        out_specs=[pl.BlockSpec((T, D), row), pl.BlockSpec((T, D), row), pl.BlockSpec((T, D), row),
                   pl.BlockSpec((16, T), lambda s: (0, jnp.minimum(s, NT - 1))),
                   pl.BlockSpec((D, D), cst2, **one), pl.BlockSpec((1, K, D), chunk), pl.BlockSpec((1, K, D), chunk),
                   pl.BlockSpec((8, D), cst2, **one), pl.BlockSpec((NC, 1, K), cst3, **one), pl.BlockSpec((NC, 1, K), cst3, **one)],
        out_shape=[jax.ShapeDtypeStruct((rows, D), bf16), jax.ShapeDtypeStruct((rows, D), f32), jax.ShapeDtypeStruct((rows, D), bf16),
                   jax.ShapeDtypeStruct((16, rows), f32), jax.ShapeDtypeStruct((D, D), bf16),
                   jax.ShapeDtypeStruct((NC, K, D), bf16), jax.ShapeDtypeStruct((NC, K, D), bf16),
                   jax.ShapeDtypeStruct((8, D), f32), jax.ShapeDtypeStruct((NC, 1, K), f32), jax.ShapeDtypeStruct((NC, 1, K), f32)],
        scratch_shapes=[pltpu.VMEM((NC, T, K), f32), pltpu.VMEM((NC, T, K), f32), pltpu.VMEM((NC, rows, K), bf16), pltpu.VMEM((NC, rows, K), bf16),
                        pltpu.VMEM((rows, D), bf16), pltpu.VMEM((rows, D), bf16), pltpu.VMEM((rows, D), bf16), pltpu.VMEM((NC, T, K), f32)],
        compiler_params=pltpu.CompilerParams(vmem_limit_bytes=62 << 20, dimension_semantics=("arbitrary",)))(
            o, x, g, g, wo, fc1, fc2, vec, mg, mb, sel)

def norm(v):
    return stats(v)


def local(tokens, cotangent, lengths, qkv_weight, out_weight, pre_gain, pre_shift, sub_gain, sub_shift,
          ffn_gain, ffn_shift, fc1_weight, mid_gain, mid_shift, fc2_weight):
    rows, D = tokens.shape
    W = D // 2
    tp = lax.axis_index("tp")
    both = ("dp", "tp")
    gather = lambda a: lax.all_gather(a, both, axis=0, tiled=True)
    small = gather(jnp.stack([pre_gain, pre_shift, sub_gain, sub_shift, ffn_gain, ffn_shift], axis=1)).astype(f32).T
    mid = gather(jnp.stack([mid_gain, mid_shift], axis=1)).astype(f32).T
    wq = gather(qkv_weight)
    wo, fc1, fc2 = gather(out_weight), gather(fc1_weight), gather(fc2_weight)
    wown = lax.dynamic_index_in_dim(wq.reshape(D, 3, 2, W), tp, 2, keepdims=False).reshape(D, 3 * W)
    x = tokens.astype(f32)
    xh, xr = norm(x)
    a = (xh * small[0] + small[1]).astype(bf16)
    afull = lax.all_gather(a, "tp", axis=0, tiled=True)
    qkv = nn(afull, wown).astype(bf16)
    o_own, lse = attn_fwd(lengths, qkv, B=512)
    o = lax.all_to_all(o_own, "tp", 0, 1, tiled=True)
    vec = jnp.concatenate([small[2:6], jnp.zeros((4, D), f32)], axis=0)
    block_out, dy, do, delta, gwo, gfc1, gfc2, gvec, gmg, gmb = ffn(o, tokens, cotangent, wo, fc1, fc2, vec, mid[0], mid[1])
    do_own = lax.all_to_all(do, "tp", 1, 0, tiled=True)
    dl_own = lax.all_to_all(delta, "tp", 0, 1, tiled=True)
    dqkv = attn_bwd(lengths, qkv, do_own, lse, dl_own, B=512)
    gq = tn(afull, dqkv)
    da = lax.psum_scatter(nt(dqkv, wown), "tp", scatter_dimension=0, tiled=True)
    grad_tokens = (dy + ln_back(da, xh, xr, small[0])).astype(bf16)
    scatter = lambda v: lax.psum_scatter(v, both, scatter_dimension=0, tiled=True)
    gq = lax.psum_scatter(gq, "dp", scatter_dimension=0, tiled=True)
    n = gq.shape[0] // 2
    gq = lax.all_to_all(gq.reshape(2, n, 3, 1, W), "tp", 0, 3, tiled=True).reshape(n, 3 * D)
    small_grads = scatter(jnp.concatenate([jnp.stack([colsum(da * xh)[0], colsum(da)[0]]), gvec[:4]], axis=0).T).T
    mid_grads = scatter(jnp.stack([gmg.reshape(-1), gmb.reshape(-1)], axis=1)).T
    gwo = scatter(gwo.astype(f32))
    gfc1 = scatter(gfc1.reshape(-1, D).astype(f32))
    gfc2 = scatter(gfc2.reshape(-1, D).astype(f32))
    return (block_out, grad_tokens, gq, gwo, small_grads[0], small_grads[1], small_grads[2], small_grads[3],
            small_grads[4], small_grads[5], gfc1, mid_grads[0], mid_grads[1], gfc2)


def solution(mesh):
    two, one = P(("dp", "tp"), None), P(("dp", "tp"))
    return jax.shard_map(
        local,
        mesh=mesh,
        in_specs=(two, two, P("dp", None), two, two, one, one, one, one, one, one, two, one, one, two),
        out_specs=(two, two, two, two, one, one, one, one, one, one, two, one, one, two),
        check_vma=False,
    )
```

```python
import functools

import jax
import jax.numpy as jnp
import numpy as np
from jax import lax
from jax.experimental import pallas as pl
from jax.experimental.pallas import tpu as pltpu
from jax.sharding import PartitionSpec as P

f32, bf16 = jnp.float32, jnp.bfloat16
EPS = 1e-5
BIG = 1e30


def nt(a, b):
    return lax.dot_general(a, b, (((1,), (1,)), ((), ())), preferred_element_type=f32)


def nn(a, b):
    return lax.dot_general(a, b, (((1,), (0,)), ((), ())), preferred_element_type=f32)


def tn(a, b):
    return lax.dot_general(a, b, (((0,), (0,)), ((), ())), preferred_element_type=f32)

def doc_features(len_ref, rows, fq, fk):
    lane = lax.broadcasted_iota(jnp.int32, (1, 128), 1)
    lo = jnp.zeros((1, 128), jnp.int32); hi = jnp.zeros((1, 128), jnp.int32)
    run = jnp.int32(0)
    for d in range(8):
        nxt = run + len_ref[0, d]
        lo = jnp.where(lane == d, run, lo); hi = jnp.where(lane == d, nxt, hi)
        run = nxt
    def body(r, _):
        place = lax.broadcasted_iota(jnp.int32, (256, 128), 0) + r * 256
        hit = (place >= lo) & (place < hi)
        sl = pl.ds(pl.multiple_of(r * 256, 256), 256)
        fq[sl, :] = jnp.where(hit, 1.0, 0.0).astype(bf16)
        fk[sl, :] = jnp.where(hit | (lane >= 8), 0.0, -BIG).astype(bf16)
        return 0
    lax.fori_loop(0, rows // 256, body, 0)

def fwd_t(len_ref, qkv, o_ref, lse_ref, fq, fk, q2, st_s, m_s, l_s, acc, *, B, pairs, variant):
    rows = qkv.shape[0]; nb = rows // B; W = pairs * 128
    doc_features(len_ref, rows, fq, fk)
    half = lax.broadcasted_iota(jnp.int32, (1, 128), 1) < 64
    causal = lax.broadcasted_iota(jnp.int32, (B, B), 0) <= lax.broadcasted_iota(jnp.int32, (B, B), 1)
    causal = jnp.concatenate([causal, causal], axis=1)
    for p in range(pairs):
        def qstep(i, _, p=p):
            qs = pl.ds(pl.multiple_of(i * B, B), B)
            q = qkv[qs, p * 128:(p + 1) * 128] * bf16(0.125)
            fqb = fq[qs, :]
            z = jnp.zeros_like(q)
            q2[...] = jnp.concatenate([
                jnp.concatenate([jnp.where(half, q, z), fqb], axis=1),
                jnp.concatenate([jnp.where(half, z, q), fqb], axis=1)], axis=0)
            def score(j):
                ks = pl.ds(pl.multiple_of(j * B, B), B)
                k2 = jnp.concatenate([qkv[ks, W + p * 128:W + (p + 1) * 128], fk[ks, :]], axis=1)
                return nt(k2, q2[...])
            def vblk(j):
                ks = pl.ds(pl.multiple_of(j * B, B), B)
                return qkv[ks, 2 * W + p * 128:2 * W + (p + 1) * 128]
            if variant == "online":
                def block(j, masked, first):
                    s = score(j)
                    if masked: s = jnp.where(causal, s, -BIG)
                    mx = jnp.max(s, axis=0, keepdims=True)
                    if first: mn = mx
                    else:
                        mo = m_s[...]
                        mn = jnp.maximum(mo, mx); al = jnp.exp(mo - mn)
                    e = jnp.exp(s - mn)
                    su = jnp.sum(e, axis=0, keepdims=True)
                    pv = tn(vblk(j), e.astype(bf16))
                    if first: l_s[...] = su; acc[...] = pv
                    else: l_s[...] = l_s[...] * al + su; acc[...] = acc[...] * al + pv
                    m_s[...] = mn
                block(i, True, True)
                def kstep(j, _):
                    block(j, False, False); return 0
                lax.fori_loop(0, i, kstep, 0)
                m = m_s[...]; l = l_s[...]
            else:
                def part(s): return jnp.max(s.reshape(B // 8, 8, 2 * B), axis=0)
                s = jnp.where(causal, score(i), -BIG)
                st_s[i] = s
                def pass1(j, m8):
                    s = score(j); st_s[j] = s
                    return jnp.maximum(m8, part(s))
                m8 = lax.fori_loop(0, i, pass1, part(s))
                m = jnp.max(m8, axis=0, keepdims=True)
                acc[...] = jnp.zeros_like(acc)
                def pass2(j, l8):
                    e = jnp.exp(st_s[j] - m)
                    acc[...] += tn(vblk(j), e.astype(bf16))
                    return l8 + jnp.sum(e.reshape(B // 8, 8, 2 * B), axis=0)
                l8 = lax.fori_loop(0, i + 1, pass2, jnp.zeros((8, 2 * B), f32))
                l = jnp.sum(l8, axis=0, keepdims=True)
            r = 1.0 / l
            a = acc[...] * r
            ot = jnp.concatenate([a[:64, :B], a[64:, B:]], axis=0)
            o_ref[qs, p * 128:(p + 1) * 128] = ot.T.astype(o_ref.dtype)
            lse = m + jnp.log(l)
            lse_ref[2 * p:2 * p + 1, qs] = lse[:, :B]
            lse_ref[2 * p + 1:2 * p + 2, qs] = lse[:, B:]
            return 0
        lax.fori_loop(0, nb, qstep, 0)

def attn_fwd(lengths, qkv, B=256, variant="online"):
    rows, w3 = qkv.shape; W = w3 // 3; pairs = W // 128; nb = rows // B
    return pl.pallas_call(functools.partial(fwd_t, B=B, pairs=pairs, variant=variant), name="attn_fwd",
        out_shape=(jax.ShapeDtypeStruct((rows, W), bf16), jax.ShapeDtypeStruct((8, rows), f32)),
        in_specs=[pl.BlockSpec(memory_space=pltpu.SMEM), pl.BlockSpec(memory_space=pltpu.VMEM)],
        out_specs=(pl.BlockSpec(memory_space=pltpu.VMEM),) * 2,
        scratch_shapes=[pltpu.VMEM((rows, 128), bf16), pltpu.VMEM((rows, 128), bf16), pltpu.VMEM((2 * B, 256), bf16),
                        pltpu.VMEM((nb if variant != "online" else 1, B, 2 * B), f32),
                        pltpu.VMEM((1, 2 * B), f32), pltpu.VMEM((1, 2 * B), f32), pltpu.VMEM((128, 2 * B), f32)],
        compiler_params=pltpu.CompilerParams(vmem_limit_bytes=56 << 20))(lengths, qkv)

def bwd_kernel(len_ref, qkv, do_ref, lse_ref, dl_ref, out, fq, fk, q2, do2, dq, dk, dv, *, B, pairs, mode):
    rows = qkv.shape[0]; nb = rows // B; W = pairs * 128
    doc_features(len_ref, rows, fq, fk)
    half = lax.broadcasted_iota(jnp.int32, (1, 128), 1) < 64
    causal = lax.broadcasted_iota(jnp.int32, (B, B), 0) <= lax.broadcasted_iota(jnp.int32, (B, B), 1)
    causal = jnp.concatenate([causal, causal], axis=1)
    for p in range(pairs):
        def prep(i, _, p=p):
            qs = pl.ds(pl.multiple_of(i * B, B), B)
            q = qkv[qs, p * 128:(p + 1) * 128] * bf16(0.125)
            d = do_ref[qs, p * 128:(p + 1) * 128]
            fqb = fq[qs, :]
            z = jnp.zeros_like(q)
            q2[i] = jnp.concatenate([
                jnp.concatenate([jnp.where(half, q, z), fqb], axis=1),
                jnp.concatenate([jnp.where(half, z, q), fqb], axis=1)], axis=0)
            do2[i] = jnp.concatenate([jnp.where(half, d, z), jnp.where(half, z, d)], axis=0)
            dq[i] = jnp.zeros(dq.shape[1:], f32)
            return 0
        lax.fori_loop(0, nb, prep, 0)
        def kstep(j, _, p=p):
            ks = pl.ds(pl.multiple_of(j * B, B), B)
            kt = qkv[ks, W + p * 128:W + (p + 1) * 128]
            v = qkv[ks, 2 * W + p * 128:2 * W + (p + 1) * 128]
            k2 = jnp.concatenate([kt, fk[ks, :]], axis=1)
            def block(i, masked, first):
                qs = pl.ds(pl.multiple_of(i * B, B), B)
                lse = jnp.concatenate([lse_ref[2 * p:2 * p + 1, qs], lse_ref[2 * p + 1:2 * p + 2, qs]], axis=1)
                dl = jnp.concatenate([dl_ref[2 * p:2 * p + 1, qs], dl_ref[2 * p + 1:2 * p + 2, qs]], axis=1)
                qq = q2[i]; dd = do2[i]
                st = nt(k2, qq)
                pt = jnp.exp(st - lse)
                if masked: pt = jnp.where(causal, pt, 0.0)
                dp = nt(v, dd)
                ds = (pt * (dp - dl)).astype(bf16)
                dvp = nn(pt.astype(bf16), dd)
                dkp = nn(ds, qq[:, :128])
                if first: dv[...] = dvp; dk[...] = dkp
                else: dv[...] += dvp; dk[...] += dkp
                if mode == "tn":
                    dq[i] += tn(ds, kt)
                else:
                    dq[i] += tn(kt, ds)
            block(j, True, True)
            def qstep(i, _):
                block(i, False, False); return 0
            lax.fori_loop(j + 1, nb, qstep, 0)
            out[ks, W + p * 128:W + (p + 1) * 128] = dk[...].astype(bf16)
            out[ks, 2 * W + p * 128:2 * W + (p + 1) * 128] = dv[...].astype(bf16)
            return 0
        lax.fori_loop(0, nb, kstep, 0)
        def fin(i, _, p=p):
            qs = pl.ds(pl.multiple_of(i * B, B), B)
            if mode == "tn":
                d = dq[i]
                r = jnp.where(half, d[:B], d[B:])
            else:
                d = dq[i]
                r = jnp.concatenate([d[:64, :B], d[64:, B:]], axis=0).T
            out[qs, p * 128:(p + 1) * 128] = (r * 0.125).astype(bf16)
            return 0
        lax.fori_loop(0, nb, fin, 0)

def attn_bwd(lengths, qkv, do, lse, dl, B=256, mode="tn"):
    rows, w3 = qkv.shape; W = w3 // 3; pairs = W // 128; nb = rows // B
    dqs = (nb, 2 * B, 128) if mode == "tn" else (nb, 128, 2 * B)
    return pl.pallas_call(functools.partial(bwd_kernel, B=B, pairs=pairs, mode=mode), name="attn_bwd",
        out_shape=jax.ShapeDtypeStruct((rows, w3), bf16),
        in_specs=[pl.BlockSpec(memory_space=pltpu.SMEM)] + [pl.BlockSpec(memory_space=pltpu.VMEM)] * 4,
        out_specs=pl.BlockSpec(memory_space=pltpu.VMEM),
        scratch_shapes=[pltpu.VMEM((rows, 128), bf16), pltpu.VMEM((rows, 128), bf16), pltpu.VMEM((nb, 2 * B, 256), bf16),
                        pltpu.VMEM((nb, 2 * B, 128), bf16), pltpu.VMEM(dqs, f32), pltpu.VMEM((B, 128), f32), pltpu.VMEM((B, 128), f32)],
        compiler_params=pltpu.CompilerParams(vmem_limit_bytes=56 << 20))(lengths, qkv, do, lse, dl)

def stats(v):
    n = v.shape[-1]
    m = jnp.sum(v, axis=-1, keepdims=True) * (1.0 / n)
    c = v - m
    s = jnp.sum(c * c, axis=-1, keepdims=True) * (1.0 / n)
    r = lax.rsqrt(s + EPS)
    return c * r, r
def ln_back(w, vh, r, g):
    n = vh.shape[-1]
    wg = w * g
    a = jnp.sum(wg, axis=-1, keepdims=True) * (1.0 / n)
    b = jnp.sum(wg * vh, axis=-1, keepdims=True) * (1.0 / n)
    return r * (wg - a - vh * b)
def gelu_parts(h):
    e = jnp.exp(h * h * -0.5)
    d = 1.0 + jnp.abs(h) * 0.23164189
    t = pl.reciprocal(d, approx=True)
    t = t * (2.0 - d * t)
    y = t * (0.127414796 + t * (-0.142248368 + t * (0.710706870 + t * (-0.726576013 + t * 0.530702714))))
    q = y * e
    return jnp.where(h >= 0, 1.0 - q, q), e * 0.3989422804014327
def colsum(v): return jnp.sum(v, axis=0, keepdims=True)

def ffn_kernel(o_ref, x_ref, g_ref, gall_ref, wo, fc1, fc2, vec, mid, sel,
               out_ref, dy_ref, do_ref, delta_ref, gwo, gfc1, gfc2, gvec, gmid,
               u_s, d_s, m_s, dh_s, c_s, b_s, db_s, e_s, *, T, NT, NC):
    step = pl.program_id(0)
    K = fc1.shape[1]
    ff = NC * K
    @pl.when(step < NT)
    def _():
        rs = pl.ds(pl.multiple_of(step * T, T), T)
        @pl.when(step == 0)
        def _():
            gvec[...] = jnp.zeros_like(gvec); gmid[...] = jnp.zeros_like(gmid)
        sg, sb, fg, fb = [vec[k:k + 1, :] for k in range(2, 6)]
        o = o_ref[...].astype(f32)
        oh, orr = stats(o)
        b = (oh * sg + sb).astype(bf16)
        b_s[rs, :] = b
        y = x_ref[...].astype(f32) + nn(b, wo[...])
        yh, yr = stats(y)
        cc = (yh * fg + fb).astype(bf16)
        c_s[rs, :] = cc
        g = g_ref[...]
        def pass_a(c, st):
            s1, s2 = st
            h = nt(c_s[rs, :], fc1[c])
            phi, den = gelu_parts(h)
            u = h * phi
            u_s[c] = u
            d_s[c] = phi + h * den
            return s1 + jnp.sum(u, axis=1, keepdims=True), s2 + jnp.sum(u * u, axis=1, keepdims=True)
        z1 = jnp.zeros((T, 1), f32)
        s1, s2 = lax.fori_loop(0, NC, pass_a, (z1, z1))
        mu = s1 * (1.0 / ff)
        R = lax.rsqrt(s2 * (1.0 / ff) - mu * mu + EPS)
        def pass_b(c, st):
            acc, se, seu = st
            uh = (u_s[c] - mu) * R
            u_s[c] = uh
            lanes = pl.ds(pl.multiple_of(c * K, K), K)
            gain = mid[0:1, lanes]
            m = (uh * gain + mid[1:2, lanes]).astype(bf16)
            m_s[c, rs, :] = m
            acc = acc + nn(m, fc2[c])
            dm = nt(g_ref[...], fc2[c])
            t = dm * uh
            gmid[6:7, lanes] += colsum(t)
            gmid[7:8, lanes] += colsum(dm)
            e = dm * gain
            e_s[c] = e
            return acc, se + jnp.sum(e, axis=1, keepdims=True), seu + jnp.sum(e * uh, axis=1, keepdims=True)
        acc, se, seu = lax.fori_loop(0, NC, pass_b, (y, z1, z1))
        out_ref[...] = acc.astype(bf16)
        se = se * (1.0 / ff); seu = seu * (1.0 / ff)
        def pass_c(c, acc):
            dh = ((e_s[c] - se - u_s[c] * seu) * R * d_s[c]).astype(bf16)
            dh_s[c, rs, :] = dh
            return acc + nn(dh, fc1[c])
        dc = lax.fori_loop(0, NC, pass_c, jnp.zeros((T, fc1.shape[2]), f32))
        gvec[4:5, :] += colsum(dc * yh)
        gvec[5:6, :] += colsum(dc)
        dy = g.astype(f32) + ln_back(dc, yh, yr, fg)
        db = dy.astype(bf16)
        dy_ref[...] = db
        db_s[rs, :] = db
        dbn = nt(db, wo[...])
        gvec[2:3, :] += colsum(dbn * oh)
        gvec[3:4, :] += colsum(dbn)
        do = ln_back(dbn, oh, orr, sg).astype(bf16)
        do_ref[...] = do
        pr = do.astype(f32) * o
        hi = pr.astype(bf16)
        lo = (pr - hi.astype(f32)).astype(bf16)
        delta_ref[...] = nt(sel[...], hi) + nt(sel[...], lo)
    @pl.when(step >= NT)
    def _():
        c = step - NT
        gfc2[0] = tn(m_s[c], gall_ref[...]).astype(bf16)
        gfc1[0] = tn(dh_s[c], c_s[...]).astype(bf16)
        @pl.when(step == NT)
        def _():
            gwo[...] = tn(b_s[...], db_s[...]).astype(bf16)

def ffn(o, x, g, wo, fc1, fc2, vec, mid, T=256, K=512):
    rows, D = x.shape; ff = fc1.shape[0]; NC = ff // K; NT = rows // T
    head = np.arange(D)[None] // 64
    sel = jnp.asarray((np.arange(16)[:, None] == head // (D // 128) * 8 + head % (D // 128)).astype(np.float32), bf16)
    fc1 = fc1.reshape(NC, K, D); fc2 = fc2.reshape(NC, K, D)
    row = lambda s: (jnp.minimum(s, NT - 1), 0)
    cst2 = lambda s: (0, 0)
    cst3 = lambda s: (0, 0, 0)
    one = dict(pipeline_mode=pl.Buffered(1))
    chunk = lambda s: (jnp.maximum(s - NT, 0), 0, 0)
    return pl.pallas_call(functools.partial(ffn_kernel, T=T, NT=NT, NC=NC), name="ffn",
        grid=(NT + NC,),
        in_specs=[pl.BlockSpec((T, D), row), pl.BlockSpec((T, D), row), pl.BlockSpec((T, D), row),
                  pl.BlockSpec((rows, D), cst2, **one), pl.BlockSpec((D, D), cst2, **one),
                  pl.BlockSpec((NC, K, D), cst3, **one), pl.BlockSpec((NC, K, D), cst3, **one),
                  pl.BlockSpec((8, D), cst2, **one), pl.BlockSpec((8, ff), cst2, **one),
                  pl.BlockSpec((16, D), cst2, **one)],
        out_specs=[pl.BlockSpec((T, D), row), pl.BlockSpec((T, D), row), pl.BlockSpec((T, D), row),
                   pl.BlockSpec((16, T), lambda s: (0, jnp.minimum(s, NT - 1))),
                   pl.BlockSpec((D, D), cst2, **one), pl.BlockSpec((1, K, D), chunk), pl.BlockSpec((1, K, D), chunk),
                   pl.BlockSpec((8, D), cst2, **one), pl.BlockSpec((8, ff), cst2, **one)],
        out_shape=[jax.ShapeDtypeStruct((rows, D), bf16), jax.ShapeDtypeStruct((rows, D), bf16), jax.ShapeDtypeStruct((rows, D), bf16),
                   jax.ShapeDtypeStruct((16, rows), f32), jax.ShapeDtypeStruct((D, D), bf16),
                   jax.ShapeDtypeStruct((NC, K, D), bf16), jax.ShapeDtypeStruct((NC, K, D), bf16),
                   jax.ShapeDtypeStruct((8, D), f32), jax.ShapeDtypeStruct((8, ff), f32)],
        scratch_shapes=[pltpu.VMEM((NC, T, K), f32), pltpu.VMEM((NC, T, K), f32), pltpu.VMEM((NC, rows, K), bf16), pltpu.VMEM((NC, rows, K), bf16),
                        pltpu.VMEM((rows, D), bf16), pltpu.VMEM((rows, D), bf16), pltpu.VMEM((rows, D), bf16), pltpu.VMEM((NC, T, K), f32)],
        compiler_params=pltpu.CompilerParams(vmem_limit_bytes=62 << 20, dimension_semantics=("arbitrary",)))(
            o, x, g, g, wo, fc1, fc2, vec, mid, sel)

MESH = pl.DeviceIdType.MESH

def place():
    dp, tp = lax.axis_index("dp"), lax.axis_index("tp")
    q, z = dp % 4, dp // 4
    dx = 1 - 2 * (dp % 2)
    dy = 2 - 4 * ((dp // 2) % 2)
    a, b = (1 - tp) * dx + tp * dy, tp * dx + (1 - tp) * dy
    return dict(dp=dp, tp=tp, z=z, q=q, qa=q + a, qb=q + b, qab=q + a + b,
                a=(dp + a, tp), b=(dp + b, tp), peer=(dp, 1 - tp),
                zs=[((dp + 4 * k) % 16, tp) for k in (1, 2, 3)], zi=[(z + k) % 4 for k in (1, 2, 3)])

def enter(w):
    bar = pltpu.get_barrier_semaphore()
    for d in [w["a"], w["b"], w["peer"]] + w["zs"]:
        pl.semaphore_signal(bar, inc=1, device_id=d, device_id_type=MESH)
    pl.semaphore_wait(bar, 6)

class Sender:
    def __init__(self, ss, rs):
        self.ss, self.rs, self.n, self.all = ss, rs, 0, []
    def __call__(self, src, dst, dev):
        c = pltpu.make_async_remote_copy(src_ref=src, dst_ref=dst, send_sem=self.ss.at[self.n], recv_sem=self.rs.at[self.n],
                                         device_id=dev, device_id_type=MESH)
        self.n += 1
        self.all.append(c)
        c.start()
        return c

class Gather:
    def __init__(self, send, w, src, slot, view, peer):
        self.send, self.w, self.src, self.slot, self.view, self.peer = send, w, src, slot, view, peer
    def plan(self):
        pass
    def start(self):
        w = self.w
        s = self.slot(w["z"], w["q"], w["tp"])
        self.cz = [self.send(self.src, s, d) for d in w["zs"]]
    def _fan(self, q, devs):
        v = self.view(q, self.w["tp"])
        return [self.send(v, v, d) for d in devs]
    def after_z(self):
        w = self.w
        for c in self.cz: c.wait_recv()
        devs = [w["a"], w["b"]] + ([w["peer"]] if self.peer else [])
        self.c1 = self._fan(w["q"], devs)
    def after_a(self):
        w = self.w
        self.c1[0].wait_recv()
        self.c2 = self._fan(w["qa"], [w["b"]] + ([w["peer"]] if self.peer else []))
    def after_b(self):
        w = self.w
        self.c1[1].wait_recv(); self.c2[0].wait_recv()
        self.c3 = []
        if self.peer:
            self.c3 = self._fan(w["qb"], [w["peer"]]) + self._fan(w["qab"], [w["peer"]])
    def finish(self):
        if self.peer:
            self.c1[2].wait_recv(); self.c2[1].wait_recv()
            for c in self.c3: c.wait_recv()

N_COPIES = 64

def k12_kernel(len_ref, tok, wq, wos, vpk, e24, e96, rsel, fc1s, fc2s,
               afull, qkv, wown, o_out, lse_ref, vec, mid, wo_h, fc1_h, fc2_h,
               xp, vbuf, sb, rb, woc, o_loc, fq, fk, q2, m_s, l_s, acc, ss, rs, ls, *, B, pairs, stage=9):
    w = place()
    tp = w["tp"]
    rows, D = tok.shape
    W = pairs * 128
    send = Sender(ss, rs)
    first = tp == 0
    sb[...] = jnp.zeros_like(sb)
    pick = lambda c0, n: (jnp.where(first, wq[:, c0:c0 + W], wq[:, c0 + W:c0 + 2 * W]).astype(bf16),
                          jnp.where(first, wq[:, c0 + W:c0 + 2 * W], wq[:, c0:c0 + W]).astype(bf16))
    mine = []
    for k in range(3):
        own, oth = pick(k * D, W)
        mine.append(own); sb[0:24, k * W:(k + 1) * W] = oth
    own_o = jnp.where(first, wos[:, :W], wos[:, W:])
    sb[0:24, 3 * W:4 * W] = jnp.where(first, wos[:, W:], wos[:, :W])
    vbuf[w["z"], w["q"], tp] = vpk[...]
    loc = [pltpu.make_async_copy(fc1s, fc1_h.at[w["z"], w["q"], tp], ls.at[0]),
           pltpu.make_async_copy(fc2s, fc2_h.at[w["z"], w["q"], tp], ls.at[1])]
    for c in loc: c.start()
    enter(w)
    cpre = send(sb, rb, w["peer"])
    gv = Gather(send, w, vbuf.at[w["z"], w["q"], tp], lambda z, q, t: vbuf.at[z, q, t], lambda q, t: vbuf.at[:, q, t], True)
    gv.start()
    cx = send(tok, xp, w["peer"])
    cpre.wait_recv()
    other = rb[0:24, :].astype(f32)
    me = jnp.concatenate(mine + [own_o], axis=1).astype(f32)
    both = jnp.concatenate([jnp.where(first, me, other), jnp.where(first, other, me)], axis=0).astype(bf16)
    wown[w["z"], w["q"]] = both[:, :3 * W]
    woc[...] = both[:, 3 * W:]
    gq = Gather(send, w, wown.at[w["z"], w["q"]], lambda z, q, t: wown.at[z, q], lambda q, t: wown.at[:, q], False)
    gq.start()
    cols = pl.ds(pl.multiple_of(tp * W, 128), W)
    lw = pltpu.make_async_copy(woc, wo_h.at[w["z"], w["q"], :, cols], ls.at[2])
    lw.start()
    gv.after_z(); gv.after_a(); gv.after_b(); gv.finish()
    small = nn(rsel[...], vbuf[...].reshape(512, 128)).astype(bf16)
    dev = lax.broadcasted_iota(jnp.int32, (32, 1), 0)
    lane = lax.broadcasted_iota(jnp.int32, (1, D), 1)
    hit = (lane >= dev * 24) & (lane < dev * 24 + 24)
    for v in range(6):
        vec[v:v + 1, :] = colsum(jnp.where(hit, nn(small[v * 32:(v + 1) * 32], e24[...]), 0.0))
    vec[6:8, :] = jnp.zeros((2, D), f32)
    lane = lax.broadcasted_iota(jnp.int32, (1, 4 * D), 1)
    hit = (lane >= dev * 96) & (lane < dev * 96 + 96)
    for v in range(2):
        mid[v:v + 1, :] = colsum(jnp.where(hit, nn(small[(6 + v) * 32:(7 + v) * 32], e96[...]), 0.0))
    mid[2:8, :] = jnp.zeros((6, 4 * D), f32)
    gq.after_z()
    for c in loc: c.wait()
    lw.wait()
    go = Gather(send, w, woc, lambda z, q, t: wo_h.at[z, q, :, cols], lambda q, t: wo_h.at[:, q, :, cols], True)
    g1 = Gather(send, w, fc1s, lambda z, q, t: fc1_h.at[z, q, t], lambda q, t: fc1_h.at[:, q, t], True)
    g2 = Gather(send, w, fc2s, lambda z, q, t: fc2_h.at[z, q, t], lambda q, t: fc2_h.at[:, q, t], True)
    go.start(); g1.start()
    def normed(src, base):
        def body(r, _):
            sl = pl.ds(pl.multiple_of(r * 256, 256), 256)
            xh, _r = stats(src[sl, :].astype(f32))
            afull[pl.ds(pl.multiple_of(base + r * 256, 256), 256), :] = (xh * vec[0:1, :] + vec[1:2, :]).astype(bf16)
            return 0
        lax.fori_loop(0, rows // 256, body, 0)
    normed(tok, tp * rows)
    gq.after_a()
    cx.wait_recv()
    normed(xp, (1 - tp) * rows)
    doc_features(len_ref, 2 * rows, fq, fk)
    gq.after_b()
    wfull = lambda: wown[...].reshape(D, 3 * W)
    def proj(r, _):
        sl = pl.ds(pl.multiple_of(r * 512, 512), 512)
        qkv[sl, :] = nn(afull[sl, :], wfull()).astype(bf16)
        return 0
    lax.fori_loop(0, 2 * rows // 512, proj, 0)
    nb = 2 * rows // B
    half = lax.broadcasted_iota(jnp.int32, (1, 128), 1) < 64
    causal = lax.broadcasted_iota(jnp.int32, (B, B), 0) <= lax.broadcasted_iota(jnp.int32, (B, B), 1)
    causal = jnp.concatenate([causal, causal], axis=1)
    def unit(u, _):
        p, i = u // nb, u % nb
        qs = pl.ds(pl.multiple_of(i * B, B), B)
        lanes = lambda k: pl.ds(pl.multiple_of(k * W + p * 128, 128), 128)
        q = qkv[qs, lanes(0)] * bf16(0.125)
        fqb = fq[qs, :]
        z = jnp.zeros_like(q)
        q2[...] = jnp.concatenate([
            jnp.concatenate([jnp.where(half, q, z), fqb], axis=1),
            jnp.concatenate([jnp.where(half, z, q), fqb], axis=1)], axis=0)
        def block(j, diag):
            ks = pl.ds(pl.multiple_of(j * B, B), B)
            s = nt(jnp.concatenate([qkv[ks, lanes(1)], fk[ks, :]], axis=1), q2[...])
            if diag: s = jnp.where(causal, s, -BIG)
            mn = jnp.max(s, axis=0, keepdims=True)
            if not diag:
                mo = m_s[...]
                mn = jnp.maximum(mo, mn); al = jnp.exp(mo - mn)
            e = jnp.exp(s - mn)
            su = jnp.sum(e, axis=0, keepdims=True)
            pv = tn(qkv[ks, lanes(2)], e.astype(bf16))
            if diag: l_s[...] = su; acc[...] = pv
            else: l_s[...] = l_s[...] * al + su; acc[...] = acc[...] * al + pv
            m_s[...] = mn
        block(i, True)
        def kstep(j, _):
            block(j, False); return 0
        lax.fori_loop(0, i, kstep, 0)
        l = l_s[...]
        a = acc[...] * (1.0 / l)
        ot = jnp.concatenate([a[:64, :B], a[64:, B:]], axis=0)
        o_loc[qs, pl.ds(pl.multiple_of(p * 128, 128), 128)] = ot.T.astype(bf16)
        lse = m_s[...] + jnp.log(l)
        lse_ref[p, 0:1, qs] = lse[:, :B]
        lse_ref[p, 1:2, qs] = lse[:, B:]
        return 0
    def units(lo, hi):
        lax.fori_loop(lo, hi, unit, 0)
    co = []
    def share(p):
        src = o_loc.at[pl.ds(pl.multiple_of((1 - tp) * rows, rows), rows), p * 128:(p + 1) * 128]
        co.append(send(src, o_out.at[:, pl.ds(pl.multiple_of(tp * W + p * 128, 128), 128)], w["peer"]))
    go.after_z(); g1.after_z(); g2.start()
    units(0, 3)
    go.after_a(); g1.after_a()
    units(3, 4); share(0)
    units(4, 6)
    go.after_b(); g1.after_b(); g2.after_z()
    units(6, 8); share(1)
    g2.after_a()
    units(8, 11)
    g2.after_b()
    units(11, 12); share(2)
    o_out[:, cols] = o_loc[pl.ds(pl.multiple_of(tp * rows, rows), rows), :]
    for c in co: c.wait_recv()
    go.finish(); g1.finish(); g2.finish()
    for c in send.all: c.wait_send()

def consts_np(D):
    k = np.arange(128)[:, None]
    e24 = (np.arange(D)[None] % 24 == k).astype(np.float32)
    e96 = (np.arange(4 * D)[None] % 96 == k).astype(np.float32)
    r = np.arange(256)[:, None]
    rsel = (np.arange(512)[None] == (r % 32) * 16 + r // 32).astype(np.float32)
    return e24, e96, rsel

def consts(D):
    return [jnp.asarray(c, bf16) for c in consts_np(D)]

def k12(lengths, tok, wq, wos, vpk, fc1s, fc2s, B=512):
    rows, D = tok.shape
    W = D // 2; pairs = W // 128
    V, A = pl.BlockSpec(memory_space=pltpu.VMEM), pl.BlockSpec(memory_space=pl.ANY)
    sds = jax.ShapeDtypeStruct
    hid = fc1s.shape[0]
    return pl.pallas_call(functools.partial(k12_kernel, B=B, pairs=pairs), name="forward",
        out_shape=(sds((2 * rows, D), bf16), sds((2 * rows, 3 * W), bf16), sds((4, 4, 48, 3 * W), bf16), sds((rows, D), bf16),
                   sds((pairs, 2, 2 * rows), f32), sds((8, D), f32), sds((8, 4 * D), f32),
                   sds((4, 4, 48, D), bf16), sds((4, 4, 2, hid, D), bf16), sds((4, 4, 2, hid, D), bf16)),
        in_specs=[pl.BlockSpec(memory_space=pltpu.SMEM)] + [V] * 7 + [A] * 2,
        out_specs=(V,) * 7 + (A,) * 3,
        scratch_shapes=[pltpu.VMEM((rows, D), bf16), pltpu.VMEM((4, 4, 2, 16, 128), bf16), pltpu.VMEM((32, 4 * W), bf16), pltpu.VMEM((32, 4 * W), bf16),
                        pltpu.VMEM((48, W), bf16), pltpu.VMEM((2 * rows, W), bf16), pltpu.VMEM((2 * rows, 128), bf16), pltpu.VMEM((2 * rows, 128), bf16),
                        pltpu.VMEM((2 * B, 256), bf16), pltpu.VMEM((1, 2 * B), f32), pltpu.VMEM((1, 2 * B), f32), pltpu.VMEM((128, 2 * B), f32),
                        pltpu.SemaphoreType.DMA((N_COPIES,)), pltpu.SemaphoreType.DMA((N_COPIES,)), pltpu.SemaphoreType.DMA((3,))],
        compiler_params=pltpu.CompilerParams(vmem_limit_bytes=60 << 20, collective_id=0, has_side_effects=True))(
            lengths, tok, wq, wos, vpk, *consts(D), fc1s, fc2s)

def pack_vectors(six, two):
    n6 = jnp.pad(jnp.stack(six), ((0, 0), (0, 128 - six[0].shape[0])))
    n2 = jnp.pad(jnp.stack(two), ((0, 8), (0, 128 - two[0].shape[0])))
    return jnp.concatenate([n6, n2], axis=0)


class Copy:
    def __init__(self, ss, rs):
        self.ss, self.rs, self.n, self.all = ss, rs, 0, []
    def __call__(self, src, dst, dev):
        c = pltpu.make_async_remote_copy(src_ref=src, dst_ref=dst, send_sem=self.ss.at[self.n], recv_sem=self.rs.at[self.n],
                                         device_id=dev, device_id_type=MESH)
        self.n += 1
        self.all.append(c)
        return c

def add(x, y):
    return (x.astype(f32) + y.astype(f32)).astype(x.dtype)

class Scatter:
    def __init__(self, copy, w, s, bb, ab, zb):
        self.w, self.s, self.bb, self.ab, self.zb = w, s, bb, ab, zb
        self.b = [copy(s.at[:, w["qb"]], bb.at[0], w["b"]), copy(s.at[:, w["qab"]], bb.at[1], w["b"])]
        self.a = [copy(s.at[:, w["qa"]], ab, w["a"])]
        self.z = [copy(s.at[w["zi"][k], w["q"]], zb.at[k], w["zs"][k]) for k in range(3)]
    def go(self, cs):
        for c in cs: c.start()
    def start(self):
        self.go(self.b)
    def after_b(self):
        for c in self.b: c.wait_recv()
        for z in range(4):
            self.s[z, self.w["qa"]] = add(self.s[z, self.w["qa"]], self.bb[1, z])
        self.go(self.a)
        for z in range(4):
            self.s[z, self.w["q"]] = add(self.s[z, self.w["q"]], self.bb[0, z])
    def after_a(self):
        for c in self.a: c.wait_recv()
        for z in range(4):
            self.s[z, self.w["q"]] = add(self.s[z, self.w["q"]], self.ab[z])
        self.go(self.z)
    def result(self):
        for c in self.z: c.wait_recv()
        r = self.s[self.w["z"], self.w["q"]].astype(f32)
        for k in range(3): r = r + self.zb[k].astype(f32)
        return r

def k45_kernel(len_ref, afull, wown, do, delta, lse_ref, vec, gvec, gmid, gwo, e24t, e96t, qkv_h, tok_h, dy_h, g1_h, g2_h,
               gtok, gq_o, gwo_o, g1_o, g2_o, small_o,
               qkv, tok, dy, do_own, dl_own, fq, fk, q2, do2, dq, dk, dv,
               s1, r1, b1, a1, z1, s2, r2, b2, a2, z2, so, ro, bo, ao, zo, sq, bq, aq, zq,
               sm, pm, s4, bm, am, zm, da, dsend, drecv, fo, xo, fqk, xq, ss, rs, ls, *, B, pairs):
    w = place()
    tp = w["tp"]
    rows, D = tok.shape
    W = pairs * 128
    nb = 2 * rows // B
    first = tp == 0
    other = 1 - tp
    mine_rows = pl.ds(pl.multiple_of(tp * rows, rows), rows)
    mine_cols = pl.ds(pl.multiple_of(tp * W, 128), W)
    other_cols = pl.ds(pl.multiple_of(other * W, 128), W)
    copy = Copy(ss, rs)
    c_do = copy(do.at[:, other_cols], do_own.at[mine_rows, :], w["peer"])
    c_dl = copy(delta.at[pl.ds(pl.multiple_of(other * 8, 8), 8), :], dl_own.at[:, mine_rows], w["peer"])
    c_r2 = copy(g2_h.at[:, :, other], r2, w["peer"])
    c_r1 = copy(g1_h.at[:, :, other], r1, w["peer"])
    c_ro = copy(gwo.at[:, other_cols], ro, w["peer"])
    f1, f2 = Scatter(copy, w, s1, b1, a1, z1), Scatter(copy, w, s2, b2, a2, z2)
    fo_ = Scatter(copy, w, so, bo, ao, zo)
    fqs = [Scatter(copy, w, sq.at[p], bq.at[p], aq.at[p], zq.at[p]) for p in range(pairs)]
    fm = Scatter(copy, w, s4, bm, am, zm)
    c_pm = copy(sm.at[:, :, other], pm, w["peer"])
    hr = rows // 2
    c_da = [copy(dsend.at[pl.ds(k * hr, hr), :], drecv.at[pl.ds(k * hr, hr), :], w["peer"]) for k in range(2)]
    n = gq_o.shape[0]
    other_n = pl.ds(pl.multiple_of(other * n, 8), n)
    mine_n = pl.ds(pl.multiple_of(tp * n, 8), n)
    c_xo = copy(fo.at[other_n, :], xo, w["peer"])
    c_xq = copy(fqk.at[other_n, :], xq, w["peer"])
    l_q = pltpu.make_async_copy(qkv_h, qkv, ls.at[0])
    l_2 = pltpu.make_async_copy(g2_h.at[:, :, tp], s2, ls.at[1])
    l_1 = pltpu.make_async_copy(g1_h.at[:, :, tp], s1, ls.at[2])
    l_t = pltpu.make_async_copy(tok_h, tok, ls.at[3])
    l_y = pltpu.make_async_copy(dy_h, dy, ls.at[4])
    for l in (l_q, l_2, l_1, l_t, l_y): l.start()
    enter(w)
    for c in (c_do, c_dl, c_ro, c_r2, c_r1): c.start()
    do_own[mine_rows, :] = do[:, mine_cols]
    dl_own[:, mine_rows] = delta[pl.ds(pl.multiple_of(tp * 8, 8), 8), :]
    doc_features(len_ref, 2 * rows, fq, fk)
    dev = lax.broadcasted_iota(jnp.int32, (32, 1, 1), 0)
    def pieces(v, e, n):
        lane = lax.broadcasted_iota(jnp.int32, (1, 1, v.shape[1]), 2)
        hit = (lane >= dev * n) & (lane < dev * n + n)
        t = jnp.where(hit, v[None], 0.0).reshape(256, v.shape[1])
        hi = t.astype(bf16)
        return nn(hi, e) + nn((t - hi.astype(f32)).astype(bf16), e)
    early = pieces(gmid[...], e96t[...], 4 * D // 32) + pieces(gvec[...], e24t[...], D // 32)
    sm[...] = early.reshape(4, 4, 2, 8, 128)
    l_q.wait()
    c_do.wait_recv(); c_dl.wait_recv()

    half = lax.broadcasted_iota(jnp.int32, (1, 128), 1) < 64
    causal = lax.broadcasted_iota(jnp.int32, (B, B), 0) <= lax.broadcasted_iota(jnp.int32, (B, B), 1)
    causal = jnp.concatenate([causal, causal], axis=1)
    def unit(u, _):
        p, j = u // nb, u % nb
        lanes = lambda k: pl.ds(pl.multiple_of(k * W + p * 128, 128), 128)
        def at(k):
            def deco(f): pl.when(u == k)(f)
            return deco
        @at(1)
        def _():
            c_r2.wait_recv(); l_2.wait()
            for z in range(4):
                for k in range(4): s2[z, k] = add(s2[z, k], r2[z, k])
            f2.start()
            c_ro.wait_recv()
            so[...] = add(gwo[:, mine_cols], ro[...]).reshape(so.shape)
            fo_.start()
        @at(2)
        def _():
            c_r1.wait_recv(); l_1.wait()
            for z in range(4):
                for k in range(4): s1[z, k] = add(s1[z, k], r1[z, k])
            f1.start()
        @at(4)
        def _():
            f2.after_b(); fo_.after_b(); fqs[0].start()
        @at(5)
        def _():
            f2.after_a(); fo_.after_a()
        @at(6)
        def _():
            f1.after_b(); fqs[0].after_b()
        @at(7)
        def _():
            fqs[0].after_a()
        @at(8)
        def _():
            f1.after_a(); fqs[1].start()
            g2_o[...] = f2.result()
            fo[...] = fo_.result()
            c_xo.start()
        @at(9)
        def _():
            fqs[1].after_b()
        @at(10)
        def _():
            fqs[1].after_a()
        @pl.when(j == 0)
        def _():
            def prep(i, _):
                qs = pl.ds(pl.multiple_of(i * B, B), B)
                q = qkv[qs, lanes(0)] * bf16(0.125)
                d = do_own[qs, pl.ds(pl.multiple_of(p * 128, 128), 128)]
                fqb = fq[qs, :]
                z = jnp.zeros_like(q)
                q2[i] = jnp.concatenate([
                    jnp.concatenate([jnp.where(half, q, z), fqb], axis=1),
                    jnp.concatenate([jnp.where(half, z, q), fqb], axis=1)], axis=0)
                do2[i] = jnp.concatenate([jnp.where(half, d, z), jnp.where(half, z, d)], axis=0)
                dq[i] = jnp.zeros(dq.shape[1:], f32)
                return 0
            lax.fori_loop(0, nb, prep, 0)
        ks = pl.ds(pl.multiple_of(j * B, B), B)
        kt = qkv[ks, lanes(1)]
        v = qkv[ks, lanes(2)]
        k2 = jnp.concatenate([kt, fk[ks, :]], axis=1)
        def block(i, diag):
            qs = pl.ds(pl.multiple_of(i * B, B), B)
            lse = jnp.concatenate([lse_ref[p, 0:1, qs], lse_ref[p, 1:2, qs]], axis=1)
            d0 = pl.ds(2 * p, 1); d1 = pl.ds(2 * p + 1, 1)
            dl = jnp.concatenate([dl_own[d0, qs], dl_own[d1, qs]], axis=1)
            qq = q2[i]; dd = do2[i]
            pt = jnp.exp(nt(k2, qq) - lse)
            if diag: pt = jnp.where(causal, pt, 0.0)
            ds = (pt * (nt(v, dd) - dl)).astype(bf16)
            dvp = nn(pt.astype(bf16), dd)
            dkp = nn(ds, qq[:, :128])
            if diag: dv[...] = dvp; dk[...] = dkp
            else: dv[...] += dvp; dk[...] += dkp
            dq[i] += tn(ds, kt)
        block(j, True)
        def qstep(i, _):
            block(i, False); return 0
        lax.fori_loop(j + 1, nb, qstep, 0)
        qkv[ks, lanes(1)] = dk[...].astype(bf16)
        qkv[ks, lanes(2)] = dv[...].astype(bf16)
        @pl.when(j == nb - 1)
        def _():
            def fin(i, _):
                qs = pl.ds(pl.multiple_of(i * B, B), B)
                d = dq[i]
                qkv[qs, lanes(0)] = (jnp.where(half, d[:B], d[B:]) * 0.125).astype(bf16)
                return 0
            lax.fori_loop(0, nb, fin, 0)
            g = jnp.concatenate([qkv[:, lanes(k)] for k in range(3)], axis=1)
            sq[p] = tn(afull[...], g).astype(bf16).reshape(sq.shape[1:])
        return 0
    lax.fori_loop(0, pairs * nb, unit, 0)
    fqs[2].start()
    for k in range(2):
        sl = pl.ds(pl.multiple_of(other * rows + k * hr, hr), hr)
        dsend[k * hr:(k + 1) * hr, :] = nt(qkv[sl, :], wown[...]).astype(bf16)
        c_da[k].start()
    fqs[2].after_b()
    g1_o[...] = f1.result()
    for k in range(2):
        sl = pl.ds(pl.multiple_of(tp * rows + k * hr, hr), hr)
        da[k * hr:(k + 1) * hr, :] = nt(qkv[sl, :], wown[...])
        if k == 0: fqs[2].after_a()
    l_t.wait(); l_y.wait()
    for c in c_da: c.wait_recv()
    gain = vec[0:1, :]
    def fin(r, st):
        gg, gb = st
        sl = pl.ds(pl.multiple_of(r * 256, 256), 256)
        d = da[sl, :] + drecv[sl, :].astype(f32)
        xh, xr = stats(tok[sl, :].astype(f32))
        gtok[sl, :] = (dy[sl, :].astype(f32) + ln_back(d, xh, xr, gain)).astype(bf16)
        return gg + colsum(d * xh), gb + colsum(d)
    z = jnp.zeros((1, D), f32)
    gg, gb = lax.fori_loop(0, rows // 256, fin, (z, z))
    late = pieces(jnp.concatenate([gg, gb, jnp.zeros((6, D), f32)], axis=0), e24t[...], D // 32)
    sm[...] = sm[...] + late.reshape(4, 4, 2, 8, 128)
    c_pm.start()
    for p in range(pairs):
        fqk[:, p * 384:(p + 1) * 384] = fqs[p].result()
    c_xq.start()
    c_pm.wait_recv()
    for z in range(4):
        for k in range(4): s4[z, k] = sm[z, k, tp] + pm[z, k]
    fm.start()
    c_xo.wait_recv()
    mine = fo[mine_n, :]
    gwo_o[:, :W] = jnp.where(first, mine, xo[...])
    gwo_o[:, W:] = jnp.where(first, xo[...], mine)
    fm.after_b()
    c_xq.wait_recv()
    for p in range(pairs):
        for k in range(3):
            src = p * 384 + k * 128
            mine = fqk[mine_n, src:src + 128]
            oth = xq[:, src:src + 128]
            c0 = k * D + p * 128
            gq_o[:, c0:c0 + 128] = jnp.where(first, mine, oth)
            gq_o[:, c0 + W:c0 + W + 128] = jnp.where(first, oth, mine)
    fm.after_a()
    small_o[...] = fm.result()
    for c in copy.all: c.wait_send()

def k45(lengths, afull, wown, do, delta, lse, vec, gvec, gmid, gwo, qkv, tok, dy, g1, g2, B=512):
    rows, D = tok.shape
    W = D // 2; pairs = W // 128; nb = 2 * rows // B
    V, A = pl.BlockSpec(memory_space=pltpu.VMEM), pl.BlockSpec(memory_space=pl.ANY)
    sds = jax.ShapeDtypeStruct
    hid = g1.shape[3]
    M = pltpu.VMEM
    e24t, e96t = [c.T for c in consts_np(D)[:2]]
    def flow(r, c, t, lead=()):
        return [M(lead + (4, 4, r, c), t), M(lead + (2, 4, r, c), t), M(lead + (4, r, c), t), M(lead + (3, r, c), t)]
    fc = flow(hid, D, bf16)
    fc = [fc[0], M((4, 4, hid, D), bf16)] + fc[1:]
    wo = flow(48, W, bf16)
    wo = [wo[0], M((D, W), bf16)] + wo[1:]
    sm = flow(8, 128, f32)
    return pl.pallas_call(functools.partial(k45_kernel, B=B, pairs=pairs), name="backward",
        out_shape=(sds((rows, D), bf16), sds((D // 32, 3 * D), f32), sds((D // 32, D), f32), sds((hid, D), f32), sds((hid, D), f32), sds((8, 128), f32)),
        in_specs=[pl.BlockSpec(memory_space=pltpu.SMEM)] + [V] * 11 + [A] * 5,
        out_specs=(V,) * 6,
        scratch_shapes=[M((2 * rows, 3 * W), bf16), M((rows, D), bf16), M((rows, D), dy.dtype), M((2 * rows, W), bf16), M((8, 2 * rows), f32),
                        M((2 * rows, 128), bf16), M((2 * rows, 128), bf16), M((nb, 2 * B, 256), bf16), M((nb, 2 * B, 128), bf16), M((nb, 2 * B, 128), f32),
                        M((B, 128), f32), M((B, 128), f32)] + fc + fc + wo + flow(48, W, bf16, (pairs,)) +
                       [M((4, 4, 2, 8, 128), f32), M((4, 4, 8, 128), f32)] + sm +
                       [M((rows, D), f32), M((rows, D), bf16), M((rows, D), bf16), M((48, W), f32), M((24, W), f32), M((48, 3 * W), f32), M((24, 3 * W), f32),
                        pltpu.SemaphoreType.DMA((64,)), pltpu.SemaphoreType.DMA((64,)), pltpu.SemaphoreType.DMA((5,))],
        compiler_params=pltpu.CompilerParams(vmem_limit_bytes=63 << 20, collective_id=1, has_side_effects=True))(
            lengths, afull, wown, do, delta, lse, vec, gvec, gmid, gwo, jnp.asarray(e24t, bf16), jnp.asarray(e96t, bf16), qkv, tok, dy, g1, g2)

def local_fast(tokens, cotangent, lengths, qkv_weight, out_weight, pre_gain, pre_shift, sub_gain, sub_shift,
          ffn_gain, ffn_shift, fc1_weight, mid_gain, mid_shift, fc2_weight):
    rows, D = tokens.shape
    vpk = pack_vectors([pre_gain, pre_shift, sub_gain, sub_shift, ffn_gain, ffn_shift], [mid_gain, mid_shift])
    afull, qkv, wown, o, lse, vec, mid, wo, fc1, fc2 = k12(lengths, tokens, qkv_weight, out_weight, vpk, fc1_weight, fc2_weight)
    block_out, dy, do, delta, gwo, g1, g2, gvec, gmid = ffn(o, tokens, cotangent, wo.reshape(D, D), fc1.reshape(4 * D, D), fc2.reshape(4 * D, D), vec, mid)
    shape = (4, 4, 2, fc1_weight.shape[0], D)
    gtok, gq, gwo, g1, g2, small = k45(lengths, afull, wown.reshape(D, -1), do, delta, lse, vec, gvec, gmid, gwo, qkv, tokens, dy, g1.reshape(shape), g2.reshape(shape))
    n, m = pre_gain.shape[0], mid_gain.shape[0]
    return (block_out, gtok, gq, gwo, small[0, :n], small[1, :n], small[2, :n], small[3, :n], small[4, :n], small[5, :n],
            g1, small[6, :m], small[7, :m], g2)

def norm(v):
    return stats(v)


def local_any(tokens, cotangent, lengths, qkv_weight, out_weight, pre_gain, pre_shift, sub_gain, sub_shift,
          ffn_gain, ffn_shift, fc1_weight, mid_gain, mid_shift, fc2_weight):
    rows, D = tokens.shape
    W = D // 2
    tp = lax.axis_index("tp")
    both = ("dp", "tp")
    gather = lambda a: lax.all_gather(a, both, axis=0, tiled=True)
    small = gather(jnp.stack([pre_gain, pre_shift, sub_gain, sub_shift, ffn_gain, ffn_shift], axis=1)).astype(f32).T
    mid = gather(jnp.stack([mid_gain, mid_shift], axis=1)).astype(f32).T
    wq = gather(qkv_weight)
    wo, fc1, fc2 = gather(out_weight), gather(fc1_weight), gather(fc2_weight)
    wown = lax.dynamic_index_in_dim(wq.reshape(D, 3, 2, W), tp, 2, keepdims=False).reshape(D, 3 * W)
    x = tokens.astype(f32)
    xh, xr = norm(x)
    a = (xh * small[0] + small[1]).astype(bf16)
    afull = lax.all_gather(a, "tp", axis=0, tiled=True)
    qkv = nn(afull, wown).astype(bf16)
    o_own, lse = attn_fwd(lengths, qkv, B=512)
    o = lax.all_to_all(o_own, "tp", 0, 1, tiled=True)
    vec = jnp.concatenate([small, jnp.zeros((2, D), f32)], axis=0)
    block_out, dy, do, delta, gwo, gfc1, gfc2, gvec, gmid = ffn(
        o, tokens, cotangent, wo, fc1, fc2, vec, jnp.concatenate([mid, jnp.zeros((6, 4 * D), f32)], axis=0))
    do_own = lax.all_to_all(do, "tp", 1, 0, tiled=True)
    dl_own = lax.all_to_all(delta, "tp", 0, 1, tiled=True)
    dqkv = attn_bwd(lengths, qkv, do_own, lse, dl_own, B=512)
    gq = tn(afull, dqkv)
    da = lax.psum_scatter(nt(dqkv, wown), "tp", scatter_dimension=0, tiled=True)
    grad_tokens = (dy.astype(f32) + ln_back(da, xh, xr, small[0])).astype(bf16)
    scatter = lambda v: lax.psum_scatter(v, both, scatter_dimension=0, tiled=True)
    gq = lax.psum_scatter(gq, "dp", scatter_dimension=0, tiled=True)
    n = gq.shape[0] // 2
    gq = lax.all_to_all(gq.reshape(2, n, 3, 1, W), "tp", 0, 3, tiled=True).reshape(n, 3 * D)
    small_grads = scatter(jnp.concatenate([jnp.stack([colsum(da * xh)[0], colsum(da)[0]]), gvec[2:6]], axis=0).T).T
    mid_grads = scatter(gmid[6:8].T).T
    gwo = scatter(gwo.astype(f32))
    gfc1 = scatter(gfc1.reshape(-1, D).astype(f32))
    gfc2 = scatter(gfc2.reshape(-1, D).astype(f32))
    return (block_out, grad_tokens, gq, gwo, small_grads[0], small_grads[1], small_grads[2], small_grads[3],
            small_grads[4], small_grads[5], gfc1, mid_grads[0], mid_grads[1], gfc2)


def local(*arrays):
    fits = lax.axis_size("dp") == 16 and lax.axis_size("tp") == 2
    return (local_fast if fits else local_any)(*arrays)


def solution(mesh):
    two, one = P(("dp", "tp"), None), P(("dp", "tp"))
    return jax.shard_map(
        local,
        mesh=mesh,
        in_specs=(two, two, P("dp", None), two, two, one, one, one, one, one, one, two, one, one, two),
        out_specs=(two, two, two, two, one, one, one, one, one, one, two, one, one, two),
        check_vma=False,
    )
```

```python
import functools

import jax
import jax.numpy as jnp
import numpy as np
from jax import lax
from jax.experimental import pallas as pl
from jax.experimental.pallas import tpu as pltpu
from jax.sharding import PartitionSpec as P

f32, bf16 = jnp.float32, jnp.bfloat16
EPS = 1e-5
BIG = 1e30


def nt(a, b):
    return lax.dot_general(a, b, (((1,), (1,)), ((), ())), preferred_element_type=f32)


def nn(a, b):
    return lax.dot_general(a, b, (((1,), (0,)), ((), ())), preferred_element_type=f32)


def tn(a, b):
    return lax.dot_general(a, b, (((0,), (0,)), ((), ())), preferred_element_type=f32)

def doc_features(len_ref, rows, fq, fk):
    lane = lax.broadcasted_iota(jnp.int32, (1, 128), 1)
    lo = jnp.zeros((1, 128), jnp.int32); hi = jnp.zeros((1, 128), jnp.int32)
    run = jnp.int32(0)
    for d in range(8):
        nxt = run + len_ref[0, d]
        lo = jnp.where(lane == d, run, lo); hi = jnp.where(lane == d, nxt, hi)
        run = nxt
    def body(r, _):
        place = lax.broadcasted_iota(jnp.int32, (256, 128), 0) + r * 256
        hit = (place >= lo) & (place < hi)
        sl = pl.ds(pl.multiple_of(r * 256, 256), 256)
        fq[sl, :] = jnp.where(hit, 1.0, 0.0).astype(bf16)
        fk[sl, :] = jnp.where(hit | (lane >= 8), 0.0, -BIG).astype(bf16)
        return 0
    lax.fori_loop(0, rows // 256, body, 0)

def fwd_t(len_ref, qkv, o_ref, lse_ref, fq, fk, q2, st_s, m_s, l_s, acc, *, B, pairs, variant):
    rows = qkv.shape[0]; nb = rows // B; W = pairs * 128
    doc_features(len_ref, rows, fq, fk)
    half = lax.broadcasted_iota(jnp.int32, (1, 128), 1) < 64
    causal = lax.broadcasted_iota(jnp.int32, (B, B), 0) <= lax.broadcasted_iota(jnp.int32, (B, B), 1)
    causal = jnp.concatenate([causal, causal], axis=1)
    for p in range(pairs):
        def qstep(i, _, p=p):
            qs = pl.ds(pl.multiple_of(i * B, B), B)
            q = qkv[qs, p * 128:(p + 1) * 128] * bf16(0.125)
            fqb = fq[qs, :]
            z = jnp.zeros_like(q)
            q2[...] = jnp.concatenate([
                jnp.concatenate([jnp.where(half, q, z), fqb], axis=1),
                jnp.concatenate([jnp.where(half, z, q), fqb], axis=1)], axis=0)
            def score(j):
                ks = pl.ds(pl.multiple_of(j * B, B), B)
                k2 = jnp.concatenate([qkv[ks, W + p * 128:W + (p + 1) * 128], fk[ks, :]], axis=1)
                return nt(k2, q2[...])
            def vblk(j):
                ks = pl.ds(pl.multiple_of(j * B, B), B)
                return qkv[ks, 2 * W + p * 128:2 * W + (p + 1) * 128]
            if variant == "online":
                def block(j, masked, first):
                    s = score(j)
                    if masked: s = jnp.where(causal, s, -BIG)
                    mx = jnp.max(s, axis=0, keepdims=True)
                    if first: mn = mx
                    else:
                        mo = m_s[...]
                        mn = jnp.maximum(mo, mx); al = jnp.exp(mo - mn)
                    e = jnp.exp(s - mn)
                    su = jnp.sum(e, axis=0, keepdims=True)
                    pv = tn(vblk(j), e.astype(bf16))
                    if first: l_s[...] = su; acc[...] = pv
                    else: l_s[...] = l_s[...] * al + su; acc[...] = acc[...] * al + pv
                    m_s[...] = mn
                block(i, True, True)
                def kstep(j, _):
                    block(j, False, False); return 0
                lax.fori_loop(0, i, kstep, 0)
                m = m_s[...]; l = l_s[...]
            else:
                def part(s): return jnp.max(s.reshape(B // 8, 8, 2 * B), axis=0)
                s = jnp.where(causal, score(i), -BIG)
                st_s[i] = s
                def pass1(j, m8):
                    s = score(j); st_s[j] = s
                    return jnp.maximum(m8, part(s))
                m8 = lax.fori_loop(0, i, pass1, part(s))
                m = jnp.max(m8, axis=0, keepdims=True)
                acc[...] = jnp.zeros_like(acc)
                def pass2(j, l8):
                    e = jnp.exp(st_s[j] - m)
                    acc[...] += tn(vblk(j), e.astype(bf16))
                    return l8 + jnp.sum(e.reshape(B // 8, 8, 2 * B), axis=0)
                l8 = lax.fori_loop(0, i + 1, pass2, jnp.zeros((8, 2 * B), f32))
                l = jnp.sum(l8, axis=0, keepdims=True)
            r = 1.0 / l
            a = acc[...] * r
            ot = jnp.concatenate([a[:64, :B], a[64:, B:]], axis=0)
            o_ref[qs, p * 128:(p + 1) * 128] = ot.T.astype(o_ref.dtype)
            lse = m + jnp.log(l)
            lse_ref[2 * p:2 * p + 1, qs] = lse[:, :B]
            lse_ref[2 * p + 1:2 * p + 2, qs] = lse[:, B:]
            return 0
        lax.fori_loop(0, nb, qstep, 0)

def attn_fwd(lengths, qkv, B=256, variant="online"):
    rows, w3 = qkv.shape; W = w3 // 3; pairs = W // 128; nb = rows // B
    return pl.pallas_call(functools.partial(fwd_t, B=B, pairs=pairs, variant=variant), name="attn_fwd",
        out_shape=(jax.ShapeDtypeStruct((rows, W), bf16), jax.ShapeDtypeStruct((8, rows), f32)),
        in_specs=[pl.BlockSpec(memory_space=pltpu.SMEM), pl.BlockSpec(memory_space=pltpu.VMEM)],
        out_specs=(pl.BlockSpec(memory_space=pltpu.VMEM),) * 2,
        scratch_shapes=[pltpu.VMEM((rows, 128), bf16), pltpu.VMEM((rows, 128), bf16), pltpu.VMEM((2 * B, 256), bf16),
                        pltpu.VMEM((nb if variant != "online" else 1, B, 2 * B), f32),
                        pltpu.VMEM((1, 2 * B), f32), pltpu.VMEM((1, 2 * B), f32), pltpu.VMEM((128, 2 * B), f32)],
        compiler_params=pltpu.CompilerParams(vmem_limit_bytes=56 << 20))(lengths, qkv)

def bwd_kernel(len_ref, qkv, do_ref, lse_ref, dl_ref, out, fq, fk, q2, do2, dq, dk, dv, *, B, pairs, mode):
    rows = qkv.shape[0]; nb = rows // B; W = pairs * 128
    doc_features(len_ref, rows, fq, fk)
    half = lax.broadcasted_iota(jnp.int32, (1, 128), 1) < 64
    causal = lax.broadcasted_iota(jnp.int32, (B, B), 0) <= lax.broadcasted_iota(jnp.int32, (B, B), 1)
    causal = jnp.concatenate([causal, causal], axis=1)
    for p in range(pairs):
        def prep(i, _, p=p):
            qs = pl.ds(pl.multiple_of(i * B, B), B)
            q = qkv[qs, p * 128:(p + 1) * 128] * bf16(0.125)
            d = do_ref[qs, p * 128:(p + 1) * 128]
            fqb = fq[qs, :]
            z = jnp.zeros_like(q)
            q2[i] = jnp.concatenate([
                jnp.concatenate([jnp.where(half, q, z), fqb], axis=1),
                jnp.concatenate([jnp.where(half, z, q), fqb], axis=1)], axis=0)
            do2[i] = jnp.concatenate([jnp.where(half, d, z), jnp.where(half, z, d)], axis=0)
            dq[i] = jnp.zeros(dq.shape[1:], f32)
            return 0
        lax.fori_loop(0, nb, prep, 0)
        def kstep(j, _, p=p):
            ks = pl.ds(pl.multiple_of(j * B, B), B)
            kt = qkv[ks, W + p * 128:W + (p + 1) * 128]
            v = qkv[ks, 2 * W + p * 128:2 * W + (p + 1) * 128]
            k2 = jnp.concatenate([kt, fk[ks, :]], axis=1)
            def block(i, masked, first):
                qs = pl.ds(pl.multiple_of(i * B, B), B)
                lse = jnp.concatenate([lse_ref[2 * p:2 * p + 1, qs], lse_ref[2 * p + 1:2 * p + 2, qs]], axis=1)
                dl = jnp.concatenate([dl_ref[2 * p:2 * p + 1, qs], dl_ref[2 * p + 1:2 * p + 2, qs]], axis=1)
                qq = q2[i]; dd = do2[i]
                st = nt(k2, qq)
                pt = jnp.exp(st - lse)
                if masked: pt = jnp.where(causal, pt, 0.0)
                dp = nt(v, dd)
                ds = (pt * (dp - dl)).astype(bf16)
                dvp = nn(pt.astype(bf16), dd)
                dkp = nn(ds, qq[:, :128])
                if first: dv[...] = dvp; dk[...] = dkp
                else: dv[...] += dvp; dk[...] += dkp
                if mode == "tn":
                    dq[i] += tn(ds, kt)
                else:
                    dq[i] += tn(kt, ds)
            block(j, True, True)
            def qstep(i, _):
                block(i, False, False); return 0
            lax.fori_loop(j + 1, nb, qstep, 0)
            out[ks, W + p * 128:W + (p + 1) * 128] = dk[...].astype(bf16)
            out[ks, 2 * W + p * 128:2 * W + (p + 1) * 128] = dv[...].astype(bf16)
            return 0
        lax.fori_loop(0, nb, kstep, 0)
        def fin(i, _, p=p):
            qs = pl.ds(pl.multiple_of(i * B, B), B)
            if mode == "tn":
                d = dq[i]
                r = jnp.where(half, d[:B], d[B:])
            else:
                d = dq[i]
                r = jnp.concatenate([d[:64, :B], d[64:, B:]], axis=0).T
            out[qs, p * 128:(p + 1) * 128] = (r * 0.125).astype(bf16)
            return 0
        lax.fori_loop(0, nb, fin, 0)

def attn_bwd(lengths, qkv, do, lse, dl, B=256, mode="tn"):
    rows, w3 = qkv.shape; W = w3 // 3; pairs = W // 128; nb = rows // B
    dqs = (nb, 2 * B, 128) if mode == "tn" else (nb, 128, 2 * B)
    return pl.pallas_call(functools.partial(bwd_kernel, B=B, pairs=pairs, mode=mode), name="attn_bwd",
        out_shape=jax.ShapeDtypeStruct((rows, w3), bf16),
        in_specs=[pl.BlockSpec(memory_space=pltpu.SMEM)] + [pl.BlockSpec(memory_space=pltpu.VMEM)] * 4,
        out_specs=pl.BlockSpec(memory_space=pltpu.VMEM),
        scratch_shapes=[pltpu.VMEM((rows, 128), bf16), pltpu.VMEM((rows, 128), bf16), pltpu.VMEM((nb, 2 * B, 256), bf16),
                        pltpu.VMEM((nb, 2 * B, 128), bf16), pltpu.VMEM(dqs, f32), pltpu.VMEM((B, 128), f32), pltpu.VMEM((B, 128), f32)],
        compiler_params=pltpu.CompilerParams(vmem_limit_bytes=56 << 20))(lengths, qkv, do, lse, dl)

def stats(v):
    n = v.shape[-1]
    m = jnp.sum(v, axis=-1, keepdims=True) * (1.0 / n)
    c = v - m
    s = jnp.sum(c * c, axis=-1, keepdims=True) * (1.0 / n)
    r = lax.rsqrt(s + EPS)
    return c * r, r
def ln_back(w, vh, r, g):
    n = vh.shape[-1]
    wg = w * g
    a = jnp.sum(wg, axis=-1, keepdims=True) * (1.0 / n)
    b = jnp.sum(wg * vh, axis=-1, keepdims=True) * (1.0 / n)
    return r * (wg - a - vh * b)
def colsum(v): return jnp.sum(v, axis=0, keepdims=True)


def gelu_parts(h):
    return 0.5 + 0.5 * lax.erf(h * 0.7071067811865476), jnp.exp2(h * h * -0.7213475204444817) * 0.3989422804014327

def ffn_kernel(vec, mid, sel, o_h, x_h, g_h, wo_h, fc1_h, fc2_h,
               delta_ref, gvec, gmid, gfc1, gfc2, out_h, dy_h, do_h, gwo_h,
               o_ref, x_ref, g_ref, wo, fc1, fc2, out_ref, dy_ref, do_ref, gwo,
               h_s, u_s, d_s, dm_s, m_s, dh_s, c_s, b_s, y_s, dc_s, st_s, ws, *, T, NT, NC, SR, UT):
    step = pl.program_id(0)
    rows = x_ref.shape[0]
    ff, D = fc1.shape
    K = ff // NC
    NS = NT // UT
    ins = [pltpu.make_async_copy(h, v, ws.at[k]) for k, (h, v) in enumerate(
        ((o_h, o_ref), (wo_h, wo), (x_h, x_ref), (fc1_h, fc1), (g_h, g_ref), (fc2_h, fc2)))]
    outs = [pltpu.make_async_copy(v, h, ws.at[6 + k]) for k, (h, v) in enumerate(
        ((out_h, out_ref), (dy_h, dy_ref), (do_h, do_ref), (gwo_h, gwo)))]
    sg, sb, fg, fb = [vec[k:k + 1, :] for k in range(2, 6)]
    tiles = [slice(t * T, (t + 1) * T) for t in range(NT)]
    subs = [slice(r * SR, (r + 1) * SR) for r in range(T // SR)]
    cols = [slice(c * K, (c + 1) * K) for c in range(NC)]
    def fold(v):
        r = v[:, :128]
        for k in range(1, v.shape[1] // 128): r = r + v[:, k * 128:(k + 1) * 128]
        return r
    @pl.when(step == 0)
    def _():
        for l in ins: l.start()
        gvec[...] = jnp.zeros_like(gvec); gmid[...] = jnp.zeros_like(gmid)
        ins[0].wait(); ins[1].wait(); ins[2].wait()
        bs = []
        for sl in tiles:
            oh, _r = stats(o_ref[sl, :].astype(f32))
            b_s[sl, :] = (oh * sg + sb).astype(bf16)
        for sl in tiles:
            y_s[sl, :] = x_ref[sl, :].astype(f32) + nn(b_s[sl, :], wo[...])
        for sl in tiles:
            yh, _r = stats(y_s[sl, :])
            c_s[sl, :] = (yh * fg + fb).astype(bf16)
        ins[3].wait(); ins[4].wait(); ins[5].wait()
    base = jnp.minimum(step, NS - 1) * T
    rs = pl.ds(pl.multiple_of(base, T), T)
    sub_rows = lambda s: pl.ds(pl.multiple_of(base + s.start, SR), SR)
    total = lambda k: jnp.sum(jnp.sum(st_s[k], axis=0), axis=1, keepdims=True) * (1.0 / ff)
    def moments():
        mu = total(0)
        return mu, lax.rsqrt(total(1) - mu * mu + EPS)
    @pl.when(step < NS)
    def _():
        h_s[0] = nt(c_s[rs, :], fc1[cols[0], :])
        for c in range(NC):
            for s in subs:
                h = h_s[c % 2, s, :]
                phi, den = gelu_parts(h)
                u = h * phi
                u_s[s, cols[c]] = u
                d_s[s, cols[c]] = phi + h * den
                st_s[0, c, s, :] = fold(u); st_s[1, c, s, :] = fold(u * u)
            if c + 1 < NC: h_s[(c + 1) % 2] = nt(c_s[rs, :], fc1[cols[c + 1], :])
            else: dm_s[:, cols[0]] = nt(g_ref[rs, :], fc2[cols[0], :])
    @pl.when(step < NS)
    def _():
        mu, R = moments()
        for c in range(NC):
            gain = mid[0:1, cols[c]]; shift = mid[1:2, cols[c]]
            g6 = jnp.zeros((8, K), f32); g7 = jnp.zeros((8, K), f32)
            for s in subs:
                uh = (u_s[s, cols[c]] - mu[s]) * R[s]
                u_s[s, cols[c]] = uh
                m_s[sub_rows(s), cols[c]] = (uh * gain + shift).astype(bf16)
                dm = dm_s[s, cols[c]]
                e = dm * gain
                dm_s[s, cols[c]] = e
                q = dm * uh
                g6 += jnp.sum(q.reshape(SR // 8, 8, K), axis=0); g7 += jnp.sum(dm.reshape(SR // 8, 8, K), axis=0)
                st_s[2, c, s, :] = fold(e); st_s[3, c, s, :] = fold(e * uh)
            gmid[6:7, cols[c]] += colsum(g6)
            gmid[7:8, cols[c]] += colsum(g7)
            if c + 1 < NC: dm_s[:, cols[c + 1]] = nt(g_ref[rs, :], fc2[cols[c + 1], :])
    @pl.when(step < NS)
    def _():
        R = moments()[1]
        se = total(2); seu = total(3)
        for c in range(NC):
            for s in subs:
                dh = (dm_s[s, cols[c]] - se[s] - u_s[s, cols[c]] * seu[s]) * R[s] * d_s[s, cols[c]]
                dh_s[sub_rows(s), cols[c]] = dh.astype(bf16)
            if c == 0:
                out_ref[rs, :] = (y_s[rs, :] + nn(m_s[rs, :], fc2[...])).astype(bf16)
    @pl.when(step < NS)
    def _():
        dc_s[rs, :] = nn(dh_s[rs, :], fc1[...])
    def grads(lanes):
        gfc2[0] = tn(m_s[:, lanes], g_ref[...]).astype(bf16)
        gfc1[0] = tn(dh_s[:, lanes], c_s[...]).astype(bf16)
    @pl.when(step == NS)
    def _():
        outs[0].start()
        hs = []
        for sl in tiles:
            yh, yr = stats(y_s[sl, :])
            dc = dc_s[sl, :]
            gvec[4:5, :] += colsum(dc * yh)
            gvec[5:6, :] += colsum(dc)
            dy_ref[sl, :] = (g_ref[sl, :].astype(f32) + ln_back(dc, yh, yr, fg)).astype(bf16)
        for sl in tiles:
            dc_s[sl, :] = nt(dy_ref[sl, :], wo[...])
        for sl in tiles:
            dbn = dc_s[sl, :]
            o = o_ref[sl, :].astype(f32)
            oh, orr = stats(o)
            gvec[2:3, :] += colsum(dbn * oh)
            gvec[3:4, :] += colsum(dbn)
            do = ln_back(dbn, oh, orr, sg).astype(bf16)
            do_ref[sl, :] = do
            pr = do.astype(f32) * o
            hi = pr.astype(bf16)
            lo = (pr - hi.astype(f32)).astype(bf16)
            delta_ref[:, sl] = nt(sel[...], hi) + nt(sel[...], lo)
        grads(cols[0])
        gwo[...] = tn(b_s[...], dy_ref[...]).astype(bf16)
        for c in outs[1:]: c.start()
    @pl.when(step > NS)
    def _():
        grads(pl.ds(pl.multiple_of((step - NS) * K, K), K))
    @pl.when(step == NS + NC - 1)
    def _():
        for c in outs: c.wait()

def ffn(o, x, g, wo, fc1, fc2, vec, mid, T=256, K=512, dt=f32, SR=16, UT=1):
    rows, D = x.shape; ff = fc1.shape[0]; NC = ff // K; NT = rows // T; NS = NT // UT
    head = np.arange(D)[None] // 64
    sel = jnp.asarray((np.arange(16)[:, None] == head // (D // 128) * 8 + head % (D // 128)).astype(np.float32), bf16)
    one = dict(pipeline_mode=pl.Buffered(1))
    full = lambda *s: pl.BlockSpec(s, lambda i: (0,) * len(s), **one)
    A = pl.BlockSpec(memory_space=pl.ANY)
    chunk = pl.BlockSpec((1, K, D), lambda s: (jnp.maximum(s - NS, 0), 0, 0))
    sds = jax.ShapeDtypeStruct
    M = pltpu.VMEM
    act = sds((rows, D), bf16)
    delta, gvec, gmid, g1, g2, out, dy, do, gwo = pl.pallas_call(functools.partial(ffn_kernel, T=T, NT=NT, NC=NC, SR=SR, UT=UT), name="ffn",
        grid=(NS + NC,),
        in_specs=[full(8, D), full(8, ff), full(16, D)] + [A] * 6,
        out_specs=[full(16, rows), full(8, D), full(8, ff), chunk, chunk] + [A] * 4,
        out_shape=[sds((16, rows), f32), sds((8, D), f32), sds((8, ff), f32), sds((NC, K, D), bf16), sds((NC, K, D), bf16),
                   act, act, act, sds((D, D), bf16)],
        scratch_shapes=[M((rows, D), bf16), M((D, D), bf16), M((rows, D), bf16)][:0] + [M((rows, D), bf16), M((rows, D), bf16), M((rows, D), bf16),
                        M((D, D), bf16), M((ff, D), bf16), M((ff, D), bf16), M((rows, D), bf16), M((rows, D), bf16), M((rows, D), bf16), M((D, D), bf16),
                        M((2, T, K), f32), M((T, ff), f32), M((T, ff), f32), M((T, ff), f32),
                        M((rows, ff), bf16), M((rows, ff), bf16), M((rows, D), bf16), M((rows, D), bf16), M((rows, D), f32), M((rows, D), f32),
                        M((4, NC, T, 128), f32), pltpu.SemaphoreType.DMA((10,))],
        compiler_params=pltpu.CompilerParams(vmem_limit_bytes=63 << 20, dimension_semantics=("arbitrary",)))(
            vec, mid, sel, o, x, g, wo, fc1, fc2)
    return out, dy, do, delta, gwo, g1, g2, gvec, gmid

MESH = pl.DeviceIdType.MESH

def place():
    dp, tp = lax.axis_index("dp"), lax.axis_index("tp")
    q, z = dp % 4, dp // 4
    dx = 1 - 2 * (dp % 2)
    dy = 2 - 4 * ((dp // 2) % 2)
    a, b = (1 - tp) * dx + tp * dy, tp * dx + (1 - tp) * dy
    return dict(dp=dp, tp=tp, z=z, q=q, qa=q + a, qb=q + b, qab=q + a + b,
                a=(dp + a, tp), b=(dp + b, tp), peer=(dp, 1 - tp),
                zs=[((dp + 4 * k) % 16, tp) for k in (1, 2, 3)], zi=[(z + k) % 4 for k in (1, 2, 3)])

def enter(w):
    bar = pltpu.get_barrier_semaphore()
    for d in [w["a"], w["b"], w["peer"]] + w["zs"]:
        pl.semaphore_signal(bar, inc=1, device_id=d, device_id_type=MESH)
    pl.semaphore_wait(bar, 6)

class Sender:
    def __init__(self, ss, rs):
        self.ss, self.rs, self.n, self.all = ss, rs, 0, []
    def __call__(self, src, dst, dev):
        c = pltpu.make_async_remote_copy(src_ref=src, dst_ref=dst, send_sem=self.ss.at[self.n], recv_sem=self.rs.at[self.n],
                                         device_id=dev, device_id_type=MESH)
        self.n += 1
        self.all.append(c)
        c.start()
        return c

class Gather:
    def __init__(self, send, w, src, slot, view, peer):
        self.send, self.w, self.src, self.slot, self.view, self.peer = send, w, src, slot, view, peer
    def plan(self):
        pass
    def start(self):
        w = self.w
        s = self.slot(w["z"], w["q"], w["tp"])
        self.cz = [self.send(self.src, s, d) for d in w["zs"]]
    def _fan(self, q, devs):
        v = self.view(q, self.w["tp"])
        return [self.send(v, v, d) for d in devs]
    def after_z(self):
        w = self.w
        for c in self.cz: c.wait_recv()
        devs = [w["a"], w["b"]] + ([w["peer"]] if self.peer else [])
        self.c1 = self._fan(w["q"], devs)
    def after_a(self):
        w = self.w
        self.c1[0].wait_recv()
        self.c2 = self._fan(w["qa"], [w["b"]] + ([w["peer"]] if self.peer else []))
    def after_b(self):
        w = self.w
        self.c1[1].wait_recv(); self.c2[0].wait_recv()
        self.c3 = []
        if self.peer:
            self.c3 = self._fan(w["qb"], [w["peer"]]) + self._fan(w["qab"], [w["peer"]])
    def finish(self):
        if self.peer:
            self.c1[2].wait_recv(); self.c2[1].wait_recv()
            for c in self.c3: c.wait_recv()

N_COPIES = 64

def k12_kernel(len_ref, tok, wq, wos, vpk, e24, e96, rsel, fc1s, fc2s,
               xh16, qkv, wown, o_out, lse_ref, vec, mid, wo_h, fc1_h, fc2_h,
               afull, xp, vbuf, sb, rb, woc, o_loc, fq, fk, q2, m_s, l_s, acc, ss, rs, ls, *, B, pairs, stage=9):
    w = place()
    tp = w["tp"]
    rows, D = tok.shape
    W = pairs * 128
    send = Sender(ss, rs)
    first = tp == 0
    sb[...] = jnp.zeros_like(sb)
    pick = lambda c0, n: (jnp.where(first, wq[:, c0:c0 + W], wq[:, c0 + W:c0 + 2 * W]).astype(bf16),
                          jnp.where(first, wq[:, c0 + W:c0 + 2 * W], wq[:, c0:c0 + W]).astype(bf16))
    mine = []
    for k in range(3):
        own, oth = pick(k * D, W)
        mine.append(own); sb[0:24, k * W:(k + 1) * W] = oth
    own_o = jnp.where(first, wos[:, :W], wos[:, W:])
    sb[0:24, 3 * W:4 * W] = jnp.where(first, wos[:, W:], wos[:, :W])
    vbuf[w["z"], w["q"], tp] = vpk[...]
    loc = [pltpu.make_async_copy(fc1s, fc1_h.at[w["z"], w["q"], tp], ls.at[0]),
           pltpu.make_async_copy(fc2s, fc2_h.at[w["z"], w["q"], tp], ls.at[1])]
    for c in loc: c.start()
    enter(w)
    cpre = send(sb, rb, w["peer"])
    gv = Gather(send, w, vbuf.at[w["z"], w["q"], tp], lambda z, q, t: vbuf.at[z, q, t], lambda q, t: vbuf.at[:, q, t], True)
    gv.start()
    cx = send(tok, xp, w["peer"])
    cpre.wait_recv()
    other = rb[0:24, :].astype(f32)
    me = jnp.concatenate(mine + [own_o], axis=1).astype(f32)
    both = jnp.concatenate([jnp.where(first, me, other), jnp.where(first, other, me)], axis=0).astype(bf16)
    wown[w["z"], w["q"]] = both[:, :3 * W]
    woc[...] = both[:, 3 * W:]
    gq = Gather(send, w, wown.at[w["z"], w["q"]], lambda z, q, t: wown.at[z, q], lambda q, t: wown.at[:, q], False)
    gq.start()
    cols = pl.ds(pl.multiple_of(tp * W, 128), W)
    lw = pltpu.make_async_copy(woc, wo_h.at[w["z"], w["q"], :, cols], ls.at[2])
    lw.start()
    gv.after_z(); gv.after_a(); gv.after_b(); gv.finish()
    small = nn(rsel[...], vbuf[...].reshape(512, 128)).astype(bf16)
    dev = lax.broadcasted_iota(jnp.int32, (32, 1), 0)
    lane = lax.broadcasted_iota(jnp.int32, (1, D), 1)
    hit = (lane >= dev * 24) & (lane < dev * 24 + 24)
    for v in range(6):
        vec[v:v + 1, :] = colsum(jnp.where(hit, nn(small[v * 32:(v + 1) * 32], e24[...]), 0.0))
    vec[6:8, :] = jnp.zeros((2, D), f32)
    lane = lax.broadcasted_iota(jnp.int32, (1, 4 * D), 1)
    hit = (lane >= dev * 96) & (lane < dev * 96 + 96)
    for v in range(2):
        mid[v:v + 1, :] = colsum(jnp.where(hit, nn(small[(6 + v) * 32:(7 + v) * 32], e96[...]), 0.0))
    mid[2:8, :] = jnp.zeros((6, 4 * D), f32)
    gq.after_z()
    for c in loc: c.wait()
    lw.wait()
    go = Gather(send, w, woc, lambda z, q, t: wo_h.at[z, q, :, cols], lambda q, t: wo_h.at[:, q, :, cols], True)
    g1 = Gather(send, w, fc1s, lambda z, q, t: fc1_h.at[z, q, t], lambda q, t: fc1_h.at[:, q, t], True)
    g2 = Gather(send, w, fc2s, lambda z, q, t: fc2_h.at[z, q, t], lambda q, t: fc2_h.at[:, q, t], True)
    go.start(); g1.start()
    def normed(src, base):
        def body(r, _):
            sl = pl.ds(pl.multiple_of(r * 256, 256), 256)
            xh, _r = stats(src[sl, :].astype(f32))
            to = pl.ds(pl.multiple_of(base + r * 256, 256), 256)
            xh16[to, :] = xh.astype(bf16)
            afull[to, :] = (xh * vec[0:1, :] + vec[1:2, :]).astype(bf16)
            return 0
        lax.fori_loop(0, rows // 256, body, 0)
    normed(tok, tp * rows)
    gq.after_a()
    cx.wait_recv()
    normed(xp, (1 - tp) * rows)
    doc_features(len_ref, 2 * rows, fq, fk)
    gq.after_b()
    wfull = lambda: wown[...].reshape(D, 3 * W)
    def proj(r, _):
        sl = pl.ds(pl.multiple_of(r * 512, 512), 512)
        qkv[sl, :] = nn(afull[sl, :], wfull()).astype(bf16)
        return 0
    lax.fori_loop(0, 2 * rows // 512, proj, 0)
    nb = 2 * rows // B
    half = lax.broadcasted_iota(jnp.int32, (1, 128), 1) < 64
    causal = lax.broadcasted_iota(jnp.int32, (B, B), 0) <= lax.broadcasted_iota(jnp.int32, (B, B), 1)
    causal = jnp.concatenate([causal, causal], axis=1)
    def unit(u, _):
        p, i = u // nb, u % nb
        qs = pl.ds(pl.multiple_of(i * B, B), B)
        lanes = lambda k: pl.ds(pl.multiple_of(k * W + p * 128, 128), 128)
        q = qkv[qs, lanes(0)] * bf16(0.125)
        fqb = fq[qs, :]
        z = jnp.zeros_like(q)
        q2[...] = jnp.concatenate([
            jnp.concatenate([jnp.where(half, q, z), fqb], axis=1),
            jnp.concatenate([jnp.where(half, z, q), fqb], axis=1)], axis=0)
        def block(j, diag):
            ks = pl.ds(pl.multiple_of(j * B, B), B)
            s = nt(jnp.concatenate([qkv[ks, lanes(1)], fk[ks, :]], axis=1), q2[...])
            if diag: s = jnp.where(causal, s, -BIG)
            mn = jnp.max(s, axis=0, keepdims=True)
            if not diag:
                mo = m_s[...]
                mn = jnp.maximum(mo, mn); al = jnp.exp(mo - mn)
            e = jnp.exp(s - mn)
            su = jnp.sum(e, axis=0, keepdims=True)
            pv = tn(qkv[ks, lanes(2)], e.astype(bf16))
            if diag: l_s[...] = su; acc[...] = pv
            else: l_s[...] = l_s[...] * al + su; acc[...] = acc[...] * al + pv
            m_s[...] = mn
        block(i, True)
        def kstep(j, _):
            block(j, False); return 0
        lax.fori_loop(0, i, kstep, 0)
        l = l_s[...]
        a = acc[...] * (1.0 / l)
        ot = jnp.concatenate([a[:64, :B], a[64:, B:]], axis=0)
        o_loc[qs, pl.ds(pl.multiple_of(p * 128, 128), 128)] = ot.T.astype(bf16)
        lse = m_s[...] + jnp.log(l)
        lse_ref[p, 0:1, qs] = lse[:, :B]
        lse_ref[p, 1:2, qs] = lse[:, B:]
        return 0
    def units(lo, hi):
        lax.fori_loop(lo, hi, unit, 0)
    co = []
    def share(p):
        src = o_loc.at[pl.ds(pl.multiple_of((1 - tp) * rows, rows), rows), p * 128:(p + 1) * 128]
        co.append(send(src, o_out.at[:, pl.ds(pl.multiple_of(tp * W + p * 128, 128), 128)], w["peer"]))
    go.after_z(); g1.after_z(); g2.start()
    units(0, 3)
    go.after_a(); g1.after_a()
    units(3, 4); share(0)
    units(4, 6)
    go.after_b(); g1.after_b(); g2.after_z()
    units(6, 8); share(1)
    g2.after_a()
    units(8, 11)
    g2.after_b()
    units(11, 12); share(2)
    o_out[:, cols] = o_loc[pl.ds(pl.multiple_of(tp * rows, rows), rows), :]
    for c in co: c.wait_recv()
    go.finish(); g1.finish(); g2.finish()
    for c in send.all: c.wait_send()

def consts_np(D):
    k = np.arange(128)[:, None]
    e24 = (np.arange(D)[None] % 24 == k).astype(np.float32)
    e96 = (np.arange(4 * D)[None] % 96 == k).astype(np.float32)
    r = np.arange(256)[:, None]
    rsel = (np.arange(512)[None] == (r % 32) * 16 + r // 32).astype(np.float32)
    return e24, e96, rsel

def consts(D):
    return [jnp.asarray(c, bf16) for c in consts_np(D)]

def k12(lengths, tok, wq, wos, vpk, fc1s, fc2s, B=512):
    rows, D = tok.shape
    W = D // 2; pairs = W // 128
    V, A = pl.BlockSpec(memory_space=pltpu.VMEM), pl.BlockSpec(memory_space=pl.ANY)
    sds = jax.ShapeDtypeStruct
    hid = fc1s.shape[0]
    return pl.pallas_call(functools.partial(k12_kernel, B=B, pairs=pairs), name="forward",
        out_shape=(sds((2 * rows, D), bf16), sds((2 * rows, 3 * W), bf16), sds((4, 4, 48, 3 * W), bf16), sds((rows, D), bf16),
                   sds((pairs, 2, 2 * rows), f32), sds((8, D), f32), sds((8, 4 * D), f32),
                   sds((4, 4, 48, D), bf16), sds((4, 4, 2, hid, D), bf16), sds((4, 4, 2, hid, D), bf16)),
        in_specs=[pl.BlockSpec(memory_space=pltpu.SMEM)] + [V] * 7 + [A] * 2,
        out_specs=(V,) * 7 + (A,) * 3,
        scratch_shapes=[pltpu.VMEM((2 * rows, D), bf16), pltpu.VMEM((rows, D), bf16), pltpu.VMEM((4, 4, 2, 16, 128), bf16), pltpu.VMEM((32, 4 * W), bf16), pltpu.VMEM((32, 4 * W), bf16),
                        pltpu.VMEM((48, W), bf16), pltpu.VMEM((2 * rows, W), bf16), pltpu.VMEM((2 * rows, 128), bf16), pltpu.VMEM((2 * rows, 128), bf16),
                        pltpu.VMEM((2 * B, 256), bf16), pltpu.VMEM((1, 2 * B), f32), pltpu.VMEM((1, 2 * B), f32), pltpu.VMEM((128, 2 * B), f32),
                        pltpu.SemaphoreType.DMA((N_COPIES,)), pltpu.SemaphoreType.DMA((N_COPIES,)), pltpu.SemaphoreType.DMA((3,))],
        compiler_params=pltpu.CompilerParams(vmem_limit_bytes=60 << 20, collective_id=0, has_side_effects=True))(
            lengths, tok, wq, wos, vpk, *consts(D), fc1s, fc2s)

def pack_vectors(six, two):
    n6 = jnp.pad(jnp.stack(six), ((0, 0), (0, 128 - six[0].shape[0])))
    n2 = jnp.pad(jnp.stack(two), ((0, 8), (0, 128 - two[0].shape[0])))
    return jnp.concatenate([n6, n2], axis=0)


class Copy:
    def __init__(self, ss, rs):
        self.ss, self.rs, self.n, self.all = ss, rs, 0, []
    def __call__(self, src, dst, dev):
        c = pltpu.make_async_remote_copy(src_ref=src, dst_ref=dst, send_sem=self.ss.at[self.n], recv_sem=self.rs.at[self.n],
                                         device_id=dev, device_id_type=MESH)
        self.n += 1
        self.all.append(c)
        return c

def add(x, y):
    return (x.astype(f32) + y.astype(f32)).astype(x.dtype)

class Scatter:
    def __init__(self, copy, w, s, bb, ab, zb):
        self.w, self.s, self.bb, self.ab, self.zb = w, s, bb, ab, zb
        self.b = [copy(s.at[:, w["qb"]], bb.at[0], w["b"]), copy(s.at[:, w["qab"]], bb.at[1], w["b"])]
        self.a = [copy(s.at[:, w["qa"]], ab, w["a"])]
        self.z = [copy(s.at[w["zi"][k], w["q"]], zb.at[k], w["zs"][k]) for k in range(3)]
    def go(self, cs):
        for c in cs: c.start()
    def start(self):
        self.go(self.b)
    def after_b(self):
        for c in self.b: c.wait_recv()
        for z in range(4):
            self.s[z, self.w["qa"]] = add(self.s[z, self.w["qa"]], self.bb[1, z])
        self.go(self.a)
        for z in range(4):
            self.s[z, self.w["q"]] = add(self.s[z, self.w["q"]], self.bb[0, z])
    def after_a(self):
        for c in self.a: c.wait_recv()
        for z in range(4):
            self.s[z, self.w["q"]] = add(self.s[z, self.w["q"]], self.ab[z])
        self.go(self.z)
    def result(self):
        for c in self.z: c.wait_recv()
        r = self.s[self.w["z"], self.w["q"]].astype(f32)
        for k in range(3): r = r + self.zb[k].astype(f32)
        return r

def k45_kernel(len_ref, do, delta, lse_ref, vec, gvec, gmid, e24t, e96t, qkv_h, xh_h, wown_h, gwo_h, tok_h, dy_h, g1_h, g2_h,
               gtok, gq_o, gwo_o, g1_o, g2_o, small_o, pre_o,
               qkv, xh16, wown, gwo, tok, dy, do_own, dl_own, fq, fk, q2, do2, dq, dk, dv,
               s1, r1, b1, a1, z1, s2, r2, b2, a2, z2, so, ro, bo, ao, zo, *rest, B, pairs):
    flows, rest = rest[:4 * pairs], rest[4 * pairs:]
    (sm, pm, s4, bm, am, zm, da, dsend, drecv, fo, xo, fqk, xq, gcol, bcol, vacc, uacc, ss, rs, ls) = rest
    w = place()
    tp = w["tp"]
    rows, D = tok.shape
    W = pairs * 128
    nb = 2 * rows // B
    first = tp == 0
    other = 1 - tp
    mine_rows = pl.ds(pl.multiple_of(tp * rows, rows), rows)
    mine_cols = pl.ds(pl.multiple_of(tp * W, 128), W)
    other_cols = pl.ds(pl.multiple_of(other * W, 128), W)
    copy = Copy(ss, rs)
    c_do = copy(do.at[:, other_cols], do_own.at[mine_rows, :], w["peer"])
    c_dl = copy(delta.at[pl.ds(pl.multiple_of(other * 8, 8), 8), :], dl_own.at[:, mine_rows], w["peer"])
    c_r2 = copy(g2_h.at[:, :, other], r2, w["peer"])
    c_r1 = copy(g1_h.at[:, :, other], r1, w["peer"])
    c_ro = copy(gwo_h.at[:, other_cols], ro, w["peer"])
    f1, f2 = Scatter(copy, w, s1, b1, a1, z1), Scatter(copy, w, s2, b2, a2, z2)
    fo_ = Scatter(copy, w, so, bo, ao, zo)
    fqs = [Scatter(copy, w, *flows[4 * p:4 * p + 4]) for p in range(pairs)]
    fm = Scatter(copy, w, s4, bm, am, zm)
    c_pm = copy(sm.at[:, :, other], pm, w["peer"])
    hr = rows // 2
    c_da = [copy(dsend.at[pl.ds(k * hr, hr), :], drecv.at[pl.ds(k * hr, hr), :], w["peer"]) for k in range(2)]
    n = gq_o.shape[0]
    other_n = pl.ds(pl.multiple_of(other * n, 8), n)
    mine_n = pl.ds(pl.multiple_of(tp * n, 8), n)
    c_xo = copy(fo.at[other_n, :], xo, w["peer"])
    c_xq = copy(fqk.at[other_n, :], xq, w["peer"])
    l_q = pltpu.make_async_copy(qkv_h, qkv, ls.at[0])
    l_2 = pltpu.make_async_copy(g2_h.at[:, :, tp], s2, ls.at[1])
    l_1 = pltpu.make_async_copy(g1_h.at[:, :, tp], s1, ls.at[2])
    l_t = pltpu.make_async_copy(tok_h, tok, ls.at[3])
    l_y = pltpu.make_async_copy(dy_h, dy, ls.at[4])
    l_o = pltpu.make_async_copy(gwo_h, gwo, ls.at[5])
    l_x = pltpu.make_async_copy(xh_h, xh16, ls.at[6])
    l_w = pltpu.make_async_copy(wown_h, wown, ls.at[7])
    for l in (l_q, l_2, l_o, l_1, l_x, l_w, l_t, l_y): l.start()
    enter(w)
    for c in (c_do, c_dl, c_ro, c_r2, c_r1): c.start()
    do_own[mine_rows, :] = do[:, mine_cols]
    dl_own[:, mine_rows] = delta[pl.ds(pl.multiple_of(tp * 8, 8), 8), :]
    doc_features(len_ref, 2 * rows, fq, fk)
    dev = lax.broadcasted_iota(jnp.int32, (32, 1, 1), 0)
    def pieces(v, e, n):
        lane = lax.broadcasted_iota(jnp.int32, (1, 1, v.shape[1]), 2)
        hit = (lane >= dev * n) & (lane < dev * n + n)
        t = jnp.where(hit, v[None], 0.0).reshape(256, v.shape[1])
        hi = t.astype(bf16)
        return nn(hi, e) + nn((t - hi.astype(f32)).astype(bf16), e)
    early = pieces(gmid[...], e96t[...], 4 * D // 32) + pieces(gvec[...], e24t[...], D // 32)
    sm[...] = early.reshape(4, 4, 2, 8, 128)
    c_pm.start()
    gcol[...] = jnp.broadcast_to(vec[0:1, :], (128, D)).T
    bcol[...] = jnp.broadcast_to(vec[1:2, :], (128, D)).T
    vacc[...] = jnp.zeros_like(vacc); uacc[...] = jnp.zeros_like(uacc)
    l_q.wait()
    c_do.wait_recv(); c_dl.wait_recv()

    half = lax.broadcasted_iota(jnp.int32, (1, 128), 1) < 64
    causal = lax.broadcasted_iota(jnp.int32, (B, B), 0) <= lax.broadcasted_iota(jnp.int32, (B, B), 1)
    causal = jnp.concatenate([causal, causal], axis=1)
    def grads(p):
        out = flows[4 * p]
        cs = [slice(k * W + p * 128, k * W + (p + 1) * 128) for k in range(3)]
        g = jnp.concatenate([qkv[:, c] for c in cs], axis=1)
        t = tn(xh16[...], g)
        gsum = jnp.sum(g.astype(f32), axis=0, keepdims=True)
        for k in range(3):
            sl = slice(k * 128, (k + 1) * 128)
            wk = wown[:, cs[k]].astype(f32)
            tk, sk = t[:, sl], gsum[:, sl]
            out[:, :, :, sl] = (gcol[...] * tk + bcol[...] * sk).astype(bf16).reshape(4, 4, 48, 128)
            vacc[...] += tk * wk
            uacc[...] += sk * wk
        if p == pairs - 1:
            lane = lax.broadcasted_iota(jnp.int32, (1, 128), 1)
            e = jnp.where(lane == 0, jnp.sum(vacc[...], axis=1, keepdims=True), 0.0)
            e = jnp.where(lane == 1, jnp.sum(uacc[...], axis=1, keepdims=True), e)
            out[:, :, :, 384:512] = e.astype(bf16).reshape(4, 4, 48, 128)
    def unit(u, _):
        p, j = u // nb, u % nb
        lanes = lambda k: pl.ds(pl.multiple_of(k * W + p * 128, 128), 128)
        def at(k):
            def deco(f): pl.when(u == k)(f)
            return deco
        @at(1)
        def _():
            c_pm.wait_recv()
            for z in range(4):
                for k in range(4): s4[z, k] = sm[z, k, tp] + pm[z, k]
            fm.start()
            c_r2.wait_recv(); l_2.wait()
            for z in range(4):
                for k in range(4): s2[z, k] = add(s2[z, k], r2[z, k])
            f2.start()
            c_ro.wait_recv(); l_o.wait()
            so[...] = add(gwo[:, mine_cols], ro[...]).reshape(so.shape)
            fo_.start()
        @at(2)
        def _():
            fm.after_b()
            c_r1.wait_recv(); l_1.wait()
            for z in range(4):
                for k in range(4): s1[z, k] = add(s1[z, k], r1[z, k])
            f1.start()
        @at(3)
        def _():
            fm.after_a()
        @at(4)
        def _():
            l_x.wait(); l_w.wait()
            grads(0)
            f2.after_b(); fo_.after_b(); fqs[0].start()
            small_o[...] = fm.result()
        @at(5)
        def _():
            f2.after_a(); fo_.after_a()
        @at(6)
        def _():
            f1.after_b(); fqs[0].after_b()
        @at(7)
        def _():
            fqs[0].after_a()
        @at(8)
        def _():
            f1.after_a(); grads(1); fqs[1].start()
            g2_o[...] = f2.result()
            fo[...] = fo_.result()
            c_xo.start()
        @at(9)
        def _():
            fqs[1].after_b()
        @at(10)
        def _():
            fqs[1].after_a()
        @pl.when(j == 0)
        def _():
            def prep(i, _):
                qs = pl.ds(pl.multiple_of(i * B, B), B)
                q = qkv[qs, lanes(0)] * bf16(0.125)
                d = do_own[qs, pl.ds(pl.multiple_of(p * 128, 128), 128)]
                fqb = fq[qs, :]
                z = jnp.zeros_like(q)
                q2[i] = jnp.concatenate([
                    jnp.concatenate([jnp.where(half, q, z), fqb], axis=1),
                    jnp.concatenate([jnp.where(half, z, q), fqb], axis=1)], axis=0)
                do2[i] = jnp.concatenate([jnp.where(half, d, z), jnp.where(half, z, d)], axis=0)
                dq[i] = jnp.zeros(dq.shape[1:], f32)
                return 0
            lax.fori_loop(0, nb, prep, 0)
        ks = pl.ds(pl.multiple_of(j * B, B), B)
        kt = qkv[ks, lanes(1)]
        v = qkv[ks, lanes(2)]
        k2 = jnp.concatenate([kt, fk[ks, :]], axis=1)
        def block(i, diag):
            qs = pl.ds(pl.multiple_of(i * B, B), B)
            lse = jnp.concatenate([lse_ref[p, 0:1, qs], lse_ref[p, 1:2, qs]], axis=1)
            d0 = pl.ds(2 * p, 1); d1 = pl.ds(2 * p + 1, 1)
            dl = jnp.concatenate([dl_own[d0, qs], dl_own[d1, qs]], axis=1)
            qq = q2[i]; dd = do2[i]
            pt = jnp.exp(nt(k2, qq) - lse)
            if diag: pt = jnp.where(causal, pt, 0.0)
            ds = (pt * (nt(v, dd) - dl)).astype(bf16)
            dvp = nn(pt.astype(bf16), dd)
            dkp = nn(ds, qq[:, :128])
            if diag: dv[...] = dvp; dk[...] = dkp
            else: dv[...] += dvp; dk[...] += dkp
            dq[i] += tn(ds, kt)
        block(j, True)
        def qstep(i, _):
            block(i, False); return 0
        lax.fori_loop(j + 1, nb, qstep, 0)
        qkv[ks, lanes(1)] = dk[...].astype(bf16)
        qkv[ks, lanes(2)] = dv[...].astype(bf16)
        @pl.when(j == nb - 1)
        def _():
            def fin(i, _):
                qs = pl.ds(pl.multiple_of(i * B, B), B)
                d = dq[i]
                qkv[qs, lanes(0)] = (jnp.where(half, d[:B], d[B:]) * 0.125).astype(bf16)
                return 0
            lax.fori_loop(0, nb, fin, 0)
        return 0
    lax.fori_loop(0, pairs * nb, unit, 0)
    grads(2)
    fqs[2].start()
    for k in range(2):
        sl = pl.ds(pl.multiple_of(other * rows + k * hr, hr), hr)
        dsend[k * hr:(k + 1) * hr, :] = nt(qkv[sl, :], wown[...]).astype(bf16)
        c_da[k].start()
    fqs[2].after_b()
    g1_o[...] = f1.result()
    for k in range(2):
        sl = pl.ds(pl.multiple_of(tp * rows + k * hr, hr), hr)
        da[k * hr:(k + 1) * hr, :] = nt(qkv[sl, :], wown[...])
        if k == 0: fqs[2].after_a()
    l_t.wait(); l_y.wait()
    for c in c_da: c.wait_recv()
    gain = vec[0:1, :]
    def fin(r, _):
        sl = pl.ds(pl.multiple_of(r * 256, 256), 256)
        d = da[sl, :] + drecv[sl, :].astype(f32)
        xh, xr = stats(tok[sl, :].astype(f32))
        gtok[sl, :] = (dy[sl, :].astype(f32) + ln_back(d, xh, xr, gain)).astype(bf16)
        return 0
    def collect(p):
        r = fqs[p].result()
        fqk[:, p * 384:(p + 1) * 384] = r[:, :384]
        if p == pairs - 1: fqk[:, pairs * 384:] = r[:, 384:]
    for p in range(pairs - 1): collect(p)
    lax.fori_loop(0, rows // 256, fin, 0)
    collect(pairs - 1)
    c_xq.start()
    c_xo.wait_recv()
    mine = fo[mine_n, :]
    gwo_o[:, :W] = jnp.where(first, mine, xo[...])
    gwo_o[:, W:] = jnp.where(first, xo[...], mine)
    c_xq.wait_recv()
    for p in range(pairs):
        for k in range(3):
            src = p * 384 + k * 128
            mine = fqk[mine_n, src:src + 128]
            oth = xq[:, src:src + 128]
            c0 = k * D + p * 128
            gq_o[:, c0:c0 + 128] = jnp.where(first, mine, oth)
            gq_o[:, c0 + W:c0 + W + 128] = jnp.where(first, oth, mine)
    pre_o[...] = fqk[mine_n, 3 * W:] + xq[:, 3 * W:]
    for c in copy.all: c.wait_send()

def k45(lengths, xh, wown, do, delta, lse, vec, gvec, gmid, gwo, qkv, tok, dy, g1, g2, B=512):
    rows, D = tok.shape
    W = D // 2; pairs = W // 128; nb = 2 * rows // B
    V, A = pl.BlockSpec(memory_space=pltpu.VMEM), pl.BlockSpec(memory_space=pl.ANY)
    sds = jax.ShapeDtypeStruct
    hid = g1.shape[3]
    M = pltpu.VMEM
    e24t, e96t = [c.T for c in consts_np(D)[:2]]
    def flow(r, c, t, lead=()):
        return [M(lead + (4, 4, r, c), t), M(lead + (2, 4, r, c), t), M(lead + (4, r, c), t), M(lead + (3, r, c), t)]
    fc = flow(hid, D, bf16)
    fc = [fc[0], M((4, 4, hid, D), bf16)] + fc[1:]
    wo = flow(48, W, bf16)
    wo = [wo[0], M((D, W), bf16)] + wo[1:]
    sm = flow(8, 128, f32)
    return pl.pallas_call(functools.partial(k45_kernel, B=B, pairs=pairs), name="backward",
        out_shape=(sds((rows, D), bf16), sds((D // 32, 3 * D), f32), sds((D // 32, D), f32), sds((hid, D), f32), sds((hid, D), f32), sds((8, 128), f32), sds((D // 32, 128), f32)),
        in_specs=[pl.BlockSpec(memory_space=pltpu.SMEM)] + [V] * 8 + [A] * 8,
        out_specs=(V,) * 7,
        scratch_shapes=[M((2 * rows, 3 * W), bf16), M((2 * rows, D), bf16), M((D, 3 * W), bf16), M((D, D), bf16), M((rows, D), bf16), M((rows, D), dy.dtype), M((2 * rows, W), bf16), M((8, 2 * rows), f32),
                        M((2 * rows, 128), bf16), M((2 * rows, 128), bf16), M((nb, 2 * B, 256), bf16), M((nb, 2 * B, 128), bf16), M((nb, 2 * B, 128), f32),
                        M((B, 128), f32), M((B, 128), f32)] + fc + fc + wo + flow(48, W, bf16) * (pairs - 1) + flow(48, W + 128, bf16) +
                       [M((4, 4, 2, 8, 128), f32), M((4, 4, 8, 128), f32)] + sm +
                       [M((rows, D), f32), M((rows, D), bf16), M((rows, D), bf16), M((48, W), f32), M((24, W), f32), M((48, 3 * W + 128), f32), M((24, 3 * W + 128), f32),
                        M((D, 128), f32), M((D, 128), f32), M((D, 128), f32), M((D, 128), f32),
                        pltpu.SemaphoreType.DMA((64,)), pltpu.SemaphoreType.DMA((64,)), pltpu.SemaphoreType.DMA((8,))],
        compiler_params=pltpu.CompilerParams(vmem_limit_bytes=63 << 20, collective_id=1, has_side_effects=True))(
            lengths, do, delta, lse, vec, gvec, gmid, jnp.asarray(e24t, bf16), jnp.asarray(e96t, bf16), qkv, xh, wown, gwo, tok, dy, g1, g2)

def local_fast(tokens, cotangent, lengths, qkv_weight, out_weight, pre_gain, pre_shift, sub_gain, sub_shift,
          ffn_gain, ffn_shift, fc1_weight, mid_gain, mid_shift, fc2_weight):
    rows, D = tokens.shape
    vpk = pack_vectors([pre_gain, pre_shift, sub_gain, sub_shift, ffn_gain, ffn_shift], [mid_gain, mid_shift])
    xh16, qkv, wown, o, lse, vec, mid, wo, fc1, fc2 = k12(lengths, tokens, qkv_weight, out_weight, vpk, fc1_weight, fc2_weight)
    block_out, dy, do, delta, gwo, g1, g2, gvec, gmid = ffn(o, tokens, cotangent, wo.reshape(D, D), fc1.reshape(4 * D, D), fc2.reshape(4 * D, D), vec, mid)
    shape = (4, 4, 2, fc1_weight.shape[0], D)
    gtok, gq, gwo, g1, g2, small, pre = k45(lengths, xh16, wown.reshape(D, -1), do, delta, lse, vec, gvec, gmid, gwo, qkv, tokens, dy, g1.reshape(shape), g2.reshape(shape))
    n, m = pre_gain.shape[0], mid_gain.shape[0]
    return (block_out, gtok, gq, gwo, pre[:, 0], pre[:, 1], small[2, :n], small[3, :n], small[4, :n], small[5, :n],
            g1, small[6, :m], small[7, :m], g2)

def norm(v):
    return stats(v)


def local_any(tokens, cotangent, lengths, qkv_weight, out_weight, pre_gain, pre_shift, sub_gain, sub_shift,
          ffn_gain, ffn_shift, fc1_weight, mid_gain, mid_shift, fc2_weight):
    rows, D = tokens.shape
    W = D // 2
    tp = lax.axis_index("tp")
    both = ("dp", "tp")
    gather = lambda a: lax.all_gather(a, both, axis=0, tiled=True)
    small = gather(jnp.stack([pre_gain, pre_shift, sub_gain, sub_shift, ffn_gain, ffn_shift], axis=1)).astype(f32).T
    mid = gather(jnp.stack([mid_gain, mid_shift], axis=1)).astype(f32).T
    wq = gather(qkv_weight)
    wo, fc1, fc2 = gather(out_weight), gather(fc1_weight), gather(fc2_weight)
    wown = lax.dynamic_index_in_dim(wq.reshape(D, 3, 2, W), tp, 2, keepdims=False).reshape(D, 3 * W)
    x = tokens.astype(f32)
    xh, xr = norm(x)
    a = (xh * small[0] + small[1]).astype(bf16)
    afull = lax.all_gather(a, "tp", axis=0, tiled=True)
    qkv = nn(afull, wown).astype(bf16)
    o_own, lse = attn_fwd(lengths, qkv, B=512)
    o = lax.all_to_all(o_own, "tp", 0, 1, tiled=True)
    vec = jnp.concatenate([small, jnp.zeros((2, D), f32)], axis=0)
    block_out, dy, do, delta, gwo, gfc1, gfc2, gvec, gmid = ffn(
        o, tokens, cotangent, wo, fc1, fc2, vec, jnp.concatenate([mid, jnp.zeros((6, 4 * D), f32)], axis=0))
    do_own = lax.all_to_all(do, "tp", 1, 0, tiled=True)
    dl_own = lax.all_to_all(delta, "tp", 0, 1, tiled=True)
    dqkv = attn_bwd(lengths, qkv, do_own, lse, dl_own, B=512)
    gq = tn(afull, dqkv)
    da = lax.psum_scatter(nt(dqkv, wown), "tp", scatter_dimension=0, tiled=True)
    grad_tokens = (dy.astype(f32) + ln_back(da, xh, xr, small[0])).astype(bf16)
    scatter = lambda v: lax.psum_scatter(v, both, scatter_dimension=0, tiled=True)
    gq = lax.psum_scatter(gq, "dp", scatter_dimension=0, tiled=True)
    n = gq.shape[0] // 2
    gq = lax.all_to_all(gq.reshape(2, n, 3, 1, W), "tp", 0, 3, tiled=True).reshape(n, 3 * D)
    small_grads = scatter(jnp.concatenate([jnp.stack([colsum(da * xh)[0], colsum(da)[0]]), gvec[2:6]], axis=0).T).T
    mid_grads = scatter(gmid[6:8].T).T
    gwo = scatter(gwo.astype(f32))
    gfc1 = scatter(gfc1.reshape(-1, D).astype(f32))
    gfc2 = scatter(gfc2.reshape(-1, D).astype(f32))
    return (block_out, grad_tokens, gq, gwo, small_grads[0], small_grads[1], small_grads[2], small_grads[3],
            small_grads[4], small_grads[5], gfc1, mid_grads[0], mid_grads[1], gfc2)


def local(*arrays):
    fits = lax.axis_size("dp") == 16 and lax.axis_size("tp") == 2
    return (local_fast if fits else local_any)(*arrays)


def solution(mesh):
    two, one = P(("dp", "tp"), None), P(("dp", "tp"))
    return jax.shard_map(
        local,
        mesh=mesh,
        in_specs=(two, two, P("dp", None), two, two, one, one, one, one, one, one, two, one, one, two),
        out_specs=(two, two, two, two, one, one, one, one, one, one, two, one, one, two),
        check_vma=False,
    )
```

```python
import functools

import jax
import jax.numpy as jnp
import numpy as np
from jax import lax
from jax.experimental import pallas as pl
from jax.experimental.pallas import tpu as pltpu
from jax.sharding import PartitionSpec as P

f32, bf16 = jnp.float32, jnp.bfloat16
EPS = 1e-5
BIG = 1e30


def nt(a, b):
    return lax.dot_general(a, b, (((1,), (1,)), ((), ())), preferred_element_type=f32)


def nn(a, b):
    return lax.dot_general(a, b, (((1,), (0,)), ((), ())), preferred_element_type=f32)


def tn(a, b):
    return lax.dot_general(a, b, (((0,), (0,)), ((), ())), preferred_element_type=f32)

def doc_features(len_ref, rows, fq, fk):
    lane = lax.broadcasted_iota(jnp.int32, (1, 128), 1)
    lo = jnp.zeros((1, 128), jnp.int32); hi = jnp.zeros((1, 128), jnp.int32)
    run = jnp.int32(0)
    for d in range(8):
        nxt = run + len_ref[0, d]
        lo = jnp.where(lane == d, run, lo); hi = jnp.where(lane == d, nxt, hi)
        run = nxt
    def body(r, _):
        place = lax.broadcasted_iota(jnp.int32, (256, 128), 0) + r * 256
        hit = (place >= lo) & (place < hi)
        sl = pl.ds(pl.multiple_of(r * 256, 256), 256)
        fq[sl, :] = jnp.where(hit, 1.0, 0.0).astype(bf16)
        fk[sl, :] = jnp.where(hit | (lane >= 8), 0.0, -BIG).astype(bf16)
        return 0
    lax.fori_loop(0, rows // 256, body, 0)

def fwd_t(len_ref, qkv, o_ref, lse_ref, fq, fk, q2, st_s, m_s, l_s, acc, *, B, pairs, variant):
    rows = qkv.shape[0]; nb = rows // B; W = pairs * 128
    doc_features(len_ref, rows, fq, fk)
    half = lax.broadcasted_iota(jnp.int32, (1, 128), 1) < 64
    causal = lax.broadcasted_iota(jnp.int32, (B, B), 0) <= lax.broadcasted_iota(jnp.int32, (B, B), 1)
    causal = jnp.concatenate([causal, causal], axis=1)
    for p in range(pairs):
        def qstep(i, _, p=p):
            qs = pl.ds(pl.multiple_of(i * B, B), B)
            q = qkv[qs, p * 128:(p + 1) * 128] * bf16(0.125)
            fqb = fq[qs, :]
            z = jnp.zeros_like(q)
            q2[...] = jnp.concatenate([
                jnp.concatenate([jnp.where(half, q, z), fqb], axis=1),
                jnp.concatenate([jnp.where(half, z, q), fqb], axis=1)], axis=0)
            def score(j):
                ks = pl.ds(pl.multiple_of(j * B, B), B)
                k2 = jnp.concatenate([qkv[ks, W + p * 128:W + (p + 1) * 128], fk[ks, :]], axis=1)
                return nt(k2, q2[...])
            def vblk(j):
                ks = pl.ds(pl.multiple_of(j * B, B), B)
                return qkv[ks, 2 * W + p * 128:2 * W + (p + 1) * 128]
            if variant == "online":
                def block(j, masked, first):
                    s = score(j)
                    if masked: s = jnp.where(causal, s, -BIG)
                    mx = jnp.max(s, axis=0, keepdims=True)
                    if first: mn = mx
                    else:
                        mo = m_s[...]
                        mn = jnp.maximum(mo, mx); al = jnp.exp(mo - mn)
                    e = jnp.exp(s - mn)
                    su = jnp.sum(e, axis=0, keepdims=True)
                    pv = tn(vblk(j), e.astype(bf16))
                    if first: l_s[...] = su; acc[...] = pv
                    else: l_s[...] = l_s[...] * al + su; acc[...] = acc[...] * al + pv
                    m_s[...] = mn
                block(i, True, True)
                def kstep(j, _):
                    block(j, False, False); return 0
                lax.fori_loop(0, i, kstep, 0)
                m = m_s[...]; l = l_s[...]
            else:
                def part(s): return jnp.max(s.reshape(B // 8, 8, 2 * B), axis=0)
                s = jnp.where(causal, score(i), -BIG)
                st_s[i] = s
                def pass1(j, m8):
                    s = score(j); st_s[j] = s
                    return jnp.maximum(m8, part(s))
                m8 = lax.fori_loop(0, i, pass1, part(s))
                m = jnp.max(m8, axis=0, keepdims=True)
                acc[...] = jnp.zeros_like(acc)
                def pass2(j, l8):
                    e = jnp.exp(st_s[j] - m)
                    acc[...] += tn(vblk(j), e.astype(bf16))
                    return l8 + jnp.sum(e.reshape(B // 8, 8, 2 * B), axis=0)
                l8 = lax.fori_loop(0, i + 1, pass2, jnp.zeros((8, 2 * B), f32))
                l = jnp.sum(l8, axis=0, keepdims=True)
            r = 1.0 / l
            a = acc[...] * r
            ot = jnp.concatenate([a[:64, :B], a[64:, B:]], axis=0)
            o_ref[qs, p * 128:(p + 1) * 128] = ot.T.astype(o_ref.dtype)
            lse = m + jnp.log(l)
            lse_ref[2 * p:2 * p + 1, qs] = lse[:, :B]
            lse_ref[2 * p + 1:2 * p + 2, qs] = lse[:, B:]
            return 0
        lax.fori_loop(0, nb, qstep, 0)

def attn_fwd(lengths, qkv, B=256, variant="online"):
    rows, w3 = qkv.shape; W = w3 // 3; pairs = W // 128; nb = rows // B
    return pl.pallas_call(functools.partial(fwd_t, B=B, pairs=pairs, variant=variant), name="attn_fwd",
        out_shape=(jax.ShapeDtypeStruct((rows, W), bf16), jax.ShapeDtypeStruct((8, rows), f32)),
        in_specs=[pl.BlockSpec(memory_space=pltpu.SMEM), pl.BlockSpec(memory_space=pltpu.VMEM)],
        out_specs=(pl.BlockSpec(memory_space=pltpu.VMEM),) * 2,
        scratch_shapes=[pltpu.VMEM((rows, 128), bf16), pltpu.VMEM((rows, 128), bf16), pltpu.VMEM((2 * B, 256), bf16),
                        pltpu.VMEM((nb if variant != "online" else 1, B, 2 * B), f32),
                        pltpu.VMEM((1, 2 * B), f32), pltpu.VMEM((1, 2 * B), f32), pltpu.VMEM((128, 2 * B), f32)],
        compiler_params=pltpu.CompilerParams(vmem_limit_bytes=56 << 20))(lengths, qkv)

def bwd_kernel(len_ref, qkv, do_ref, lse_ref, dl_ref, out, fq, fk, q2, do2, dq, dk, dv, *, B, pairs, mode):
    rows = qkv.shape[0]; nb = rows // B; W = pairs * 128
    doc_features(len_ref, rows, fq, fk)
    half = lax.broadcasted_iota(jnp.int32, (1, 128), 1) < 64
    causal = lax.broadcasted_iota(jnp.int32, (B, B), 0) <= lax.broadcasted_iota(jnp.int32, (B, B), 1)
    causal = jnp.concatenate([causal, causal], axis=1)
    for p in range(pairs):
        def prep(i, _, p=p):
            qs = pl.ds(pl.multiple_of(i * B, B), B)
            q = qkv[qs, p * 128:(p + 1) * 128] * bf16(0.125)
            d = do_ref[qs, p * 128:(p + 1) * 128]
            fqb = fq[qs, :]
            z = jnp.zeros_like(q)
            q2[i] = jnp.concatenate([
                jnp.concatenate([jnp.where(half, q, z), fqb], axis=1),
                jnp.concatenate([jnp.where(half, z, q), fqb], axis=1)], axis=0)
            do2[i] = jnp.concatenate([jnp.where(half, d, z), jnp.where(half, z, d)], axis=0)
            dq[i] = jnp.zeros(dq.shape[1:], f32)
            return 0
        lax.fori_loop(0, nb, prep, 0)
        def kstep(j, _, p=p):
            ks = pl.ds(pl.multiple_of(j * B, B), B)
            kt = qkv[ks, W + p * 128:W + (p + 1) * 128]
            v = qkv[ks, 2 * W + p * 128:2 * W + (p + 1) * 128]
            k2 = jnp.concatenate([kt, fk[ks, :]], axis=1)
            def block(i, masked, first):
                qs = pl.ds(pl.multiple_of(i * B, B), B)
                lse = jnp.concatenate([lse_ref[2 * p:2 * p + 1, qs], lse_ref[2 * p + 1:2 * p + 2, qs]], axis=1)
                dl = jnp.concatenate([dl_ref[2 * p:2 * p + 1, qs], dl_ref[2 * p + 1:2 * p + 2, qs]], axis=1)
                qq = q2[i]; dd = do2[i]
                st = nt(k2, qq)
                pt = jnp.exp(st - lse)
                if masked: pt = jnp.where(causal, pt, 0.0)
                dp = nt(v, dd)
                ds = (pt * (dp - dl)).astype(bf16)
                dvp = nn(pt.astype(bf16), dd)
                dkp = nn(ds, qq[:, :128])
                if first: dv[...] = dvp; dk[...] = dkp
                else: dv[...] += dvp; dk[...] += dkp
                if mode == "tn":
                    dq[i] += tn(ds, kt)
                else:
                    dq[i] += tn(kt, ds)
            block(j, True, True)
            def qstep(i, _):
                block(i, False, False); return 0
            lax.fori_loop(j + 1, nb, qstep, 0)
            out[ks, W + p * 128:W + (p + 1) * 128] = dk[...].astype(bf16)
            out[ks, 2 * W + p * 128:2 * W + (p + 1) * 128] = dv[...].astype(bf16)
            return 0
        lax.fori_loop(0, nb, kstep, 0)
        def fin(i, _, p=p):
            qs = pl.ds(pl.multiple_of(i * B, B), B)
            if mode == "tn":
                d = dq[i]
                r = jnp.where(half, d[:B], d[B:])
            else:
                d = dq[i]
                r = jnp.concatenate([d[:64, :B], d[64:, B:]], axis=0).T
            out[qs, p * 128:(p + 1) * 128] = (r * 0.125).astype(bf16)
            return 0
        lax.fori_loop(0, nb, fin, 0)

def attn_bwd(lengths, qkv, do, lse, dl, B=256, mode="tn"):
    rows, w3 = qkv.shape; W = w3 // 3; pairs = W // 128; nb = rows // B
    dqs = (nb, 2 * B, 128) if mode == "tn" else (nb, 128, 2 * B)
    return pl.pallas_call(functools.partial(bwd_kernel, B=B, pairs=pairs, mode=mode), name="attn_bwd",
        out_shape=jax.ShapeDtypeStruct((rows, w3), bf16),
        in_specs=[pl.BlockSpec(memory_space=pltpu.SMEM)] + [pl.BlockSpec(memory_space=pltpu.VMEM)] * 4,
        out_specs=pl.BlockSpec(memory_space=pltpu.VMEM),
        scratch_shapes=[pltpu.VMEM((rows, 128), bf16), pltpu.VMEM((rows, 128), bf16), pltpu.VMEM((nb, 2 * B, 256), bf16),
                        pltpu.VMEM((nb, 2 * B, 128), bf16), pltpu.VMEM(dqs, f32), pltpu.VMEM((B, 128), f32), pltpu.VMEM((B, 128), f32)],
        compiler_params=pltpu.CompilerParams(vmem_limit_bytes=56 << 20))(lengths, qkv, do, lse, dl)

def stats(v):
    n = v.shape[-1]
    m = jnp.sum(v, axis=-1, keepdims=True) * (1.0 / n)
    c = v - m
    s = jnp.sum(c * c, axis=-1, keepdims=True) * (1.0 / n)
    r = lax.rsqrt(s + EPS)
    return c * r, r
def ln_back(w, vh, r, g):
    n = vh.shape[-1]
    wg = w * g
    a = jnp.sum(wg, axis=-1, keepdims=True) * (1.0 / n)
    b = jnp.sum(wg * vh, axis=-1, keepdims=True) * (1.0 / n)
    return r * (wg - a - vh * b)
def colsum(v): return jnp.sum(v, axis=0, keepdims=True)


def gelu_parts(h):
    return 0.5 + 0.5 * lax.erf(h * 0.7071067811865476), jnp.exp2(h * h * -0.7213475204444817) * 0.3989422804014327

def ffn_kernel(vec, mid, sel, o_h, x_h, g_h, wo_h, fc1_h, fc2_h,
               delta_ref, gvec, gmid, gfc1, gfc2, out_ref, dy_h, do_h, gwo_h,
               o_ref, x_ref, g_ref, wo, fc1, fc2, dy_ref, do_ref, gwo,
               h_s, u_s, d_s, dm_s, m_s, dh_s, c_s, b_s, y_s, dc_s, st_s, ws, *, T, NT, NC, SR, UT):
    step = pl.program_id(0)
    rows = x_ref.shape[0]
    ff, D = fc1.shape
    K = ff // NC
    NS = NT // UT
    ins = [pltpu.make_async_copy(h, v, ws.at[k]) for k, (h, v) in enumerate(
        ((o_h, o_ref), (wo_h, wo), (x_h, x_ref), (fc1_h, fc1), (g_h, g_ref), (fc2_h, fc2)))]
    outs = [pltpu.make_async_copy(v, h, ws.at[6 + k]) for k, (h, v) in enumerate(
        ((dy_h, dy_ref), (do_h, do_ref), (gwo_h, gwo)))]
    sg, sb, fg, fb = [vec[k:k + 1, :] for k in range(2, 6)]
    tiles = [slice(t * T, (t + 1) * T) for t in range(NT)]
    subs = [slice(r * SR, (r + 1) * SR) for r in range(T // SR)]
    cols = [slice(c * K, (c + 1) * K) for c in range(NC)]
    def fold(v):
        r = v[:, :128]
        for k in range(1, v.shape[1] // 128): r = r + v[:, k * 128:(k + 1) * 128]
        return r
    @pl.when(step == 0)
    def _():
        for l in ins: l.start()
        gvec[...] = jnp.zeros_like(gvec); gmid[...] = jnp.zeros_like(gmid)
        ins[0].wait(); ins[1].wait(); ins[2].wait()
        bs = []
        for sl in tiles:
            oh, _r = stats(o_ref[sl, :].astype(f32))
            b_s[sl, :] = (oh * sg + sb).astype(bf16)
        for sl in tiles:
            y_s[sl, :] = x_ref[sl, :].astype(f32) + nn(b_s[sl, :], wo[...])
        for sl in tiles:
            yh, _r = stats(y_s[sl, :])
            c_s[sl, :] = (yh * fg + fb).astype(bf16)
        ins[3].wait()
    base = jnp.minimum(step, NS - 1) * T
    rs = pl.ds(pl.multiple_of(base, T), T)
    sub_rows = lambda s: pl.ds(pl.multiple_of(base + s.start, SR), SR)
    total = lambda k: jnp.sum(jnp.sum(st_s[k], axis=0), axis=1, keepdims=True) * (1.0 / ff)
    def moments():
        mu = total(0)
        return mu, lax.rsqrt(total(1) - mu * mu + EPS)
    @pl.when(step < NS)
    def _():
        h_s[0] = nt(c_s[rs, :], fc1[cols[0], :])
        for c in range(NC):
            for s in subs:
                h = h_s[c % 2, s, :]
                phi, den = gelu_parts(h)
                u = h * phi
                u_s[s, cols[c]] = u
                d_s[s, cols[c]] = phi + h * den
                st_s[0, c, s, :] = fold(u); st_s[1, c, s, :] = fold(u * u)
            if c + 1 < NC: h_s[(c + 1) % 2] = nt(c_s[rs, :], fc1[cols[c + 1], :])
    @pl.when(step == 0)
    def _():
        ins[4].wait(); ins[5].wait()
    @pl.when(step < NS)
    def _():
        mu, R = moments()
        dm_s[:, cols[0]] = nt(g_ref[rs, :], fc2[cols[0], :])
        for c in range(NC):
            gain = mid[0:1, cols[c]]; shift = mid[1:2, cols[c]]
            g6 = jnp.zeros((8, K), f32); g7 = jnp.zeros((8, K), f32)
            for s in subs:
                uh = (u_s[s, cols[c]] - mu[s]) * R[s]
                u_s[s, cols[c]] = uh
                m_s[sub_rows(s), cols[c]] = (uh * gain + shift).astype(bf16)
                dm = dm_s[s, cols[c]]
                e = dm * gain
                dm_s[s, cols[c]] = e
                q = dm * uh
                g6 += jnp.sum(q.reshape(SR // 8, 8, K), axis=0); g7 += jnp.sum(dm.reshape(SR // 8, 8, K), axis=0)
                st_s[2, c, s, :] = fold(e); st_s[3, c, s, :] = fold(e * uh)
            gmid[6:7, cols[c]] += colsum(g6)
            gmid[7:8, cols[c]] += colsum(g7)
            if c + 1 < NC: dm_s[:, cols[c + 1]] = nt(g_ref[rs, :], fc2[cols[c + 1], :])
    @pl.when(step < NS)
    def _():
        R = moments()[1]
        se = total(2); seu = total(3)
        for c in range(NC):
            for s in subs:
                dh = (dm_s[s, cols[c]] - se[s] - u_s[s, cols[c]] * seu[s]) * R[s] * d_s[s, cols[c]]
                dh_s[sub_rows(s), cols[c]] = dh.astype(bf16)
            if c == 0:
                out_ref[rs, :] = (y_s[rs, :] + nn(m_s[rs, :], fc2[...])).astype(bf16)
    @pl.when(step < NS)
    def _():
        dc_s[rs, :] = nn(dh_s[rs, :], fc1[...])
    def grads(lanes):
        gfc2[0] = tn(m_s[:, lanes], g_ref[...]).astype(bf16)
        gfc1[0] = tn(dh_s[:, lanes], c_s[...]).astype(bf16)
    @pl.when(step == NS)
    def _():
        hs = []
        for sl in tiles:
            yh, yr = stats(y_s[sl, :])
            dc = dc_s[sl, :]
            gvec[4:5, :] += colsum(dc * yh)
            gvec[5:6, :] += colsum(dc)
            dy_ref[sl, :] = (g_ref[sl, :].astype(f32) + ln_back(dc, yh, yr, fg)).astype(bf16)
        for sl in tiles:
            dc_s[sl, :] = nt(dy_ref[sl, :], wo[...])
        for sl in tiles:
            dbn = dc_s[sl, :]
            o = o_ref[sl, :].astype(f32)
            oh, orr = stats(o)
            gvec[2:3, :] += colsum(dbn * oh)
            gvec[3:4, :] += colsum(dbn)
            do = ln_back(dbn, oh, orr, sg).astype(bf16)
            do_ref[sl, :] = do
            pr = do.astype(f32) * o
            hi = pr.astype(bf16)
            lo = (pr - hi.astype(f32)).astype(bf16)
            delta_ref[:, sl] = nt(sel[...], hi) + nt(sel[...], lo)
        grads(cols[0])
        gwo[...] = tn(b_s[...], dy_ref[...]).astype(bf16)
        for c in outs: c.start()
    @pl.when(step > NS)
    def _():
        grads(pl.ds(pl.multiple_of((step - NS) * K, K), K))
    @pl.when(step == NS + NC - 1)
    def _():
        for c in outs: c.wait()

def ffn(o, x, g, wo, fc1, fc2, vec, mid, T=256, K=512, dt=f32, SR=16, UT=1):
    rows, D = x.shape; ff = fc1.shape[0]; NC = ff // K; NT = rows // T; NS = NT // UT
    head = np.arange(D)[None] // 64
    sel = jnp.asarray((np.arange(16)[:, None] == head // (D // 128) * 8 + head % (D // 128)).astype(np.float32), bf16)
    one = dict(pipeline_mode=pl.Buffered(1))
    full = lambda *s: pl.BlockSpec(s, lambda i: (0,) * len(s), **one)
    A = pl.BlockSpec(memory_space=pl.ANY)
    chunk = pl.BlockSpec((1, K, D), lambda s: (jnp.maximum(s - NS, 0), 0, 0))
    sds = jax.ShapeDtypeStruct
    M = pltpu.VMEM
    act = sds((rows, D), bf16)
    delta, gvec, gmid, g1, g2, out, dy, do, gwo = pl.pallas_call(functools.partial(ffn_kernel, T=T, NT=NT, NC=NC, SR=SR, UT=UT), name="ffn",
        grid=(NS + NC,),
        in_specs=[full(8, D), full(8, ff), full(16, D)] + [A] * 6,
        out_specs=[full(16, rows), full(8, D), full(8, ff), chunk, chunk, full(rows, D)] + [A] * 3,
        out_shape=[sds((16, rows), f32), sds((8, D), f32), sds((8, ff), f32), sds((NC, K, D), bf16), sds((NC, K, D), bf16),
                   act, act, act, sds((D, D), bf16)],
        scratch_shapes=[M((rows, D), bf16), M((D, D), bf16), M((rows, D), bf16)][:0] + [M((rows, D), bf16), M((rows, D), bf16), M((rows, D), bf16),
                        M((D, D), bf16), M((ff, D), bf16), M((ff, D), bf16), M((rows, D), bf16), M((rows, D), bf16), M((D, D), bf16),
                        M((2, T, K), f32), M((T, ff), f32), M((T, ff), f32), M((T, ff), f32),
                        M((rows, ff), bf16), M((rows, ff), bf16), M((rows, D), bf16), M((rows, D), bf16), M((rows, D), f32), M((rows, D), f32),
                        M((4, NC, T, 128), f32), pltpu.SemaphoreType.DMA((10,))],
        compiler_params=pltpu.CompilerParams(vmem_limit_bytes=63 << 20, dimension_semantics=("arbitrary",)))(
            vec, mid, sel, o, x, g, wo, fc1, fc2)
    return out, dy, do, delta, gwo, g1, g2, gvec, gmid

MESH = pl.DeviceIdType.MESH

def place():
    dp, tp = lax.axis_index("dp"), lax.axis_index("tp")
    q, z = dp % 4, dp // 4
    dx = 1 - 2 * (dp % 2)
    dy = 2 - 4 * ((dp // 2) % 2)
    a, b = (1 - tp) * dx + tp * dy, tp * dx + (1 - tp) * dy
    return dict(dp=dp, tp=tp, z=z, q=q, qa=q + a, qb=q + b, qab=q + a + b,
                a=(dp + a, tp), b=(dp + b, tp), peer=(dp, 1 - tp),
                zs=[((dp + 4 * k) % 16, tp) for k in (1, 2, 3)], zi=[(z + k) % 4 for k in (1, 2, 3)])

def enter(w):
    bar = pltpu.get_barrier_semaphore()
    for d in [w["a"], w["b"], w["peer"]] + w["zs"]:
        pl.semaphore_signal(bar, inc=1, device_id=d, device_id_type=MESH)
    pl.semaphore_wait(bar, 6)

class Copy:
    def __init__(self, ss, rs):
        self.ss, self.rs, self.n, self.all = ss, rs, 0, []
    def __call__(self, src, dst, dev):
        c = pltpu.make_async_remote_copy(src_ref=src, dst_ref=dst, send_sem=self.ss.at[self.n], recv_sem=self.rs.at[self.n],
                                         device_id=dev, device_id_type=MESH)
        self.n += 1
        self.all.append(c)
        return c

def go_all(cs):
    for c in cs: c.start()

def got(cs):
    for c in cs: c.wait_recv()

class Gather:
    def __init__(self, copy, w, src, slot, view, peer):
        q, qa, qb, qab = w["q"], w["qa"], w["qb"], w["qab"]
        own = slot(w["z"], q)
        far = [slot(z, q) for z in w["zi"]]
        self.z = [copy(src, own, d) for d in w["zs"]]
        self.a = [copy(src, own, w["a"])] + [copy(s, s, w["a"]) for s in far]
        self.b = [copy(src, own, w["b"])] + [copy(s, s, w["b"]) for s in far]
        self.ab = [copy(view(qa), view(qa), w["b"])]
        self.p = [copy(view(c), view(c), w["peer"]) for c in (q, qa, qb, qab)] if peer else []
    def start(self):
        go_all(self.z + self.a[:1] + self.b[:1])
    def after_z(self):
        got(self.z)
        for k in (1, 2, 3): go_all([self.a[k], self.b[k]])
        go_all(self.p[:1])
    def after_a(self):
        got(self.a)
        go_all(self.ab + self.p[1:2])
    def after_b(self):
        got(self.b + self.ab)
        go_all(self.p[2:])
    def finish(self):
        got(self.p)

N_COPIES = 112

def k12_kernel(len_ref, tok, wq, wos, vpk, e24, e96, rsel, fc1s, fc2s,
               o_out, lse_ref, vec, mid, xh_h, qkv_h, wown_h, wo_h, fc1_h, fc2_h,
               xh16, qkv, wown, afull, xp, vbuf, sb, rb, woc, o_loc, fq, fk, q2, m_s, l_s, acc, ss, rs, ls, *, B, pairs, stage=9):
    w = place()
    tp = w["tp"]
    rows, D = tok.shape
    W = pairs * 128
    send = Copy(ss, rs)
    first = tp == 0
    sb[...] = jnp.zeros_like(sb)
    pick = lambda c0, n: (jnp.where(first, wq[:, c0:c0 + W], wq[:, c0 + W:c0 + 2 * W]).astype(bf16),
                          jnp.where(first, wq[:, c0 + W:c0 + 2 * W], wq[:, c0:c0 + W]).astype(bf16))
    mine = []
    for k in range(3):
        own, oth = pick(k * D, W)
        mine.append(own); sb[0:24, k * W:(k + 1) * W] = oth
    own_o = jnp.where(first, wos[:, :W], wos[:, W:])
    sb[0:24, 3 * W:4 * W] = jnp.where(first, wos[:, W:], wos[:, :W])
    vbuf[w["z"], w["q"], tp] = vpk[...]
    loc = [pltpu.make_async_copy(fc1s, fc1_h.at[w["z"], w["q"], tp], ls.at[0]),
           pltpu.make_async_copy(fc2s, fc2_h.at[w["z"], w["q"], tp], ls.at[1])]
    for c in loc: c.start()
    enter(w)
    cpre = send(sb, rb, w["peer"])
    gv = Gather(send, w, vbuf.at[w["z"], w["q"], tp], lambda z, q: vbuf.at[z, q, tp], lambda q: vbuf.at[:, q, tp], True)
    cx = send(tok, xp, w["peer"])
    gq = [Gather(send, w, wown.at[p, w["z"], w["q"]], lambda z, q, p=p: wown.at[p, z, q], lambda q, p=p: wown.at[p, :, q], False)
          for p in range(pairs)]
    keep = [pltpu.make_async_copy(v, h, ls.at[3 + k]) for k, (v, h) in enumerate(((xh16, xh_h), (qkv, qkv_h), (wown, wown_h)))]
    cols = pl.ds(pl.multiple_of(tp * W, 128), W)
    go = Gather(send, w, woc, lambda z, q: wo_h.at[z, q, :, cols], lambda q: wo_h.at[:, q, :, cols], True)
    g1 = Gather(send, w, fc1s, lambda z, q: fc1_h.at[z, q, tp], lambda q: fc1_h.at[:, q, tp], True)
    g2 = Gather(send, w, fc2s, lambda z, q: fc2_h.at[z, q, tp], lambda q: fc2_h.at[:, q, tp], True)
    peer_rows = pl.ds(pl.multiple_of((1 - tp) * rows, rows), rows)
    co = [send(o_loc.at[peer_rows, p * 128:(p + 1) * 128],
               o_out.at[:, pl.ds(pl.multiple_of(tp * W + p * 128, 128), 128)], w["peer"]) for p in range(pairs)]
    cpre.start()
    gv.start()
    cx.start()
    cpre.wait_recv()
    other = rb[0:24, :].astype(f32)
    me = jnp.concatenate(mine + [own_o], axis=1).astype(f32)
    both = jnp.concatenate([jnp.where(first, me, other), jnp.where(first, other, me)], axis=0).astype(bf16)
    for p in range(pairs):
        for k in range(3):
            wown[p, w["z"], w["q"], :, k * 128:(k + 1) * 128] = both[:, k * W + p * 128:k * W + (p + 1) * 128]
    woc[...] = both[:, 3 * W:]
    gq[0].start()
    lw = pltpu.make_async_copy(woc, wo_h.at[w["z"], w["q"], :, cols], ls.at[2])
    lw.start()
    gv.after_z(); gv.after_a()
    gq[0].after_z()
    gq[1].start()
    gv.after_b(); gv.finish()
    small = nn(rsel[...], vbuf[...].reshape(512, 128)).astype(bf16)
    dev = lax.broadcasted_iota(jnp.int32, (32, 1), 0)
    def spread(v, e, n):
        lane = lax.broadcasted_iota(jnp.int32, (1, e.shape[1]), 1)
        hit = (lane >= dev * n) & (lane < dev * n + n)
        return colsum(jnp.where(hit, nn(small[v * 32:(v + 1) * 32], e[...]), 0.0))
    for v in range(2): vec[v:v + 1, :] = spread(v, e24, 24)
    gq[0].after_a()
    def normed(src, base):
        def body(r, _):
            sl = pl.ds(pl.multiple_of(r * 256, 256), 256)
            xh, _r = stats(src[sl, :].astype(f32))
            to = pl.ds(pl.multiple_of(base + r * 256, 256), 256)
            xh16[to, :] = xh.astype(bf16)
            afull[to, :] = (xh * vec[0:1, :] + vec[1:2, :]).astype(bf16)
            return 0
        lax.fori_loop(0, rows // 256, body, 0)
    normed(tok, tp * rows)
    gq[0].after_b()
    gq[1].after_z()
    gq[2].start()
    for c in loc: c.wait()
    lw.wait()
    go.start(); g1.start()
    cx.wait_recv()
    normed(xp, (1 - tp) * rows)
    keep[0].start()
    doc_features(len_ref, 2 * rows, fq, fk)
    def proj(p):
        def body(r, _):
            sl = pl.ds(pl.multiple_of(r * 512, 512), 512)
            qkv[sl, p * 3 * 128:(p + 1) * 3 * 128] = nn(afull[sl, :], wown[p].reshape(D, 3 * 128)).astype(bf16)
            return 0
        lax.fori_loop(0, 2 * rows // 512, body, 0)
    proj(0)
    gq[1].after_a(); gq[2].after_z()
    g2.start()
    for v in range(2, 6): vec[v:v + 1, :] = spread(v, e24, 24)
    vec[6:8, :] = jnp.zeros((2, D), f32)
    for v in range(2): mid[v:v + 1, :] = spread(6 + v, e96, 96)
    mid[2:8, :] = jnp.zeros((6, 4 * D), f32)
    nb = 2 * rows // B
    half = lax.broadcasted_iota(jnp.int32, (1, 128), 1) < 64
    causal = lax.broadcasted_iota(jnp.int32, (B, B), 0) <= lax.broadcasted_iota(jnp.int32, (B, B), 1)
    causal = jnp.concatenate([causal, causal], axis=1)
    def unit(u, _):
        p, i = u // nb, u % nb
        def at(k):
            def deco(f): pl.when(u == k)(f)
            return deco
        @at(1)
        def _():
            gq[1].after_b(); gq[2].after_a()
        @at(3)
        def _():
            gq[2].after_b()
            keep[2].start()
        @at(4)
        def _():
            co[0].start()
            go.after_z(); g1.after_z()
            proj(1)
        @at(6)
        def _():
            go.after_a(); g1.after_a(); g2.after_z()
        @at(7)
        def _():
            go.after_b()
        @at(8)
        def _():
            co[1].start()
            proj(2)
            keep[1].start()
            g1.after_b()
        @at(10)
        def _():
            g2.after_a()
        qs = pl.ds(pl.multiple_of(i * B, B), B)
        lanes = lambda k: pl.ds(pl.multiple_of(p * 384 + k * 128, 128), 128)
        q = qkv[qs, lanes(0)] * bf16(0.125)
        fqb = fq[qs, :]
        z = jnp.zeros_like(q)
        q2[...] = jnp.concatenate([
            jnp.concatenate([jnp.where(half, q, z), fqb], axis=1),
            jnp.concatenate([jnp.where(half, z, q), fqb], axis=1)], axis=0)
        def block(j, diag):
            ks = pl.ds(pl.multiple_of(j * B, B), B)
            s = nt(jnp.concatenate([qkv[ks, lanes(1)], fk[ks, :]], axis=1), q2[...])
            if diag: s = jnp.where(causal, s, -BIG)
            mn = jnp.max(s, axis=0, keepdims=True)
            if not diag:
                mo = m_s[...]
                mn = jnp.maximum(mo, mn); al = jnp.exp(mo - mn)
            e = jnp.exp(s - mn)
            su = jnp.sum(e, axis=0, keepdims=True)
            pv = tn(qkv[ks, lanes(2)], e.astype(bf16))
            if diag: l_s[...] = su; acc[...] = pv
            else: l_s[...] = l_s[...] * al + su; acc[...] = acc[...] * al + pv
            m_s[...] = mn
        block(i, True)
        def kstep(j, _):
            block(j, False); return 0
        lax.fori_loop(0, i, kstep, 0)
        l = l_s[...]
        a = acc[...] * (1.0 / l)
        ot = jnp.concatenate([a[:64, :B], a[64:, B:]], axis=0)
        o_loc[qs, pl.ds(pl.multiple_of(p * 128, 128), 128)] = ot.T.astype(bf16)
        lse = m_s[...] + jnp.log(l)
        lse_ref[p, 0:1, qs] = lse[:, :B]
        lse_ref[p, 1:2, qs] = lse[:, B:]
        return 0
    lax.fori_loop(0, pairs * nb, unit, 0)
    co[2].start()
    g2.after_b()
    o_out[:, cols] = o_loc[pl.ds(pl.multiple_of(tp * rows, rows), rows), :]
    got(co)
    go.finish(); g1.finish(); g2.finish()
    for c in send.all: c.wait_send()
    for c in keep: c.wait()

def consts_np(D):
    k = np.arange(128)[:, None]
    e24 = (np.arange(D)[None] % 24 == k).astype(np.float32)
    e96 = (np.arange(4 * D)[None] % 96 == k).astype(np.float32)
    r = np.arange(256)[:, None]
    rsel = (np.arange(512)[None] == (r % 32) * 16 + r // 32).astype(np.float32)
    return e24, e96, rsel

def consts(D):
    return [jnp.asarray(c, bf16) for c in consts_np(D)]

def k12(lengths, tok, wq, wos, vpk, fc1s, fc2s, B=512):
    rows, D = tok.shape
    W = D // 2; pairs = W // 128
    V, A = pl.BlockSpec(memory_space=pltpu.VMEM), pl.BlockSpec(memory_space=pl.ANY)
    sds = jax.ShapeDtypeStruct
    hid = fc1s.shape[0]
    return pl.pallas_call(functools.partial(k12_kernel, B=B, pairs=pairs), name="forward",
        out_shape=(sds((rows, D), bf16), sds((pairs, 2, 2 * rows), f32), sds((8, D), f32), sds((8, 4 * D), f32),
                   sds((2 * rows, D), bf16), sds((2 * rows, 3 * W), bf16), sds((pairs, 4, 4, 48, 3 * 128), bf16),
                   sds((4, 4, 48, D), bf16), sds((4, 4, 2, hid, D), bf16), sds((4, 4, 2, hid, D), bf16)),
        in_specs=[pl.BlockSpec(memory_space=pltpu.SMEM)] + [V] * 7 + [A] * 2,
        out_specs=(V,) * 4 + (A,) * 6,
        scratch_shapes=[pltpu.VMEM((2 * rows, D), bf16), pltpu.VMEM((2 * rows, 3 * W), bf16), pltpu.VMEM((pairs, 4, 4, 48, 3 * 128), bf16), pltpu.VMEM((2 * rows, D), bf16), pltpu.VMEM((rows, D), bf16), pltpu.VMEM((4, 4, 2, 16, 128), bf16), pltpu.VMEM((32, 4 * W), bf16), pltpu.VMEM((32, 4 * W), bf16),
                        pltpu.VMEM((48, W), bf16), pltpu.VMEM((2 * rows, W), bf16), pltpu.VMEM((2 * rows, 128), bf16), pltpu.VMEM((2 * rows, 128), bf16),
                        pltpu.VMEM((2 * B, 256), bf16), pltpu.VMEM((1, 2 * B), f32), pltpu.VMEM((1, 2 * B), f32), pltpu.VMEM((128, 2 * B), f32),
                        pltpu.SemaphoreType.DMA((N_COPIES,)), pltpu.SemaphoreType.DMA((N_COPIES,)), pltpu.SemaphoreType.DMA((6,))],
        compiler_params=pltpu.CompilerParams(vmem_limit_bytes=60 << 20, collective_id=0, has_side_effects=True))(
            lengths, tok, wq, wos, vpk, *consts(D), fc1s, fc2s)

def pack_vectors(six, two):
    n6 = jnp.pad(jnp.stack(six), ((0, 0), (0, 128 - six[0].shape[0])))
    n2 = jnp.pad(jnp.stack(two), ((0, 8), (0, 128 - two[0].shape[0])))
    return jnp.concatenate([n6, n2], axis=0)


def add(x, y):
    return (x.astype(f32) + y.astype(f32)).astype(x.dtype)

class Scatter:
    def __init__(self, copy, w, s, bb, ab, zb):
        self.w, self.s, self.bb, self.ab, self.zb = w, s, bb, ab, zb
        self.b = [copy(s.at[:, w["qb"]], bb.at[0], w["b"]), copy(s.at[:, w["qab"]], bb.at[1], w["b"])]
        self.a = [copy(s.at[:, w["qa"]], ab, w["a"])]
        self.z = [copy(s.at[w["zi"][k], w["q"]], zb.at[k], w["zs"][k]) for k in range(3)]
    def go(self, cs):
        for c in cs: c.start()
    def start(self):
        self.go(self.b)
    def after_b(self):
        for c in self.b: c.wait_recv()
        for z in range(4):
            self.s[z, self.w["qa"]] = add(self.s[z, self.w["qa"]], self.bb[1, z])
        self.go(self.a)
        for z in range(4):
            self.s[z, self.w["q"]] = add(self.s[z, self.w["q"]], self.bb[0, z])
    def after_a(self):
        for c in self.a: c.wait_recv()
        for z in range(4):
            self.s[z, self.w["q"]] = add(self.s[z, self.w["q"]], self.ab[z])
        self.go(self.z)
    def result(self):
        for c in self.z: c.wait_recv()
        r = self.s[self.w["z"], self.w["q"]].astype(f32)
        for k in range(3): r = r + self.zb[k].astype(f32)
        return r

def k45_kernel(len_ref, do, delta, lse_ref, vec, gvec, gmid, e24t, e96t, qkv_h, xh_h, wown_h, gwo_h, tok_h, dy_h, g1_h, g2_h,
               gtok, gq_o, gwo_o, g1_o, g2_o, small_o, pre_o,
               qkv, xh16, wown, gwo, tok, dy, do_own, dl_own, fq, fk, q2, do2, dq, dk, dv,
               s1, r1, b1, a1, z1, s2, r2, b2, a2, z2, so, ro, bo, ao, zo, *rest, B, pairs):
    flows, rest = rest[:4 * pairs], rest[4 * pairs:]
    (sm, pm, s4, bm, am, zm, da, dsend, drecv, fo, xo, fqk, xq, gcol, bcol, vacc, uacc, ss, rs, ls) = rest
    w = place()
    tp = w["tp"]
    rows, D = tok.shape
    W = pairs * 128
    nb = 2 * rows // B
    first = tp == 0
    other = 1 - tp
    mine_rows = pl.ds(pl.multiple_of(tp * rows, rows), rows)
    mine_cols = pl.ds(pl.multiple_of(tp * W, 128), W)
    other_cols = pl.ds(pl.multiple_of(other * W, 128), W)
    copy = Copy(ss, rs)
    c_do = copy(do.at[:, other_cols], do_own.at[mine_rows, :], w["peer"])
    c_dl = copy(delta.at[pl.ds(pl.multiple_of(other * 8, 8), 8), :], dl_own.at[:, mine_rows], w["peer"])
    c_r2 = copy(g2_h.at[:, :, other], r2, w["peer"])
    c_r1 = copy(g1_h.at[:, :, other], r1, w["peer"])
    c_ro = copy(gwo_h.at[:, other_cols], ro, w["peer"])
    f1, f2 = Scatter(copy, w, s1, b1, a1, z1), Scatter(copy, w, s2, b2, a2, z2)
    fo_ = Scatter(copy, w, so, bo, ao, zo)
    fqs = [Scatter(copy, w, *flows[4 * p:4 * p + 4]) for p in range(pairs)]
    fm = Scatter(copy, w, s4, bm, am, zm)
    c_pm = copy(sm.at[:, :, other], pm, w["peer"])
    hr = rows // 2
    c_da = [copy(dsend.at[pl.ds(k * hr, hr), :], drecv.at[pl.ds(k * hr, hr), :], w["peer"]) for k in range(2)]
    n = gq_o.shape[0]
    other_n = pl.ds(pl.multiple_of(other * n, 8), n)
    mine_n = pl.ds(pl.multiple_of(tp * n, 8), n)
    c_xo = copy(fo.at[other_n, :], xo, w["peer"])
    c_xq = copy(fqk.at[other_n, :], xq, w["peer"])
    l_q = pltpu.make_async_copy(qkv_h, qkv, ls.at[0])
    l_2 = pltpu.make_async_copy(g2_h.at[:, :, tp], s2, ls.at[1])
    l_1 = pltpu.make_async_copy(g1_h.at[:, :, tp], s1, ls.at[2])
    l_t = pltpu.make_async_copy(tok_h, tok, ls.at[3])
    l_y = pltpu.make_async_copy(dy_h, dy, ls.at[4])
    l_o = pltpu.make_async_copy(gwo_h, gwo, ls.at[5])
    l_x = pltpu.make_async_copy(xh_h, xh16, ls.at[6])
    l_w = [pltpu.make_async_copy(wown_h.at[p], wown.at[:, p * 384:(p + 1) * 384], ls.at[7 + p]) for p in range(pairs)]
    for l in [l_q, l_2, l_o, l_1, l_x] + l_w + [l_t, l_y]: l.start()
    enter(w)
    for c in (c_do, c_dl, c_ro, c_r2, c_r1): c.start()
    do_own[mine_rows, :] = do[:, mine_cols]
    dl_own[:, mine_rows] = delta[pl.ds(pl.multiple_of(tp * 8, 8), 8), :]
    doc_features(len_ref, 2 * rows, fq, fk)
    dev = lax.broadcasted_iota(jnp.int32, (32, 1, 1), 0)
    def pieces(v, e, n):
        lane = lax.broadcasted_iota(jnp.int32, (1, 1, v.shape[1]), 2)
        hit = (lane >= dev * n) & (lane < dev * n + n)
        t = jnp.where(hit, v[None], 0.0).reshape(256, v.shape[1])
        hi = t.astype(bf16)
        return nn(hi, e) + nn((t - hi.astype(f32)).astype(bf16), e)
    early = pieces(gmid[...], e96t[...], 4 * D // 32) + pieces(gvec[...], e24t[...], D // 32)
    sm[...] = early.reshape(4, 4, 2, 8, 128)
    c_pm.start()
    gcol[...] = jnp.broadcast_to(vec[0:1, :], (128, D)).T
    bcol[...] = jnp.broadcast_to(vec[1:2, :], (128, D)).T
    vacc[...] = jnp.zeros_like(vacc); uacc[...] = jnp.zeros_like(uacc)
    l_q.wait()
    c_do.wait_recv(); c_dl.wait_recv()

    half = lax.broadcasted_iota(jnp.int32, (1, 128), 1) < 64
    causal = lax.broadcasted_iota(jnp.int32, (B, B), 0) <= lax.broadcasted_iota(jnp.int32, (B, B), 1)
    causal = jnp.concatenate([causal, causal], axis=1)
    def grads(p):
        out = flows[4 * p]
        cs = [slice(p * 384 + k * 128, p * 384 + (k + 1) * 128) for k in range(3)]
        g = qkv[:, p * 384:(p + 1) * 384]
        t = tn(xh16[...], g)
        gsum = jnp.sum(g.astype(f32), axis=0, keepdims=True)
        for k in range(3):
            sl = slice(k * 128, (k + 1) * 128)
            wk = wown[:, cs[k]].astype(f32)
            tk, sk = t[:, sl], gsum[:, sl]
            out[:, :, :, sl] = (gcol[...] * tk + bcol[...] * sk).astype(bf16).reshape(4, 4, 48, 128)
            vacc[...] += tk * wk
            uacc[...] += sk * wk
        if p == pairs - 1:
            lane = lax.broadcasted_iota(jnp.int32, (1, 128), 1)
            e = jnp.where(lane == 0, jnp.sum(vacc[...], axis=1, keepdims=True), 0.0)
            e = jnp.where(lane == 1, jnp.sum(uacc[...], axis=1, keepdims=True), e)
            out[:, :, :, 384:512] = e.astype(bf16).reshape(4, 4, 48, 128)
    def unit(u, _):
        p, j = u // nb, u % nb
        lanes = lambda k: pl.ds(pl.multiple_of(p * 384 + k * 128, 128), 128)
        def at(k):
            def deco(f): pl.when(u == k)(f)
            return deco
        @at(1)
        def _():
            c_pm.wait_recv()
            for z in range(4):
                for k in range(4): s4[z, k] = sm[z, k, tp] + pm[z, k]
            fm.start()
            c_r2.wait_recv(); l_2.wait()
            for z in range(4):
                for k in range(4): s2[z, k] = add(s2[z, k], r2[z, k])
            f2.start()
            c_ro.wait_recv(); l_o.wait()
            so[...] = add(gwo[:, mine_cols], ro[...]).reshape(so.shape)
            fo_.start()
        @at(2)
        def _():
            fm.after_b()
            c_r1.wait_recv(); l_1.wait()
            for z in range(4):
                for k in range(4): s1[z, k] = add(s1[z, k], r1[z, k])
            f1.start()
        @at(3)
        def _():
            fm.after_a()
        @at(4)
        def _():
            l_x.wait()
            for l in l_w: l.wait()
            grads(0)
            f2.after_b(); fo_.after_b(); fqs[0].start()
            small_o[...] = fm.result()
        @at(5)
        def _():
            f2.after_a(); fo_.after_a()
        @at(6)
        def _():
            f1.after_b(); fqs[0].after_b()
        @at(7)
        def _():
            fqs[0].after_a()
        @at(8)
        def _():
            f1.after_a(); grads(1); fqs[1].start()
            g2_o[...] = f2.result()
            fo[...] = fo_.result()
            c_xo.start()
        @at(9)
        def _():
            fqs[1].after_b()
        @at(10)
        def _():
            fqs[1].after_a()
        @pl.when(j == 0)
        def _():
            def prep(i, _):
                qs = pl.ds(pl.multiple_of(i * B, B), B)
                q = qkv[qs, lanes(0)] * bf16(0.125)
                d = do_own[qs, pl.ds(pl.multiple_of(p * 128, 128), 128)]
                fqb = fq[qs, :]
                z = jnp.zeros_like(q)
                q2[i] = jnp.concatenate([
                    jnp.concatenate([jnp.where(half, q, z), fqb], axis=1),
                    jnp.concatenate([jnp.where(half, z, q), fqb], axis=1)], axis=0)
                do2[i] = jnp.concatenate([jnp.where(half, d, z), jnp.where(half, z, d)], axis=0)
                dq[i] = jnp.zeros(dq.shape[1:], f32)
                return 0
            lax.fori_loop(0, nb, prep, 0)
        ks = pl.ds(pl.multiple_of(j * B, B), B)
        kt = qkv[ks, lanes(1)]
        v = qkv[ks, lanes(2)]
        k2 = jnp.concatenate([kt, fk[ks, :]], axis=1)
        def block(i, diag):
            qs = pl.ds(pl.multiple_of(i * B, B), B)
            lse = jnp.concatenate([lse_ref[p, 0:1, qs], lse_ref[p, 1:2, qs]], axis=1)
            d0 = pl.ds(2 * p, 1); d1 = pl.ds(2 * p + 1, 1)
            dl = jnp.concatenate([dl_own[d0, qs], dl_own[d1, qs]], axis=1)
            qq = q2[i]; dd = do2[i]
            pt = jnp.exp(nt(k2, qq) - lse)
            if diag: pt = jnp.where(causal, pt, 0.0)
            ds = (pt * (nt(v, dd) - dl)).astype(bf16)
            dvp = nn(pt.astype(bf16), dd)
            dkp = nn(ds, qq[:, :128])
            if diag: dv[...] = dvp; dk[...] = dkp
            else: dv[...] += dvp; dk[...] += dkp
            dq[i] += tn(ds, kt)
        block(j, True)
        def qstep(i, _):
            block(i, False); return 0
        lax.fori_loop(j + 1, nb, qstep, 0)
        qkv[ks, lanes(1)] = dk[...].astype(bf16)
        qkv[ks, lanes(2)] = dv[...].astype(bf16)
        @pl.when(j == nb - 1)
        def _():
            def fin(i, _):
                qs = pl.ds(pl.multiple_of(i * B, B), B)
                d = dq[i]
                qkv[qs, lanes(0)] = (jnp.where(half, d[:B], d[B:]) * 0.125).astype(bf16)
                return 0
            lax.fori_loop(0, nb, fin, 0)
        return 0
    lax.fori_loop(0, pairs * nb, unit, 0)
    grads(2)
    fqs[2].start()
    for k in range(2):
        sl = pl.ds(pl.multiple_of(other * rows + k * hr, hr), hr)
        dsend[k * hr:(k + 1) * hr, :] = nt(qkv[sl, :], wown[...]).astype(bf16)
        c_da[k].start()
    fqs[2].after_b()
    g1_o[...] = f1.result()
    for k in range(2):
        sl = pl.ds(pl.multiple_of(tp * rows + k * hr, hr), hr)
        da[k * hr:(k + 1) * hr, :] = nt(qkv[sl, :], wown[...])
        if k == 0: fqs[2].after_a()
    l_t.wait(); l_y.wait()
    for c in c_da: c.wait_recv()
    gain = vec[0:1, :]
    def fin(r, _):
        sl = pl.ds(pl.multiple_of(r * 256, 256), 256)
        d = da[sl, :] + drecv[sl, :].astype(f32)
        xh, xr = stats(tok[sl, :].astype(f32))
        gtok[sl, :] = (dy[sl, :].astype(f32) + ln_back(d, xh, xr, gain)).astype(bf16)
        return 0
    def collect(p):
        r = fqs[p].result()
        fqk[:, p * 384:(p + 1) * 384] = r[:, :384]
        if p == pairs - 1: fqk[:, pairs * 384:] = r[:, 384:]
    for p in range(pairs - 1): collect(p)
    lax.fori_loop(0, rows // 256, fin, 0)
    collect(pairs - 1)
    c_xq.start()
    c_xo.wait_recv()
    mine = fo[mine_n, :]
    gwo_o[:, :W] = jnp.where(first, mine, xo[...])
    gwo_o[:, W:] = jnp.where(first, xo[...], mine)
    c_xq.wait_recv()
    for p in range(pairs):
        for k in range(3):
            src = p * 384 + k * 128
            mine = fqk[mine_n, src:src + 128]
            oth = xq[:, src:src + 128]
            c0 = k * D + p * 128
            gq_o[:, c0:c0 + 128] = jnp.where(first, mine, oth)
            gq_o[:, c0 + W:c0 + W + 128] = jnp.where(first, oth, mine)
    pre_o[...] = fqk[mine_n, 3 * W:] + xq[:, 3 * W:]
    for c in copy.all: c.wait_send()

def k45(lengths, xh, wown, do, delta, lse, vec, gvec, gmid, gwo, qkv, tok, dy, g1, g2, B=512):
    rows, D = tok.shape
    W = D // 2; pairs = W // 128; nb = 2 * rows // B
    V, A = pl.BlockSpec(memory_space=pltpu.VMEM), pl.BlockSpec(memory_space=pl.ANY)
    sds = jax.ShapeDtypeStruct
    hid = g1.shape[3]
    M = pltpu.VMEM
    e24t, e96t = [c.T for c in consts_np(D)[:2]]
    def flow(r, c, t, lead=()):
        return [M(lead + (4, 4, r, c), t), M(lead + (2, 4, r, c), t), M(lead + (4, r, c), t), M(lead + (3, r, c), t)]
    fc = flow(hid, D, bf16)
    fc = [fc[0], M((4, 4, hid, D), bf16)] + fc[1:]
    wo = flow(48, W, bf16)
    wo = [wo[0], M((D, W), bf16)] + wo[1:]
    sm = flow(8, 128, f32)
    return pl.pallas_call(functools.partial(k45_kernel, B=B, pairs=pairs), name="backward",
        out_shape=(sds((rows, D), bf16), sds((D // 32, 3 * D), f32), sds((D // 32, D), f32), sds((hid, D), f32), sds((hid, D), f32), sds((8, 128), f32), sds((D // 32, 128), f32)),
        in_specs=[pl.BlockSpec(memory_space=pltpu.SMEM)] + [V] * 8 + [A] * 8,
        out_specs=(V,) * 7,
        scratch_shapes=[M((2 * rows, 3 * W), bf16), M((2 * rows, D), bf16), M((D, 3 * W), bf16), M((D, D), bf16), M((rows, D), bf16), M((rows, D), dy.dtype), M((2 * rows, W), bf16), M((8, 2 * rows), f32),
                        M((2 * rows, 128), bf16), M((2 * rows, 128), bf16), M((nb, 2 * B, 256), bf16), M((nb, 2 * B, 128), bf16), M((nb, 2 * B, 128), f32),
                        M((B, 128), f32), M((B, 128), f32)] + fc + fc + wo + flow(48, W, bf16) * (pairs - 1) + flow(48, W + 128, bf16) +
                       [M((4, 4, 2, 8, 128), f32), M((4, 4, 8, 128), f32)] + sm +
                       [M((rows, D), f32), M((rows, D), bf16), M((rows, D), bf16), M((48, W), f32), M((24, W), f32), M((48, 3 * W + 128), f32), M((24, 3 * W + 128), f32),
                        M((D, 128), f32), M((D, 128), f32), M((D, 128), f32), M((D, 128), f32),
                        pltpu.SemaphoreType.DMA((64,)), pltpu.SemaphoreType.DMA((64,)), pltpu.SemaphoreType.DMA((10,))],
        compiler_params=pltpu.CompilerParams(vmem_limit_bytes=63 << 20, collective_id=1, has_side_effects=True))(
            lengths, do, delta, lse, vec, gvec, gmid, jnp.asarray(e24t, bf16), jnp.asarray(e96t, bf16), qkv, xh, wown, gwo, tok, dy, g1, g2)

def local_fast(tokens, cotangent, lengths, qkv_weight, out_weight, pre_gain, pre_shift, sub_gain, sub_shift,
          ffn_gain, ffn_shift, fc1_weight, mid_gain, mid_shift, fc2_weight):
    rows, D = tokens.shape
    vpk = pack_vectors([pre_gain, pre_shift, sub_gain, sub_shift, ffn_gain, ffn_shift], [mid_gain, mid_shift])
    o, lse, vec, mid, xh16, qkv, wown, wo, fc1, fc2 = k12(lengths, tokens, qkv_weight, out_weight, vpk, fc1_weight, fc2_weight)
    block_out, dy, do, delta, gwo, g1, g2, gvec, gmid = ffn(o, tokens, cotangent, wo.reshape(D, D), fc1.reshape(4 * D, D), fc2.reshape(4 * D, D), vec, mid)
    shape = (4, 4, 2, fc1_weight.shape[0], D)
    gtok, gq, gwo, g1, g2, small, pre = k45(lengths, xh16, wown.reshape(3, D, 384), do, delta, lse, vec, gvec, gmid, gwo, qkv, tokens, dy, g1.reshape(shape), g2.reshape(shape))
    n, m = pre_gain.shape[0], mid_gain.shape[0]
    return (block_out, gtok, gq, gwo, pre[:, 0], pre[:, 1], small[2, :n], small[3, :n], small[4, :n], small[5, :n],
            g1, small[6, :m], small[7, :m], g2)

def norm(v):
    return stats(v)


def local_any(tokens, cotangent, lengths, qkv_weight, out_weight, pre_gain, pre_shift, sub_gain, sub_shift,
          ffn_gain, ffn_shift, fc1_weight, mid_gain, mid_shift, fc2_weight):
    rows, D = tokens.shape
    W = D // 2
    tp = lax.axis_index("tp")
    both = ("dp", "tp")
    gather = lambda a: lax.all_gather(a, both, axis=0, tiled=True)
    small = gather(jnp.stack([pre_gain, pre_shift, sub_gain, sub_shift, ffn_gain, ffn_shift], axis=1)).astype(f32).T
    mid = gather(jnp.stack([mid_gain, mid_shift], axis=1)).astype(f32).T
    wq = gather(qkv_weight)
    wo, fc1, fc2 = gather(out_weight), gather(fc1_weight), gather(fc2_weight)
    wown = lax.dynamic_index_in_dim(wq.reshape(D, 3, 2, W), tp, 2, keepdims=False).reshape(D, 3 * W)
    x = tokens.astype(f32)
    xh, xr = norm(x)
    a = (xh * small[0] + small[1]).astype(bf16)
    afull = lax.all_gather(a, "tp", axis=0, tiled=True)
    qkv = nn(afull, wown).astype(bf16)
    o_own, lse = attn_fwd(lengths, qkv, B=512)
    o = lax.all_to_all(o_own, "tp", 0, 1, tiled=True)
    vec = jnp.concatenate([small, jnp.zeros((2, D), f32)], axis=0)
    block_out, dy, do, delta, gwo, gfc1, gfc2, gvec, gmid = ffn(
        o, tokens, cotangent, wo, fc1, fc2, vec, jnp.concatenate([mid, jnp.zeros((6, 4 * D), f32)], axis=0))
    do_own = lax.all_to_all(do, "tp", 1, 0, tiled=True)
    dl_own = lax.all_to_all(delta, "tp", 0, 1, tiled=True)
    dqkv = attn_bwd(lengths, qkv, do_own, lse, dl_own, B=512)
    gq = tn(afull, dqkv)
    da = lax.psum_scatter(nt(dqkv, wown), "tp", scatter_dimension=0, tiled=True)
    grad_tokens = (dy.astype(f32) + ln_back(da, xh, xr, small[0])).astype(bf16)
    scatter = lambda v: lax.psum_scatter(v, both, scatter_dimension=0, tiled=True)
    gq = lax.psum_scatter(gq, "dp", scatter_dimension=0, tiled=True)
    n = gq.shape[0] // 2
    gq = lax.all_to_all(gq.reshape(2, n, 3, 1, W), "tp", 0, 3, tiled=True).reshape(n, 3 * D)
    small_grads = scatter(jnp.concatenate([jnp.stack([colsum(da * xh)[0], colsum(da)[0]]), gvec[2:6]], axis=0).T).T
    mid_grads = scatter(gmid[6:8].T).T
    gwo = scatter(gwo.astype(f32))
    gfc1 = scatter(gfc1.reshape(-1, D).astype(f32))
    gfc2 = scatter(gfc2.reshape(-1, D).astype(f32))
    return (block_out, grad_tokens, gq, gwo, small_grads[0], small_grads[1], small_grads[2], small_grads[3],
            small_grads[4], small_grads[5], gfc1, mid_grads[0], mid_grads[1], gfc2)


def local(*arrays):
    fits = lax.axis_size("dp") == 16 and lax.axis_size("tp") == 2
    return (local_fast if fits else local_any)(*arrays)


def solution(mesh):
    two, one = P(("dp", "tp"), None), P(("dp", "tp"))
    return jax.shard_map(
        local,
        mesh=mesh,
        in_specs=(two, two, P("dp", None), two, two, one, one, one, one, one, one, two, one, one, two),
        out_specs=(two, two, two, two, one, one, one, one, one, one, two, one, one, two),
        check_vma=False,
    )
```

```python
import functools

import jax
import jax.numpy as jnp
import numpy as np
from jax import lax
from jax.experimental import pallas as pl
from jax.experimental.pallas import tpu as pltpu
from jax.sharding import PartitionSpec as P

f32, bf16 = jnp.float32, jnp.bfloat16
EPS = 1e-5
BIG = 1e30


def nt(a, b):
    return lax.dot_general(a, b, (((1,), (1,)), ((), ())), preferred_element_type=f32)


def nn(a, b):
    return lax.dot_general(a, b, (((1,), (0,)), ((), ())), preferred_element_type=f32)


def tn(a, b):
    return lax.dot_general(a, b, (((0,), (0,)), ((), ())), preferred_element_type=f32)

def doc_features(len_ref, rows, fq, fk):
    lane = lax.broadcasted_iota(jnp.int32, (1, 128), 1)
    lo = jnp.zeros((1, 128), jnp.int32); hi = jnp.zeros((1, 128), jnp.int32)
    run = jnp.int32(0)
    for d in range(8):
        nxt = run + len_ref[0, d]
        lo = jnp.where(lane == d, run, lo); hi = jnp.where(lane == d, nxt, hi)
        run = nxt
    def body(r, _):
        place = lax.broadcasted_iota(jnp.int32, (256, 128), 0) + r * 256
        hit = (place >= lo) & (place < hi)
        sl = pl.ds(pl.multiple_of(r * 256, 256), 256)
        fq[sl, :] = jnp.where(hit, 1.0, 0.0).astype(bf16)
        fk[sl, :] = jnp.where(hit | (lane >= 8), 0.0, -BIG).astype(bf16)
        return 0
    lax.fori_loop(0, rows // 256, body, 0)

def fwd_t(len_ref, qkv, o_ref, lse_ref, fq, fk, q2, st_s, m_s, l_s, acc, *, B, pairs, variant):
    rows = qkv.shape[0]; nb = rows // B; W = pairs * 128
    doc_features(len_ref, rows, fq, fk)
    half = lax.broadcasted_iota(jnp.int32, (1, 128), 1) < 64
    causal = lax.broadcasted_iota(jnp.int32, (B, B), 0) <= lax.broadcasted_iota(jnp.int32, (B, B), 1)
    causal = jnp.concatenate([causal, causal], axis=1)
    for p in range(pairs):
        def qstep(i, _, p=p):
            qs = pl.ds(pl.multiple_of(i * B, B), B)
            q = qkv[qs, p * 128:(p + 1) * 128] * bf16(0.125)
            fqb = fq[qs, :]
            z = jnp.zeros_like(q)
            q2[...] = jnp.concatenate([
                jnp.concatenate([jnp.where(half, q, z), fqb], axis=1),
                jnp.concatenate([jnp.where(half, z, q), fqb], axis=1)], axis=0)
            def score(j):
                ks = pl.ds(pl.multiple_of(j * B, B), B)
                k2 = jnp.concatenate([qkv[ks, W + p * 128:W + (p + 1) * 128], fk[ks, :]], axis=1)
                return nt(k2, q2[...])
            def vblk(j):
                ks = pl.ds(pl.multiple_of(j * B, B), B)
                return qkv[ks, 2 * W + p * 128:2 * W + (p + 1) * 128]
            if variant == "online":
                def block(j, masked, first):
                    s = score(j)
                    if masked: s = jnp.where(causal, s, -BIG)
                    mx = jnp.max(s, axis=0, keepdims=True)
                    if first: mn = mx
                    else:
                        mo = m_s[...]
                        mn = jnp.maximum(mo, mx); al = jnp.exp(mo - mn)
                    e = jnp.exp(s - mn)
                    su = jnp.sum(e, axis=0, keepdims=True)
                    pv = tn(vblk(j), e.astype(bf16))
                    if first: l_s[...] = su; acc[...] = pv
                    else: l_s[...] = l_s[...] * al + su; acc[...] = acc[...] * al + pv
                    m_s[...] = mn
                block(i, True, True)
                def kstep(j, _):
                    block(j, False, False); return 0
                lax.fori_loop(0, i, kstep, 0)
                m = m_s[...]; l = l_s[...]
            else:
                def part(s): return jnp.max(s.reshape(B // 8, 8, 2 * B), axis=0)
                s = jnp.where(causal, score(i), -BIG)
                st_s[i] = s
                def pass1(j, m8):
                    s = score(j); st_s[j] = s
                    return jnp.maximum(m8, part(s))
                m8 = lax.fori_loop(0, i, pass1, part(s))
                m = jnp.max(m8, axis=0, keepdims=True)
                acc[...] = jnp.zeros_like(acc)
                def pass2(j, l8):
                    e = jnp.exp(st_s[j] - m)
                    acc[...] += tn(vblk(j), e.astype(bf16))
                    return l8 + jnp.sum(e.reshape(B // 8, 8, 2 * B), axis=0)
                l8 = lax.fori_loop(0, i + 1, pass2, jnp.zeros((8, 2 * B), f32))
                l = jnp.sum(l8, axis=0, keepdims=True)
            r = 1.0 / l
            a = acc[...] * r
            ot = jnp.concatenate([a[:64, :B], a[64:, B:]], axis=0)
            o_ref[qs, p * 128:(p + 1) * 128] = ot.T.astype(o_ref.dtype)
            lse = m + jnp.log(l)
            lse_ref[2 * p:2 * p + 1, qs] = lse[:, :B]
            lse_ref[2 * p + 1:2 * p + 2, qs] = lse[:, B:]
            return 0
        lax.fori_loop(0, nb, qstep, 0)

def attn_fwd(lengths, qkv, B=256, variant="online"):
    rows, w3 = qkv.shape; W = w3 // 3; pairs = W // 128; nb = rows // B
    return pl.pallas_call(functools.partial(fwd_t, B=B, pairs=pairs, variant=variant), name="attn_fwd",
        out_shape=(jax.ShapeDtypeStruct((rows, W), bf16), jax.ShapeDtypeStruct((8, rows), f32)),
        in_specs=[pl.BlockSpec(memory_space=pltpu.SMEM), pl.BlockSpec(memory_space=pltpu.VMEM)],
        out_specs=(pl.BlockSpec(memory_space=pltpu.VMEM),) * 2,
        scratch_shapes=[pltpu.VMEM((rows, 128), bf16), pltpu.VMEM((rows, 128), bf16), pltpu.VMEM((2 * B, 256), bf16),
                        pltpu.VMEM((nb if variant != "online" else 1, B, 2 * B), f32),
                        pltpu.VMEM((1, 2 * B), f32), pltpu.VMEM((1, 2 * B), f32), pltpu.VMEM((128, 2 * B), f32)],
        compiler_params=pltpu.CompilerParams(vmem_limit_bytes=56 << 20))(lengths, qkv)

def bwd_kernel(len_ref, qkv, do_ref, lse_ref, dl_ref, out, fq, fk, q2, do2, dq, dk, dv, *, B, pairs, mode):
    rows = qkv.shape[0]; nb = rows // B; W = pairs * 128
    doc_features(len_ref, rows, fq, fk)
    half = lax.broadcasted_iota(jnp.int32, (1, 128), 1) < 64
    causal = lax.broadcasted_iota(jnp.int32, (B, B), 0) <= lax.broadcasted_iota(jnp.int32, (B, B), 1)
    causal = jnp.concatenate([causal, causal], axis=1)
    for p in range(pairs):
        def prep(i, _, p=p):
            qs = pl.ds(pl.multiple_of(i * B, B), B)
            q = qkv[qs, p * 128:(p + 1) * 128] * bf16(0.125)
            d = do_ref[qs, p * 128:(p + 1) * 128]
            fqb = fq[qs, :]
            z = jnp.zeros_like(q)
            q2[i] = jnp.concatenate([
                jnp.concatenate([jnp.where(half, q, z), fqb], axis=1),
                jnp.concatenate([jnp.where(half, z, q), fqb], axis=1)], axis=0)
            do2[i] = jnp.concatenate([jnp.where(half, d, z), jnp.where(half, z, d)], axis=0)
            dq[i] = jnp.zeros(dq.shape[1:], f32)
            return 0
        lax.fori_loop(0, nb, prep, 0)
        def kstep(j, _, p=p):
            ks = pl.ds(pl.multiple_of(j * B, B), B)
            kt = qkv[ks, W + p * 128:W + (p + 1) * 128]
            v = qkv[ks, 2 * W + p * 128:2 * W + (p + 1) * 128]
            k2 = jnp.concatenate([kt, fk[ks, :]], axis=1)
            def block(i, masked, first):
                qs = pl.ds(pl.multiple_of(i * B, B), B)
                lse = jnp.concatenate([lse_ref[2 * p:2 * p + 1, qs], lse_ref[2 * p + 1:2 * p + 2, qs]], axis=1)
                dl = jnp.concatenate([dl_ref[2 * p:2 * p + 1, qs], dl_ref[2 * p + 1:2 * p + 2, qs]], axis=1)
                qq = q2[i]; dd = do2[i]
                st = nt(k2, qq)
                pt = jnp.exp(st - lse)
                if masked: pt = jnp.where(causal, pt, 0.0)
                dp = nt(v, dd)
                ds = (pt * (dp - dl)).astype(bf16)
                dvp = nn(pt.astype(bf16), dd)
                dkp = nn(ds, qq[:, :128])
                if first: dv[...] = dvp; dk[...] = dkp
                else: dv[...] += dvp; dk[...] += dkp
                if mode == "tn":
                    dq[i] += tn(ds, kt)
                else:
                    dq[i] += tn(kt, ds)
            block(j, True, True)
            def qstep(i, _):
                block(i, False, False); return 0
            lax.fori_loop(j + 1, nb, qstep, 0)
            out[ks, W + p * 128:W + (p + 1) * 128] = dk[...].astype(bf16)
            out[ks, 2 * W + p * 128:2 * W + (p + 1) * 128] = dv[...].astype(bf16)
            return 0
        lax.fori_loop(0, nb, kstep, 0)
        def fin(i, _, p=p):
            qs = pl.ds(pl.multiple_of(i * B, B), B)
            if mode == "tn":
                d = dq[i]
                r = jnp.where(half, d[:B], d[B:])
            else:
                d = dq[i]
                r = jnp.concatenate([d[:64, :B], d[64:, B:]], axis=0).T
            out[qs, p * 128:(p + 1) * 128] = (r * 0.125).astype(bf16)
            return 0
        lax.fori_loop(0, nb, fin, 0)

def attn_bwd(lengths, qkv, do, lse, dl, B=256, mode="tn"):
    rows, w3 = qkv.shape; W = w3 // 3; pairs = W // 128; nb = rows // B
    dqs = (nb, 2 * B, 128) if mode == "tn" else (nb, 128, 2 * B)
    return pl.pallas_call(functools.partial(bwd_kernel, B=B, pairs=pairs, mode=mode), name="attn_bwd",
        out_shape=jax.ShapeDtypeStruct((rows, w3), bf16),
        in_specs=[pl.BlockSpec(memory_space=pltpu.SMEM)] + [pl.BlockSpec(memory_space=pltpu.VMEM)] * 4,
        out_specs=pl.BlockSpec(memory_space=pltpu.VMEM),
        scratch_shapes=[pltpu.VMEM((rows, 128), bf16), pltpu.VMEM((rows, 128), bf16), pltpu.VMEM((nb, 2 * B, 256), bf16),
                        pltpu.VMEM((nb, 2 * B, 128), bf16), pltpu.VMEM(dqs, f32), pltpu.VMEM((B, 128), f32), pltpu.VMEM((B, 128), f32)],
        compiler_params=pltpu.CompilerParams(vmem_limit_bytes=56 << 20))(lengths, qkv, do, lse, dl)

def stats(v):
    n = v.shape[-1]
    m = jnp.sum(v, axis=-1, keepdims=True) * (1.0 / n)
    c = v - m
    s = jnp.sum(c * c, axis=-1, keepdims=True) * (1.0 / n)
    r = lax.rsqrt(s + EPS)
    return c * r, r
def ln_back(w, vh, r, g):
    n = vh.shape[-1]
    wg = w * g
    a = jnp.sum(wg, axis=-1, keepdims=True) * (1.0 / n)
    b = jnp.sum(wg * vh, axis=-1, keepdims=True) * (1.0 / n)
    return r * (wg - a - vh * b)
def colsum(v): return jnp.sum(v, axis=0, keepdims=True)


def gelu_parts(h):
    return 0.5 + 0.5 * lax.erf(h * 0.7071067811865476), jnp.exp2(h * h * -0.7213475204444817) * 0.3989422804014327

def ffn_kernel(vec, mid, sel, o_h, x_h, g_h, wo_h, fc1_h, fc2_h,
               delta_ref, gvec, gmid, gfc1, gfc2, out_ref, dy_h, do_h, gwo_h,
               o_ref, x_ref, g_ref, wo, fc1, fc2, dy_ref, do_ref, gwo,
               h_s, u_s, d_s, dm_s, m_s, dh_s, c_s, b_s, y_s, dc_s, st_s, ws, *, T, NT, NC, SR, UT):
    step = pl.program_id(0)
    rows = x_ref.shape[0]
    ff, D = fc1.shape
    K = ff // NC
    NS = NT // UT
    ins = [pltpu.make_async_copy(h, v, ws.at[k]) for k, (h, v) in enumerate(
        ((o_h, o_ref), (wo_h, wo), (x_h, x_ref), (fc1_h, fc1), (g_h, g_ref), (fc2_h, fc2)))]
    outs = [pltpu.make_async_copy(v, h, ws.at[6 + k]) for k, (h, v) in enumerate(
        ((dy_h, dy_ref), (do_h, do_ref), (gwo_h, gwo)))]
    sg, sb, fg, fb = [vec[k:k + 1, :] for k in range(2, 6)]
    tiles = [slice(t * T, (t + 1) * T) for t in range(NT)]
    subs = [slice(r * SR, (r + 1) * SR) for r in range(T // SR)]
    cols = [slice(c * K, (c + 1) * K) for c in range(NC)]
    def fold(v):
        r = v[:, :128]
        for k in range(1, v.shape[1] // 128): r = r + v[:, k * 128:(k + 1) * 128]
        return r
    @pl.when(step == 0)
    def _():
        for l in ins: l.start()
        gvec[...] = jnp.zeros_like(gvec); gmid[...] = jnp.zeros_like(gmid)
        ins[0].wait(); ins[1].wait(); ins[2].wait()
        bs = []
        for sl in tiles:
            oh, _r = stats(o_ref[sl, :].astype(f32))
            b_s[sl, :] = (oh * sg + sb).astype(bf16)
        for sl in tiles:
            y_s[sl, :] = x_ref[sl, :].astype(f32) + nn(b_s[sl, :], wo[...])
        for sl in tiles:
            yh, _r = stats(y_s[sl, :])
            c_s[sl, :] = (yh * fg + fb).astype(bf16)
        ins[3].wait()
    base = jnp.minimum(step, NS - 1) * T
    rs = pl.ds(pl.multiple_of(base, T), T)
    sub_rows = lambda s: pl.ds(pl.multiple_of(base + s.start, SR), SR)
    total = lambda k: jnp.sum(jnp.sum(st_s[k], axis=0), axis=1, keepdims=True) * (1.0 / ff)
    def moments():
        mu = total(0)
        return mu, lax.rsqrt(total(1) - mu * mu + EPS)
    @pl.when(step < NS)
    def _():
        h_s[0] = nt(c_s[rs, :], fc1[cols[0], :])
        for c in range(NC):
            for s in subs:
                h = h_s[c % 2, s, :]
                phi, den = gelu_parts(h)
                u = h * phi
                u_s[s, cols[c]] = u
                d_s[s, cols[c]] = phi + h * den
                st_s[0, c, s, :] = fold(u); st_s[1, c, s, :] = fold(u * u)
            if c + 1 < NC: h_s[(c + 1) % 2] = nt(c_s[rs, :], fc1[cols[c + 1], :])
    @pl.when(step == 0)
    def _():
        ins[4].wait(); ins[5].wait()
    @pl.when(step < NS)
    def _():
        mu, R = moments()
        dm_s[:, cols[0]] = nt(g_ref[rs, :], fc2[cols[0], :])
        for c in range(NC):
            gain = mid[0:1, cols[c]]; shift = mid[1:2, cols[c]]
            g6 = jnp.zeros((8, K), f32); g7 = jnp.zeros((8, K), f32)
            for s in subs:
                uh = (u_s[s, cols[c]] - mu[s]) * R[s]
                u_s[s, cols[c]] = uh
                m_s[sub_rows(s), cols[c]] = (uh * gain + shift).astype(bf16)
                dm = dm_s[s, cols[c]]
                e = dm * gain
                dm_s[s, cols[c]] = e
                q = dm * uh
                g6 += jnp.sum(q.reshape(SR // 8, 8, K), axis=0); g7 += jnp.sum(dm.reshape(SR // 8, 8, K), axis=0)
                st_s[2, c, s, :] = fold(e); st_s[3, c, s, :] = fold(e * uh)
            gmid[6:7, cols[c]] += colsum(g6)
            gmid[7:8, cols[c]] += colsum(g7)
            if c + 1 < NC: dm_s[:, cols[c + 1]] = nt(g_ref[rs, :], fc2[cols[c + 1], :])
    @pl.when(step < NS)
    def _():
        R = moments()[1]
        se = total(2); seu = total(3)
        for c in range(NC):
            for s in subs:
                dh = (dm_s[s, cols[c]] - se[s] - u_s[s, cols[c]] * seu[s]) * R[s] * d_s[s, cols[c]]
                dh_s[sub_rows(s), cols[c]] = dh.astype(bf16)
            if c == 0:
                out_ref[rs, :] = (y_s[rs, :] + nn(m_s[rs, :], fc2[...])).astype(bf16)
    @pl.when(step < NS)
    def _():
        dc_s[rs, :] = nn(dh_s[rs, :], fc1[...])
    def grads(lanes):
        gfc2[0] = tn(m_s[:, lanes], g_ref[...]).astype(bf16)
        gfc1[0] = tn(dh_s[:, lanes], c_s[...]).astype(bf16)
    @pl.when(step == NS)
    def _():
        hs = []
        for sl in tiles:
            yh, yr = stats(y_s[sl, :])
            dc = dc_s[sl, :]
            gvec[4:5, :] += colsum(dc * yh)
            gvec[5:6, :] += colsum(dc)
            dy_ref[sl, :] = (g_ref[sl, :].astype(f32) + ln_back(dc, yh, yr, fg)).astype(bf16)
        for sl in tiles:
            dc_s[sl, :] = nt(dy_ref[sl, :], wo[...])
        for sl in tiles:
            dbn = dc_s[sl, :]
            o = o_ref[sl, :].astype(f32)
            oh, orr = stats(o)
            gvec[2:3, :] += colsum(dbn * oh)
            gvec[3:4, :] += colsum(dbn)
            do = ln_back(dbn, oh, orr, sg).astype(bf16)
            do_ref[sl, :] = do
            pr = do.astype(f32) * o
            hi = pr.astype(bf16)
            lo = (pr - hi.astype(f32)).astype(bf16)
            delta_ref[:, sl] = nt(sel[...], hi) + nt(sel[...], lo)
        grads(cols[0])
        gwo[...] = tn(b_s[...], dy_ref[...]).astype(bf16)
        for c in outs: c.start()
    @pl.when(step > NS)
    def _():
        grads(pl.ds(pl.multiple_of((step - NS) * K, K), K))
    @pl.when(step == NS + NC - 1)
    def _():
        for c in outs: c.wait()

def ffn(o, x, g, wo, fc1, fc2, vec, mid, T=256, K=512, dt=f32, SR=16, UT=1):
    rows, D = x.shape; ff = fc1.shape[0]; NC = ff // K; NT = rows // T; NS = NT // UT
    head = np.arange(D)[None] // 64
    sel = jnp.asarray((np.arange(16)[:, None] == head // (D // 128) * 8 + head % (D // 128)).astype(np.float32), bf16)
    one = dict(pipeline_mode=pl.Buffered(1))
    full = lambda *s: pl.BlockSpec(s, lambda i: (0,) * len(s), **one)
    A = pl.BlockSpec(memory_space=pl.ANY)
    chunk = pl.BlockSpec((1, K, D), lambda s: (jnp.maximum(s - NS, 0), 0, 0))
    sds = jax.ShapeDtypeStruct
    M = pltpu.VMEM
    act = sds((rows, D), bf16)
    delta, gvec, gmid, g1, g2, out, dy, do, gwo = pl.pallas_call(functools.partial(ffn_kernel, T=T, NT=NT, NC=NC, SR=SR, UT=UT), name="ffn",
        grid=(NS + NC,),
        in_specs=[full(8, D), full(8, ff), full(16, D)] + [A] * 6,
        out_specs=[full(16, rows), full(8, D), full(8, ff), chunk, chunk, full(rows, D)] + [A] * 3,
        out_shape=[sds((16, rows), f32), sds((8, D), f32), sds((8, ff), f32), sds((NC, K, D), bf16), sds((NC, K, D), bf16),
                   act, act, act, sds((D, D), bf16)],
        scratch_shapes=[M((rows, D), bf16), M((D, D), bf16), M((rows, D), bf16)][:0] + [M((rows, D), bf16), M((rows, D), bf16), M((rows, D), bf16),
                        M((D, D), bf16), M((ff, D), bf16), M((ff, D), bf16), M((rows, D), bf16), M((rows, D), bf16), M((D, D), bf16),
                        M((2, T, K), f32), M((T, ff), f32), M((T, ff), f32), M((T, ff), f32),
                        M((rows, ff), bf16), M((rows, ff), bf16), M((rows, D), bf16), M((rows, D), bf16), M((rows, D), f32), M((rows, D), f32),
                        M((4, NC, T, 128), f32), pltpu.SemaphoreType.DMA((10,))],
        compiler_params=pltpu.CompilerParams(vmem_limit_bytes=63 << 20, dimension_semantics=("arbitrary",)))(
            vec, mid, sel, o, x, g, wo, fc1, fc2)
    return out, dy, do, delta, gwo, g1, g2, gvec, gmid

MESH = pl.DeviceIdType.MESH

def place():
    dp, tp = lax.axis_index("dp"), lax.axis_index("tp")
    q, z = dp % 4, dp // 4
    dx = 1 - 2 * (dp % 2)
    dy = 2 - 4 * ((dp // 2) % 2)
    a, b = (1 - tp) * dx + tp * dy, tp * dx + (1 - tp) * dy
    return dict(dp=dp, tp=tp, z=z, q=q, qa=q + a, qb=q + b, qab=q + a + b,
                a=(dp + a, tp), b=(dp + b, tp), peer=(dp, 1 - tp),
                zs=[((dp + 4 * k) % 16, tp) for k in (1, 2, 3)], zi=[(z + k) % 4 for k in (1, 2, 3)])

def enter(w):
    bar = pltpu.get_barrier_semaphore()
    for d in [w["a"], w["b"], w["peer"]] + w["zs"]:
        pl.semaphore_signal(bar, inc=1, device_id=d, device_id_type=MESH)
    pl.semaphore_wait(bar, 6)

class Copy:
    def __init__(self, ss, rs):
        self.ss, self.rs, self.n, self.all = ss, rs, 0, []
    def __call__(self, src, dst, dev):
        c = pltpu.make_async_remote_copy(src_ref=src, dst_ref=dst, send_sem=self.ss.at[self.n], recv_sem=self.rs.at[self.n],
                                         device_id=dev, device_id_type=MESH)
        self.n += 1
        self.all.append(c)
        return c

def go_all(cs):
    for c in cs: c.start()

def got(cs):
    for c in cs: c.wait_recv()

class Gather:
    def __init__(self, copy, w, src, slot, view, peer):
        q, qa, qb, qab = w["q"], w["qa"], w["qb"], w["qab"]
        own = slot(w["z"], q)
        far = [slot(z, q) for z in w["zi"]]
        self.z = [copy(src, own, d) for d in w["zs"]]
        self.a = [copy(src, own, w["a"])] + [copy(s, s, w["a"]) for s in far]
        self.b = [copy(src, own, w["b"])] + [copy(s, s, w["b"]) for s in far]
        self.ab = [copy(view(qa), view(qa), w["b"])]
        self.p = [copy(view(c), view(c), w["peer"]) for c in (q, qa, qb, qab)] if peer else []
    def start(self):
        go_all(self.z + self.a[:1] + self.b[:1])
    def after_z(self):
        got(self.z)
        for k in (1, 2, 3): go_all([self.a[k], self.b[k]])
        go_all(self.p[:1])
    def after_a(self):
        got(self.a)
        go_all(self.ab + self.p[1:2])
    def after_b(self):
        got(self.b + self.ab)
        go_all(self.p[2:])
    def finish(self):
        got(self.p)

N_COPIES = 112

def k12_kernel(len_ref, tok, wq, wos, vpk, e24, e96, rsel, fc1s, fc2s,
               o_out, lse_ref, vec, mid, xh_h, qkv_h, wown_h, wo_h, fc1_h, fc2_h,
               xh16, qkv, wown, afull, xp, vbuf, sb, rb, woc, o_loc, fq, fk, q2, m_s, l_s, acc, ss, rs, ls, *, B, pairs, stage=9):
    w = place()
    tp = w["tp"]
    rows, D = tok.shape
    W = pairs * 128
    send = Copy(ss, rs)
    first = tp == 0
    sb[...] = jnp.zeros_like(sb)
    pick = lambda c0, n: (jnp.where(first, wq[:, c0:c0 + W], wq[:, c0 + W:c0 + 2 * W]).astype(bf16),
                          jnp.where(first, wq[:, c0 + W:c0 + 2 * W], wq[:, c0:c0 + W]).astype(bf16))
    mine = []
    for k in range(3):
        own, oth = pick(k * D, W)
        mine.append(own); sb[0:24, k * W:(k + 1) * W] = oth
    own_o = jnp.where(first, wos[:, :W], wos[:, W:])
    sb[0:24, 3 * W:4 * W] = jnp.where(first, wos[:, W:], wos[:, :W])
    vbuf[w["z"], w["q"], tp] = vpk[...]
    loc = [pltpu.make_async_copy(fc1s, fc1_h.at[w["z"], w["q"], tp], ls.at[0]),
           pltpu.make_async_copy(fc2s, fc2_h.at[w["z"], w["q"], tp], ls.at[1])]
    for c in loc: c.start()
    enter(w)
    cpre = send(sb, rb, w["peer"])
    gv = Gather(send, w, vbuf.at[w["z"], w["q"], tp], lambda z, q: vbuf.at[z, q, tp], lambda q: vbuf.at[:, q, tp], True)
    cx = send(tok, xp, w["peer"])
    gq = [Gather(send, w, wown.at[p, w["z"], w["q"]], lambda z, q, p=p: wown.at[p, z, q], lambda q, p=p: wown.at[p, :, q], False)
          for p in range(pairs)]
    keep = [pltpu.make_async_copy(v, h, ls.at[3 + k]) for k, (v, h) in enumerate(((xh16, xh_h), (qkv, qkv_h), (wown, wown_h)))]
    cols = pl.ds(pl.multiple_of(tp * W, 128), W)
    go = Gather(send, w, woc, lambda z, q: wo_h.at[z, q, :, cols], lambda q: wo_h.at[:, q, :, cols], True)
    g1 = Gather(send, w, fc1s, lambda z, q: fc1_h.at[z, q, tp], lambda q: fc1_h.at[:, q, tp], True)
    g2 = Gather(send, w, fc2s, lambda z, q: fc2_h.at[z, q, tp], lambda q: fc2_h.at[:, q, tp], True)
    peer_rows = pl.ds(pl.multiple_of((1 - tp) * rows, rows), rows)
    co = [send(o_loc.at[peer_rows, p * 128:(p + 1) * 128],
               o_out.at[:, pl.ds(pl.multiple_of(tp * W + p * 128, 128), 128)], w["peer"]) for p in range(pairs)]
    cpre.start()
    gv.start()
    cx.start()
    cpre.wait_recv()
    other = rb[0:24, :].astype(f32)
    me = jnp.concatenate(mine + [own_o], axis=1).astype(f32)
    both = jnp.concatenate([jnp.where(first, me, other), jnp.where(first, other, me)], axis=0).astype(bf16)
    for p in range(pairs):
        for k in range(3):
            wown[p, w["z"], w["q"], :, k * 128:(k + 1) * 128] = both[:, k * W + p * 128:k * W + (p + 1) * 128]
    woc[...] = both[:, 3 * W:]
    gq[0].start()
    lw = pltpu.make_async_copy(woc, wo_h.at[w["z"], w["q"], :, cols], ls.at[2])
    lw.start()
    gv.after_z(); gv.after_a()
    gq[0].after_z()
    gq[1].start()
    gv.after_b(); gv.finish()
    small = nn(rsel[...], vbuf[...].reshape(512, 128)).astype(bf16)
    dev = lax.broadcasted_iota(jnp.int32, (32, 1), 0)
    def spread(v, e, n):
        lane = lax.broadcasted_iota(jnp.int32, (1, e.shape[1]), 1)
        hit = (lane >= dev * n) & (lane < dev * n + n)
        return colsum(jnp.where(hit, nn(small[v * 32:(v + 1) * 32], e[...]), 0.0))
    for v in range(2): vec[v:v + 1, :] = spread(v, e24, 24)
    gq[0].after_a()
    def normed(src, base):
        def body(r, _):
            sl = pl.ds(pl.multiple_of(r * 256, 256), 256)
            xh, _r = stats(src[sl, :].astype(f32))
            to = pl.ds(pl.multiple_of(base + r * 256, 256), 256)
            xh16[to, :] = xh.astype(bf16)
            afull[to, :] = (xh * vec[0:1, :] + vec[1:2, :]).astype(bf16)
            return 0
        lax.fori_loop(0, rows // 256, body, 0)
    normed(tok, tp * rows)
    gq[0].after_b()
    gq[1].after_z()
    gq[2].start()
    for c in loc: c.wait()
    lw.wait()
    go.start(); g1.start()
    cx.wait_recv()
    normed(xp, (1 - tp) * rows)
    keep[0].start()
    doc_features(len_ref, 2 * rows, fq, fk)
    def proj(p):
        def body(r, _):
            sl = pl.ds(pl.multiple_of(r * 512, 512), 512)
            qkv[sl, p * 3 * 128:(p + 1) * 3 * 128] = nn(afull[sl, :], wown[p].reshape(D, 3 * 128)).astype(bf16)
            return 0
        lax.fori_loop(0, 2 * rows // 512, body, 0)
    proj(0)
    gq[1].after_a(); gq[2].after_z()
    g2.start()
    for v in range(2, 6): vec[v:v + 1, :] = spread(v, e24, 24)
    vec[6:8, :] = jnp.zeros((2, D), f32)
    for v in range(2): mid[v:v + 1, :] = spread(6 + v, e96, 96)
    mid[2:8, :] = jnp.zeros((6, 4 * D), f32)
    nb = 2 * rows // B
    half = lax.broadcasted_iota(jnp.int32, (1, 128), 1) < 64
    causal = lax.broadcasted_iota(jnp.int32, (B, B), 0) <= lax.broadcasted_iota(jnp.int32, (B, B), 1)
    causal = jnp.concatenate([causal, causal], axis=1)
    def unit(u, _):
        p, i = u // nb, u % nb
        def at(k):
            def deco(f): pl.when(u == k)(f)
            return deco
        @at(1)
        def _():
            gq[1].after_b(); gq[2].after_a()
        @at(3)
        def _():
            gq[2].after_b()
            keep[2].start()
        @at(4)
        def _():
            co[0].start()
            go.after_z(); g1.after_z()
            proj(1)
        @at(6)
        def _():
            go.after_a(); g1.after_a(); g2.after_z()
        @at(7)
        def _():
            go.after_b()
        @at(8)
        def _():
            co[1].start()
            proj(2)
            keep[1].start()
            g1.after_b()
        @at(10)
        def _():
            g2.after_a()
        qs = pl.ds(pl.multiple_of(i * B, B), B)
        lanes = lambda k: pl.ds(pl.multiple_of(p * 384 + k * 128, 128), 128)
        q = qkv[qs, lanes(0)] * bf16(0.125)
        fqb = fq[qs, :]
        z = jnp.zeros_like(q)
        q2[...] = jnp.concatenate([
            jnp.concatenate([jnp.where(half, q, z), fqb], axis=1),
            jnp.concatenate([jnp.where(half, z, q), fqb], axis=1)], axis=0)
        def block(j, diag):
            ks = pl.ds(pl.multiple_of(j * B, B), B)
            s = nt(jnp.concatenate([qkv[ks, lanes(1)], fk[ks, :]], axis=1), q2[...])
            if diag: s = jnp.where(causal, s, -BIG)
            mn = jnp.max(s, axis=0, keepdims=True)
            if not diag:
                mo = m_s[...]
                mn = jnp.maximum(mo, mn); al = jnp.exp(mo - mn)
            e = jnp.exp(s - mn)
            su = jnp.sum(e, axis=0, keepdims=True)
            pv = tn(qkv[ks, lanes(2)], e.astype(bf16))
            if diag: l_s[...] = su; acc[...] = pv
            else: l_s[...] = l_s[...] * al + su; acc[...] = acc[...] * al + pv
            m_s[...] = mn
        block(i, True)
        def kstep(j, _):
            block(j, False); return 0
        lax.fori_loop(0, i, kstep, 0)
        l = l_s[...]
        a = acc[...] * (1.0 / l)
        ot = jnp.concatenate([a[:64, :B], a[64:, B:]], axis=0)
        o_loc[qs, pl.ds(pl.multiple_of(p * 128, 128), 128)] = ot.T.astype(bf16)
        lse = m_s[...] + jnp.log(l)
        lse_ref[p, 0:1, qs] = lse[:, :B]
        lse_ref[p, 1:2, qs] = lse[:, B:]
        return 0
    lax.fori_loop(0, pairs * nb, unit, 0)
    co[2].start()
    g2.after_b()
    o_out[:, cols] = o_loc[pl.ds(pl.multiple_of(tp * rows, rows), rows), :]
    got(co)
    go.finish(); g1.finish(); g2.finish()
    for c in send.all: c.wait_send()
    for c in keep: c.wait()

def consts_np(D):
    k = np.arange(128)[:, None]
    e24 = (np.arange(D)[None] % 24 == k).astype(np.float32)
    e96 = (np.arange(4 * D)[None] % 96 == k).astype(np.float32)
    r = np.arange(256)[:, None]
    rsel = (np.arange(512)[None] == (r % 32) * 16 + r // 32).astype(np.float32)
    return e24, e96, rsel

def consts(D):
    return [jnp.asarray(c, bf16) for c in consts_np(D)]

def k12(lengths, tok, wq, wos, vpk, fc1s, fc2s, B=512):
    rows, D = tok.shape
    W = D // 2; pairs = W // 128
    V, A = pl.BlockSpec(memory_space=pltpu.VMEM), pl.BlockSpec(memory_space=pl.ANY)
    sds = jax.ShapeDtypeStruct
    hid = fc1s.shape[0]
    return pl.pallas_call(functools.partial(k12_kernel, B=B, pairs=pairs), name="forward",
        out_shape=(sds((rows, D), bf16), sds((pairs, 2, 2 * rows), f32), sds((8, D), f32), sds((8, 4 * D), f32),
                   sds((2 * rows, D), bf16), sds((2 * rows, 3 * W), bf16), sds((pairs, 4, 4, 48, 3 * 128), bf16),
                   sds((4, 4, 48, D), bf16), sds((4, 4, 2, hid, D), bf16), sds((4, 4, 2, hid, D), bf16)),
        in_specs=[pl.BlockSpec(memory_space=pltpu.SMEM)] + [V] * 7 + [A] * 2,
        out_specs=(V,) * 4 + (A,) * 6,
        scratch_shapes=[pltpu.VMEM((2 * rows, D), bf16), pltpu.VMEM((2 * rows, 3 * W), bf16), pltpu.VMEM((pairs, 4, 4, 48, 3 * 128), bf16), pltpu.VMEM((2 * rows, D), bf16), pltpu.VMEM((rows, D), bf16), pltpu.VMEM((4, 4, 2, 16, 128), bf16), pltpu.VMEM((32, 4 * W), bf16), pltpu.VMEM((32, 4 * W), bf16),
                        pltpu.VMEM((48, W), bf16), pltpu.VMEM((2 * rows, W), bf16), pltpu.VMEM((2 * rows, 128), bf16), pltpu.VMEM((2 * rows, 128), bf16),
                        pltpu.VMEM((2 * B, 256), bf16), pltpu.VMEM((1, 2 * B), f32), pltpu.VMEM((1, 2 * B), f32), pltpu.VMEM((128, 2 * B), f32),
                        pltpu.SemaphoreType.DMA((N_COPIES,)), pltpu.SemaphoreType.DMA((N_COPIES,)), pltpu.SemaphoreType.DMA((6,))],
        compiler_params=pltpu.CompilerParams(vmem_limit_bytes=60 << 20, collective_id=0, has_side_effects=True))(
            lengths, tok, wq, wos, vpk, *consts(D), fc1s, fc2s)

def pack_vectors(six, two):
    n6 = jnp.pad(jnp.stack(six), ((0, 0), (0, 128 - six[0].shape[0])))
    n2 = jnp.pad(jnp.stack(two), ((0, 8), (0, 128 - two[0].shape[0])))
    return jnp.concatenate([n6, n2], axis=0)


def add(x, y):
    return (x.astype(f32) + y.astype(f32)).astype(x.dtype)

class Scatter:
    def __init__(self, copy, w, s, bb, ab, zb):
        self.w, self.s, self.bb, self.ab, self.zb = w, s, bb, ab, zb
        self.b = [copy(s.at[:, w["qb"]], bb.at[0], w["b"]), copy(s.at[:, w["qab"]], bb.at[1], w["b"])]
        self.a = [copy(s.at[:, w["qa"]], ab, w["a"])]
        self.z = [copy(s.at[w["zi"][k], w["q"]], zb.at[k], w["zs"][k]) for k in range(3)]
    def go(self, cs):
        for c in cs: c.start()
    def start(self):
        self.go(self.b)
    def after_b(self):
        for c in self.b: c.wait_recv()
        for z in range(4):
            self.s[z, self.w["qa"]] = add(self.s[z, self.w["qa"]], self.bb[1, z])
        self.go(self.a)
        for z in range(4):
            self.s[z, self.w["q"]] = add(self.s[z, self.w["q"]], self.bb[0, z])
    def after_a(self):
        for c in self.a: c.wait_recv()
        for z in range(4):
            self.s[z, self.w["q"]] = add(self.s[z, self.w["q"]], self.ab[z])
        self.go(self.z)
    def result(self):
        for c in self.z: c.wait_recv()
        r = self.s[self.w["z"], self.w["q"]].astype(f32)
        for k in range(3): r = r + self.zb[k].astype(f32)
        return r

def k45_kernel(len_ref, do, delta, lse_ref, vec, gvec, gmid, e24t, e96t, qkv_h, xh_h, wown_h, gwo_h, tok_h, dy_h, g1_h, g2_h,
               gtok, gq_o, gwo_o, g1_o, g2_o, small_o, pre_o,
               qkv, xh16, wown, gwo, tok, dy, do_own, dl_own, fq, fk, q2, do2, dq, dk, dv,
               s1, r1, b1, a1, z1, s2, r2, b2, a2, z2, so, ro, bo, ao, zo, *rest, B, pairs):
    flows, rest = rest[:4 * pairs], rest[4 * pairs:]
    (sm, pm, s4, bm, am, zm, da, dsend, drecv, fo, xo, fqk, xq, gcol, bcol, vacc, uacc, ss, rs, ls) = rest
    w = place()
    tp = w["tp"]
    rows, D = tok.shape
    W = pairs * 128
    nb = 2 * rows // B
    first = tp == 0
    other = 1 - tp
    mine_rows = pl.ds(pl.multiple_of(tp * rows, rows), rows)
    mine_cols = pl.ds(pl.multiple_of(tp * W, 128), W)
    other_cols = pl.ds(pl.multiple_of(other * W, 128), W)
    copy = Copy(ss, rs)
    c_do = copy(do.at[:, other_cols], do_own.at[mine_rows, :], w["peer"])
    c_dl = copy(delta.at[pl.ds(pl.multiple_of(other * 8, 8), 8), :], dl_own.at[:, mine_rows], w["peer"])
    c_r2 = copy(g2_h.at[:, :, other], r2, w["peer"])
    c_r1 = copy(g1_h.at[:, :, other], r1, w["peer"])
    c_ro = copy(gwo_h.at[:, other_cols], ro, w["peer"])
    f1, f2 = Scatter(copy, w, s1, b1, a1, z1), Scatter(copy, w, s2, b2, a2, z2)
    fo_ = Scatter(copy, w, so, bo, ao, zo)
    fqs = [Scatter(copy, w, *flows[4 * p:4 * p + 4]) for p in range(pairs)]
    fm = Scatter(copy, w, s4, bm, am, zm)
    c_pm = copy(sm.at[:, :, other], pm, w["peer"])
    hr = rows // 2
    c_da = [copy(dsend.at[pl.ds(k * hr, hr), :], drecv.at[pl.ds(k * hr, hr), :], w["peer"]) for k in range(2)]
    n = gq_o.shape[0]
    other_n = pl.ds(pl.multiple_of(other * n, 8), n)
    mine_n = pl.ds(pl.multiple_of(tp * n, 8), n)
    c_xo = copy(fo.at[other_n, :], xo, w["peer"])
    c_xq = copy(fqk.at[other_n, :], xq, w["peer"])
    l_q = pltpu.make_async_copy(qkv_h, qkv, ls.at[0])
    l_2 = pltpu.make_async_copy(g2_h.at[:, :, tp], s2, ls.at[1])
    l_1 = pltpu.make_async_copy(g1_h.at[:, :, tp], s1, ls.at[2])
    l_t = pltpu.make_async_copy(tok_h, tok, ls.at[3])
    l_y = pltpu.make_async_copy(dy_h, dy, ls.at[4])
    l_o = pltpu.make_async_copy(gwo_h, gwo, ls.at[5])
    l_x = pltpu.make_async_copy(xh_h, xh16, ls.at[6])
    l_w = [pltpu.make_async_copy(wown_h.at[p], wown.at[:, p * 384:(p + 1) * 384], ls.at[7 + p]) for p in range(pairs)]
    for l in [l_q, l_2, l_o, l_1, l_x] + l_w + [l_t, l_y]: l.start()
    enter(w)
    for c in (c_do, c_dl): c.start()
    do_own[mine_rows, :] = do[:, mine_cols]
    dl_own[:, mine_rows] = delta[pl.ds(pl.multiple_of(tp * 8, 8), 8), :]
    doc_features(len_ref, 2 * rows, fq, fk)
    dev = lax.broadcasted_iota(jnp.int32, (32, 1, 1), 0)
    def pieces(v, e, n):
        lane = lax.broadcasted_iota(jnp.int32, (1, 1, v.shape[1]), 2)
        hit = (lane >= dev * n) & (lane < dev * n + n)
        t = jnp.where(hit, v[None], 0.0).reshape(256, v.shape[1])
        hi = t.astype(bf16)
        return nn(hi, e) + nn((t - hi.astype(f32)).astype(bf16), e)
    early = pieces(gmid[...], e96t[...], 4 * D // 32) + pieces(gvec[...], e24t[...], D // 32)
    sm[...] = early.reshape(4, 4, 2, 8, 128)
    c_pm.start()
    gcol[...] = jnp.broadcast_to(vec[0:1, :], (128, D)).T
    bcol[...] = jnp.broadcast_to(vec[1:2, :], (128, D)).T
    vacc[...] = jnp.zeros_like(vacc); uacc[...] = jnp.zeros_like(uacc)
    l_q.wait()
    c_do.wait_recv(); c_dl.wait_recv()
    c_r2.start(); c_ro.start()

    half = lax.broadcasted_iota(jnp.int32, (1, 128), 1) < 64
    causal = lax.broadcasted_iota(jnp.int32, (B, B), 0) <= lax.broadcasted_iota(jnp.int32, (B, B), 1)
    causal = jnp.concatenate([causal, causal], axis=1)
    def grads(p):
        out = flows[4 * p]
        cs = [slice(p * 384 + k * 128, p * 384 + (k + 1) * 128) for k in range(3)]
        g = qkv[:, p * 384:(p + 1) * 384]
        t = tn(xh16[...], g)
        gsum = jnp.sum(g.astype(f32), axis=0, keepdims=True)
        for k in range(3):
            sl = slice(k * 128, (k + 1) * 128)
            wk = wown[:, cs[k]].astype(f32)
            tk, sk = t[:, sl], gsum[:, sl]
            out[:, :, :, sl] = (gcol[...] * tk + bcol[...] * sk).astype(bf16).reshape(4, 4, 48, 128)
            vacc[...] += tk * wk
            uacc[...] += sk * wk
        if p == pairs - 1:
            lane = lax.broadcasted_iota(jnp.int32, (1, 128), 1)
            e = jnp.where(lane == 0, jnp.sum(vacc[...], axis=1, keepdims=True), 0.0)
            e = jnp.where(lane == 1, jnp.sum(uacc[...], axis=1, keepdims=True), e)
            out[:, :, :, 384:512] = e.astype(bf16).reshape(4, 4, 48, 128)
    def unit(u, _):
        p, j = u // nb, u % nb
        lanes = lambda k: pl.ds(pl.multiple_of(p * 384 + k * 128, 128), 128)
        def at(k):
            def deco(f): pl.when(u == k)(f)
            return deco
        @at(1)
        def _():
            c_pm.wait_recv()
            for z in range(4):
                for k in range(4): s4[z, k] = sm[z, k, tp] + pm[z, k]
            fm.start()
            c_r2.wait_recv(); l_2.wait()
            c_r1.start()
            for z in range(4):
                for k in range(4): s2[z, k] = add(s2[z, k], r2[z, k])
            f2.start()
            c_ro.wait_recv(); l_o.wait()
            so[...] = add(gwo[:, mine_cols], ro[...]).reshape(so.shape)
            fo_.start()
        @at(2)
        def _():
            fm.after_b()
            c_r1.wait_recv(); l_1.wait()
            for z in range(4):
                for k in range(4): s1[z, k] = add(s1[z, k], r1[z, k])
        @at(3)
        def _():
            fm.after_a()
        @at(4)
        def _():
            l_x.wait()
            for l in l_w: l.wait()
            grads(0)
            f2.after_b(); fo_.after_b(); f1.start()
            small_o[...] = fm.result()
        @at(5)
        def _():
            fqs[0].start()
        @at(6)
        def _():
            fo_.after_a()
        @at(7)
        def _():
            f2.after_a(); fqs[0].after_b()
        @at(8)
        def _():
            grads(1)
            f1.after_b(); fqs[1].start()
        @at(9)
        def _():
            f1.after_a(); fqs[0].after_a()
            fo[...] = fo_.result()
            c_xo.start()
        @at(10)
        def _():
            fqs[1].after_b()
        @at(11)
        def _():
            fqs[1].after_a()
            g2_o[...] = f2.result()
        @pl.when(j == 0)
        def _():
            def prep(i, _):
                qs = pl.ds(pl.multiple_of(i * B, B), B)
                q = qkv[qs, lanes(0)] * bf16(0.125)
                d = do_own[qs, pl.ds(pl.multiple_of(p * 128, 128), 128)]
                fqb = fq[qs, :]
                z = jnp.zeros_like(q)
                q2[i] = jnp.concatenate([
                    jnp.concatenate([jnp.where(half, q, z), fqb], axis=1),
                    jnp.concatenate([jnp.where(half, z, q), fqb], axis=1)], axis=0)
                do2[i] = jnp.concatenate([jnp.where(half, d, z), jnp.where(half, z, d)], axis=0)
                dq[i] = jnp.zeros(dq.shape[1:], f32)
                return 0
            lax.fori_loop(0, nb, prep, 0)
        ks = pl.ds(pl.multiple_of(j * B, B), B)
        kt = qkv[ks, lanes(1)]
        v = qkv[ks, lanes(2)]
        k2 = jnp.concatenate([kt, fk[ks, :]], axis=1)
        def block(i, diag):
            qs = pl.ds(pl.multiple_of(i * B, B), B)
            lse = jnp.concatenate([lse_ref[p, 0:1, qs], lse_ref[p, 1:2, qs]], axis=1)
            d0 = pl.ds(2 * p, 1); d1 = pl.ds(2 * p + 1, 1)
            dl = jnp.concatenate([dl_own[d0, qs], dl_own[d1, qs]], axis=1)
            qq = q2[i]; dd = do2[i]
            pt = jnp.exp(nt(k2, qq) - lse)
            if diag: pt = jnp.where(causal, pt, 0.0)
            ds = (pt * (nt(v, dd) - dl)).astype(bf16)
            dvp = nn(pt.astype(bf16), dd)
            dkp = nn(ds, qq[:, :128])
            if diag: dv[...] = dvp; dk[...] = dkp
            else: dv[...] += dvp; dk[...] += dkp
            dq[i] += tn(ds, kt)
        block(j, True)
        def qstep(i, _):
            block(i, False); return 0
        lax.fori_loop(j + 1, nb, qstep, 0)
        qkv[ks, lanes(1)] = dk[...].astype(bf16)
        qkv[ks, lanes(2)] = dv[...].astype(bf16)
        @pl.when(j == nb - 1)
        def _():
            def fin(i, _):
                qs = pl.ds(pl.multiple_of(i * B, B), B)
                d = dq[i]
                qkv[qs, lanes(0)] = (jnp.where(half, d[:B], d[B:]) * 0.125).astype(bf16)
                return 0
            lax.fori_loop(0, nb, fin, 0)
        return 0
    lax.fori_loop(0, pairs * nb, unit, 0)
    grads(2)
    fqs[2].start()
    for k in range(2):
        sl = pl.ds(pl.multiple_of(other * rows + k * hr, hr), hr)
        dsend[k * hr:(k + 1) * hr, :] = nt(qkv[sl, :], wown[...]).astype(bf16)
        c_da[k].start()
    fqs[2].after_b()
    g1_o[...] = f1.result()
    for k in range(2):
        sl = pl.ds(pl.multiple_of(tp * rows + k * hr, hr), hr)
        da[k * hr:(k + 1) * hr, :] = nt(qkv[sl, :], wown[...])
        if k == 0: fqs[2].after_a()
    l_t.wait(); l_y.wait()
    for c in c_da: c.wait_recv()
    gain = vec[0:1, :]
    def fin(r, _):
        sl = pl.ds(pl.multiple_of(r * 256, 256), 256)
        d = da[sl, :] + drecv[sl, :].astype(f32)
        xh, xr = stats(tok[sl, :].astype(f32))
        gtok[sl, :] = (dy[sl, :].astype(f32) + ln_back(d, xh, xr, gain)).astype(bf16)
        return 0
    def collect(p):
        r = fqs[p].result()
        fqk[:, p * 384:(p + 1) * 384] = r[:, :384]
        if p == pairs - 1: fqk[:, pairs * 384:] = r[:, 384:]
    for p in range(pairs - 1): collect(p)
    lax.fori_loop(0, rows // 256, fin, 0)
    collect(pairs - 1)
    c_xq.start()
    c_xo.wait_recv()
    mine = fo[mine_n, :]
    gwo_o[:, :W] = jnp.where(first, mine, xo[...])
    gwo_o[:, W:] = jnp.where(first, xo[...], mine)
    c_xq.wait_recv()
    for p in range(pairs):
        for k in range(3):
            src = p * 384 + k * 128
            mine = fqk[mine_n, src:src + 128]
            oth = xq[:, src:src + 128]
            c0 = k * D + p * 128
            gq_o[:, c0:c0 + 128] = jnp.where(first, mine, oth)
            gq_o[:, c0 + W:c0 + W + 128] = jnp.where(first, oth, mine)
    pre_o[...] = fqk[mine_n, 3 * W:] + xq[:, 3 * W:]
    for c in copy.all: c.wait_send()

def k45(lengths, xh, wown, do, delta, lse, vec, gvec, gmid, gwo, qkv, tok, dy, g1, g2, B=512):
    rows, D = tok.shape
    W = D // 2; pairs = W // 128; nb = 2 * rows // B
    V, A = pl.BlockSpec(memory_space=pltpu.VMEM), pl.BlockSpec(memory_space=pl.ANY)
    sds = jax.ShapeDtypeStruct
    hid = g1.shape[3]
    M = pltpu.VMEM
    e24t, e96t = [c.T for c in consts_np(D)[:2]]
    def flow(r, c, t, lead=()):
        return [M(lead + (4, 4, r, c), t), M(lead + (2, 4, r, c), t), M(lead + (4, r, c), t), M(lead + (3, r, c), t)]
    fc = flow(hid, D, bf16)
    fc = [fc[0], M((4, 4, hid, D), bf16)] + fc[1:]
    wo = flow(48, W, bf16)
    wo = [wo[0], M((D, W), bf16)] + wo[1:]
    sm = flow(8, 128, f32)
    return pl.pallas_call(functools.partial(k45_kernel, B=B, pairs=pairs), name="backward",
        out_shape=(sds((rows, D), bf16), sds((D // 32, 3 * D), f32), sds((D // 32, D), f32), sds((hid, D), f32), sds((hid, D), f32), sds((8, 128), f32), sds((D // 32, 128), f32)),
        in_specs=[pl.BlockSpec(memory_space=pltpu.SMEM)] + [V] * 8 + [A] * 8,
        out_specs=(V,) * 7,
        scratch_shapes=[M((2 * rows, 3 * W), bf16), M((2 * rows, D), bf16), M((D, 3 * W), bf16), M((D, D), bf16), M((rows, D), bf16), M((rows, D), dy.dtype), M((2 * rows, W), bf16), M((8, 2 * rows), f32),
                        M((2 * rows, 128), bf16), M((2 * rows, 128), bf16), M((nb, 2 * B, 256), bf16), M((nb, 2 * B, 128), bf16), M((nb, 2 * B, 128), f32),
                        M((B, 128), f32), M((B, 128), f32)] + fc + fc + wo + flow(48, W, bf16) * (pairs - 1) + flow(48, W + 128, bf16) +
                       [M((4, 4, 2, 8, 128), f32), M((4, 4, 8, 128), f32)] + sm +
                       [M((rows, D), f32), M((rows, D), bf16), M((rows, D), bf16), M((48, W), f32), M((24, W), f32), M((48, 3 * W + 128), f32), M((24, 3 * W + 128), f32),
                        M((D, 128), f32), M((D, 128), f32), M((D, 128), f32), M((D, 128), f32),
                        pltpu.SemaphoreType.DMA((64,)), pltpu.SemaphoreType.DMA((64,)), pltpu.SemaphoreType.DMA((10,))],
        compiler_params=pltpu.CompilerParams(vmem_limit_bytes=63 << 20, collective_id=1, has_side_effects=True))(
            lengths, do, delta, lse, vec, gvec, gmid, jnp.asarray(e24t, bf16), jnp.asarray(e96t, bf16), qkv, xh, wown, gwo, tok, dy, g1, g2)

def local_fast(tokens, cotangent, lengths, qkv_weight, out_weight, pre_gain, pre_shift, sub_gain, sub_shift,
          ffn_gain, ffn_shift, fc1_weight, mid_gain, mid_shift, fc2_weight):
    rows, D = tokens.shape
    vpk = pack_vectors([pre_gain, pre_shift, sub_gain, sub_shift, ffn_gain, ffn_shift], [mid_gain, mid_shift])
    o, lse, vec, mid, xh16, qkv, wown, wo, fc1, fc2 = k12(lengths, tokens, qkv_weight, out_weight, vpk, fc1_weight, fc2_weight)
    block_out, dy, do, delta, gwo, g1, g2, gvec, gmid = ffn(o, tokens, cotangent, wo.reshape(D, D), fc1.reshape(4 * D, D), fc2.reshape(4 * D, D), vec, mid)
    shape = (4, 4, 2, fc1_weight.shape[0], D)
    gtok, gq, gwo, g1, g2, small, pre = k45(lengths, xh16, wown.reshape(3, D, 384), do, delta, lse, vec, gvec, gmid, gwo, qkv, tokens, dy, g1.reshape(shape), g2.reshape(shape))
    n, m = pre_gain.shape[0], mid_gain.shape[0]
    return (block_out, gtok, gq, gwo, pre[:, 0], pre[:, 1], small[2, :n], small[3, :n], small[4, :n], small[5, :n],
            g1, small[6, :m], small[7, :m], g2)

def norm(v):
    return stats(v)


def local_any(tokens, cotangent, lengths, qkv_weight, out_weight, pre_gain, pre_shift, sub_gain, sub_shift,
          ffn_gain, ffn_shift, fc1_weight, mid_gain, mid_shift, fc2_weight):
    rows, D = tokens.shape
    W = D // 2
    tp = lax.axis_index("tp")
    both = ("dp", "tp")
    gather = lambda a: lax.all_gather(a, both, axis=0, tiled=True)
    small = gather(jnp.stack([pre_gain, pre_shift, sub_gain, sub_shift, ffn_gain, ffn_shift], axis=1)).astype(f32).T
    mid = gather(jnp.stack([mid_gain, mid_shift], axis=1)).astype(f32).T
    wq = gather(qkv_weight)
    wo, fc1, fc2 = gather(out_weight), gather(fc1_weight), gather(fc2_weight)
    wown = lax.dynamic_index_in_dim(wq.reshape(D, 3, 2, W), tp, 2, keepdims=False).reshape(D, 3 * W)
    x = tokens.astype(f32)
    xh, xr = norm(x)
    a = (xh * small[0] + small[1]).astype(bf16)
    afull = lax.all_gather(a, "tp", axis=0, tiled=True)
    qkv = nn(afull, wown).astype(bf16)
    o_own, lse = attn_fwd(lengths, qkv, B=512)
    o = lax.all_to_all(o_own, "tp", 0, 1, tiled=True)
    vec = jnp.concatenate([small, jnp.zeros((2, D), f32)], axis=0)
    block_out, dy, do, delta, gwo, gfc1, gfc2, gvec, gmid = ffn(
        o, tokens, cotangent, wo, fc1, fc2, vec, jnp.concatenate([mid, jnp.zeros((6, 4 * D), f32)], axis=0))
    do_own = lax.all_to_all(do, "tp", 1, 0, tiled=True)
    dl_own = lax.all_to_all(delta, "tp", 0, 1, tiled=True)
    dqkv = attn_bwd(lengths, qkv, do_own, lse, dl_own, B=512)
    gq = tn(afull, dqkv)
    da = lax.psum_scatter(nt(dqkv, wown), "tp", scatter_dimension=0, tiled=True)
    grad_tokens = (dy.astype(f32) + ln_back(da, xh, xr, small[0])).astype(bf16)
    scatter = lambda v: lax.psum_scatter(v, both, scatter_dimension=0, tiled=True)
    gq = lax.psum_scatter(gq, "dp", scatter_dimension=0, tiled=True)
    n = gq.shape[0] // 2
    gq = lax.all_to_all(gq.reshape(2, n, 3, 1, W), "tp", 0, 3, tiled=True).reshape(n, 3 * D)
    small_grads = scatter(jnp.concatenate([jnp.stack([colsum(da * xh)[0], colsum(da)[0]]), gvec[2:6]], axis=0).T).T
    mid_grads = scatter(gmid[6:8].T).T
    gwo = scatter(gwo.astype(f32))
    gfc1 = scatter(gfc1.reshape(-1, D).astype(f32))
    gfc2 = scatter(gfc2.reshape(-1, D).astype(f32))
    return (block_out, grad_tokens, gq, gwo, small_grads[0], small_grads[1], small_grads[2], small_grads[3],
            small_grads[4], small_grads[5], gfc1, mid_grads[0], mid_grads[1], gfc2)


def local(*arrays):
    fits = lax.axis_size("dp") == 16 and lax.axis_size("tp") == 2
    return (local_fast if fits else local_any)(*arrays)


def solution(mesh):
    two, one = P(("dp", "tp"), None), P(("dp", "tp"))
    return jax.shard_map(
        local,
        mesh=mesh,
        in_specs=(two, two, P("dp", None), two, two, one, one, one, one, one, one, two, one, one, two),
        out_specs=(two, two, two, two, one, one, one, one, one, one, two, one, one, two),
        check_vma=False,
    )
```

```python
import functools

import jax
import jax.numpy as jnp
import numpy as np
from jax import lax
from jax.experimental import pallas as pl
from jax.experimental.pallas import tpu as pltpu
from jax.sharding import PartitionSpec as P

f32, bf16 = jnp.float32, jnp.bfloat16
EPS = 1e-5
BIG = 1e30


def nt(a, b):
    return lax.dot_general(a, b, (((1,), (1,)), ((), ())), preferred_element_type=f32)


def nn(a, b):
    return lax.dot_general(a, b, (((1,), (0,)), ((), ())), preferred_element_type=f32)


def tn(a, b):
    return lax.dot_general(a, b, (((0,), (0,)), ((), ())), preferred_element_type=f32)

def doc_features(len_ref, rows, fq, fk):
    lane = lax.broadcasted_iota(jnp.int32, (1, 128), 1)
    lo = jnp.zeros((1, 128), jnp.int32); hi = jnp.zeros((1, 128), jnp.int32)
    run = jnp.int32(0)
    for d in range(8):
        nxt = run + len_ref[0, d]
        lo = jnp.where(lane == d, run, lo); hi = jnp.where(lane == d, nxt, hi)
        run = nxt
    def body(r, _):
        place = lax.broadcasted_iota(jnp.int32, (256, 128), 0) + r * 256
        hit = (place >= lo) & (place < hi)
        sl = pl.ds(pl.multiple_of(r * 256, 256), 256)
        fq[sl, :] = jnp.where(hit, 1.0, 0.0).astype(bf16)
        fk[sl, :] = jnp.where(hit | (lane >= 8), 0.0, -BIG).astype(bf16)
        return 0
    lax.fori_loop(0, rows // 256, body, 0)

def fwd_t(len_ref, qkv, o_ref, lse_ref, fq, fk, q2, st_s, m_s, l_s, acc, *, B, pairs, variant):
    rows = qkv.shape[0]; nb = rows // B; W = pairs * 128
    doc_features(len_ref, rows, fq, fk)
    half = lax.broadcasted_iota(jnp.int32, (1, 128), 1) < 64
    causal = lax.broadcasted_iota(jnp.int32, (B, B), 0) <= lax.broadcasted_iota(jnp.int32, (B, B), 1)
    causal = jnp.concatenate([causal, causal], axis=1)
    for p in range(pairs):
        def qstep(i, _, p=p):
            qs = pl.ds(pl.multiple_of(i * B, B), B)
            q = qkv[qs, p * 128:(p + 1) * 128] * bf16(0.125)
            fqb = fq[qs, :]
            z = jnp.zeros_like(q)
            q2[...] = jnp.concatenate([
                jnp.concatenate([jnp.where(half, q, z), fqb], axis=1),
                jnp.concatenate([jnp.where(half, z, q), fqb], axis=1)], axis=0)
            def score(j):
                ks = pl.ds(pl.multiple_of(j * B, B), B)
                k2 = jnp.concatenate([qkv[ks, W + p * 128:W + (p + 1) * 128], fk[ks, :]], axis=1)
                return nt(k2, q2[...])
            def vblk(j):
                ks = pl.ds(pl.multiple_of(j * B, B), B)
                return qkv[ks, 2 * W + p * 128:2 * W + (p + 1) * 128]
            if variant == "online":
                def block(j, masked, first):
                    s = score(j)
                    if masked: s = jnp.where(causal, s, -BIG)
                    mx = jnp.max(s, axis=0, keepdims=True)
                    if first: mn = mx
                    else:
                        mo = m_s[...]
                        mn = jnp.maximum(mo, mx); al = jnp.exp(mo - mn)
                    e = jnp.exp(s - mn)
                    su = jnp.sum(e, axis=0, keepdims=True)
                    pv = tn(vblk(j), e.astype(bf16))
                    if first: l_s[...] = su; acc[...] = pv
                    else: l_s[...] = l_s[...] * al + su; acc[...] = acc[...] * al + pv
                    m_s[...] = mn
                block(i, True, True)
                def kstep(j, _):
                    block(j, False, False); return 0
                lax.fori_loop(0, i, kstep, 0)
                m = m_s[...]; l = l_s[...]
            else:
                def part(s): return jnp.max(s.reshape(B // 8, 8, 2 * B), axis=0)
                s = jnp.where(causal, score(i), -BIG)
                st_s[i] = s
                def pass1(j, m8):
                    s = score(j); st_s[j] = s
                    return jnp.maximum(m8, part(s))
                m8 = lax.fori_loop(0, i, pass1, part(s))
                m = jnp.max(m8, axis=0, keepdims=True)
                acc[...] = jnp.zeros_like(acc)
                def pass2(j, l8):
                    e = jnp.exp(st_s[j] - m)
                    acc[...] += tn(vblk(j), e.astype(bf16))
                    return l8 + jnp.sum(e.reshape(B // 8, 8, 2 * B), axis=0)
                l8 = lax.fori_loop(0, i + 1, pass2, jnp.zeros((8, 2 * B), f32))
                l = jnp.sum(l8, axis=0, keepdims=True)
            r = 1.0 / l
            a = acc[...] * r
            ot = jnp.concatenate([a[:64, :B], a[64:, B:]], axis=0)
            o_ref[qs, p * 128:(p + 1) * 128] = ot.T.astype(o_ref.dtype)
            lse = m + jnp.log(l)
            lse_ref[2 * p:2 * p + 1, qs] = lse[:, :B]
            lse_ref[2 * p + 1:2 * p + 2, qs] = lse[:, B:]
            return 0
        lax.fori_loop(0, nb, qstep, 0)

def attn_fwd(lengths, qkv, B=256, variant="online"):
    rows, w3 = qkv.shape; W = w3 // 3; pairs = W // 128; nb = rows // B
    return pl.pallas_call(functools.partial(fwd_t, B=B, pairs=pairs, variant=variant), name="attn_fwd",
        out_shape=(jax.ShapeDtypeStruct((rows, W), bf16), jax.ShapeDtypeStruct((8, rows), f32)),
        in_specs=[pl.BlockSpec(memory_space=pltpu.SMEM), pl.BlockSpec(memory_space=pltpu.VMEM)],
        out_specs=(pl.BlockSpec(memory_space=pltpu.VMEM),) * 2,
        scratch_shapes=[pltpu.VMEM((rows, 128), bf16), pltpu.VMEM((rows, 128), bf16), pltpu.VMEM((2 * B, 256), bf16),
                        pltpu.VMEM((nb if variant != "online" else 1, B, 2 * B), f32),
                        pltpu.VMEM((1, 2 * B), f32), pltpu.VMEM((1, 2 * B), f32), pltpu.VMEM((128, 2 * B), f32)],
        compiler_params=pltpu.CompilerParams(vmem_limit_bytes=56 << 20))(lengths, qkv)

def bwd_kernel(len_ref, qkv, do_ref, lse_ref, dl_ref, out, fq, fk, q2, do2, dq, dk, dv, *, B, pairs, mode):
    rows = qkv.shape[0]; nb = rows // B; W = pairs * 128
    doc_features(len_ref, rows, fq, fk)
    half = lax.broadcasted_iota(jnp.int32, (1, 128), 1) < 64
    causal = lax.broadcasted_iota(jnp.int32, (B, B), 0) <= lax.broadcasted_iota(jnp.int32, (B, B), 1)
    causal = jnp.concatenate([causal, causal], axis=1)
    for p in range(pairs):
        def prep(i, _, p=p):
            qs = pl.ds(pl.multiple_of(i * B, B), B)
            q = qkv[qs, p * 128:(p + 1) * 128] * bf16(0.125)
            d = do_ref[qs, p * 128:(p + 1) * 128]
            fqb = fq[qs, :]
            z = jnp.zeros_like(q)
            q2[i] = jnp.concatenate([
                jnp.concatenate([jnp.where(half, q, z), fqb], axis=1),
                jnp.concatenate([jnp.where(half, z, q), fqb], axis=1)], axis=0)
            do2[i] = jnp.concatenate([jnp.where(half, d, z), jnp.where(half, z, d)], axis=0)
            dq[i] = jnp.zeros(dq.shape[1:], f32)
            return 0
        lax.fori_loop(0, nb, prep, 0)
        def kstep(j, _, p=p):
            ks = pl.ds(pl.multiple_of(j * B, B), B)
            kt = qkv[ks, W + p * 128:W + (p + 1) * 128]
            v = qkv[ks, 2 * W + p * 128:2 * W + (p + 1) * 128]
            k2 = jnp.concatenate([kt, fk[ks, :]], axis=1)
            def block(i, masked, first):
                qs = pl.ds(pl.multiple_of(i * B, B), B)
                lse = jnp.concatenate([lse_ref[2 * p:2 * p + 1, qs], lse_ref[2 * p + 1:2 * p + 2, qs]], axis=1)
                dl = jnp.concatenate([dl_ref[2 * p:2 * p + 1, qs], dl_ref[2 * p + 1:2 * p + 2, qs]], axis=1)
                qq = q2[i]; dd = do2[i]
                st = nt(k2, qq)
                pt = jnp.exp(st - lse)
                if masked: pt = jnp.where(causal, pt, 0.0)
                dp = nt(v, dd)
                ds = (pt * (dp - dl)).astype(bf16)
                dvp = nn(pt.astype(bf16), dd)
                dkp = nn(ds, qq[:, :128])
                if first: dv[...] = dvp; dk[...] = dkp
                else: dv[...] += dvp; dk[...] += dkp
                if mode == "tn":
                    dq[i] += tn(ds, kt)
                else:
                    dq[i] += tn(kt, ds)
            block(j, True, True)
            def qstep(i, _):
                block(i, False, False); return 0
            lax.fori_loop(j + 1, nb, qstep, 0)
            out[ks, W + p * 128:W + (p + 1) * 128] = dk[...].astype(bf16)
            out[ks, 2 * W + p * 128:2 * W + (p + 1) * 128] = dv[...].astype(bf16)
            return 0
        lax.fori_loop(0, nb, kstep, 0)
        def fin(i, _, p=p):
            qs = pl.ds(pl.multiple_of(i * B, B), B)
            if mode == "tn":
                d = dq[i]
                r = jnp.where(half, d[:B], d[B:])
            else:
                d = dq[i]
                r = jnp.concatenate([d[:64, :B], d[64:, B:]], axis=0).T
            out[qs, p * 128:(p + 1) * 128] = (r * 0.125).astype(bf16)
            return 0
        lax.fori_loop(0, nb, fin, 0)

def attn_bwd(lengths, qkv, do, lse, dl, B=256, mode="tn"):
    rows, w3 = qkv.shape; W = w3 // 3; pairs = W // 128; nb = rows // B
    dqs = (nb, 2 * B, 128) if mode == "tn" else (nb, 128, 2 * B)
    return pl.pallas_call(functools.partial(bwd_kernel, B=B, pairs=pairs, mode=mode), name="attn_bwd",
        out_shape=jax.ShapeDtypeStruct((rows, w3), bf16),
        in_specs=[pl.BlockSpec(memory_space=pltpu.SMEM)] + [pl.BlockSpec(memory_space=pltpu.VMEM)] * 4,
        out_specs=pl.BlockSpec(memory_space=pltpu.VMEM),
        scratch_shapes=[pltpu.VMEM((rows, 128), bf16), pltpu.VMEM((rows, 128), bf16), pltpu.VMEM((nb, 2 * B, 256), bf16),
                        pltpu.VMEM((nb, 2 * B, 128), bf16), pltpu.VMEM(dqs, f32), pltpu.VMEM((B, 128), f32), pltpu.VMEM((B, 128), f32)],
        compiler_params=pltpu.CompilerParams(vmem_limit_bytes=56 << 20))(lengths, qkv, do, lse, dl)

def stats(v):
    n = v.shape[-1]
    m = jnp.sum(v, axis=-1, keepdims=True) * (1.0 / n)
    c = v - m
    s = jnp.sum(c * c, axis=-1, keepdims=True) * (1.0 / n)
    r = lax.rsqrt(s + EPS)
    return c * r, r
def ln_back(w, vh, r, g):
    n = vh.shape[-1]
    wg = w * g
    a = jnp.sum(wg, axis=-1, keepdims=True) * (1.0 / n)
    b = jnp.sum(wg * vh, axis=-1, keepdims=True) * (1.0 / n)
    return r * (wg - a - vh * b)
def colsum(v): return jnp.sum(v, axis=0, keepdims=True)


def gelu_parts(h):
    return 0.5 + 0.5 * lax.erf(h * 0.7071067811865476), jnp.exp2(h * h * -0.7213475204444817) * 0.3989422804014327

def ffn_kernel(vec, mid, sel, o_h, x_h, g_h, wo_h, fc1_h, fc2_h,
               delta_ref, gvec, gmid, gfc1, gfc2, out_ref, dy_h, do_h, gwo_h,
               o_ref, x_ref, g_ref, wo, fc1, fc2, dy_ref, do_ref, gwo,
               h_s, u_s, d_s, dm_s, m_s, dh_s, c_s, b_s, y_s, dc_s, st_s, ws, *, T, NT, NC, SR, UT):
    step = pl.program_id(0)
    rows = x_ref.shape[0]
    ff, D = fc1.shape
    K = ff // NC
    NS = NT // UT
    def parts(h, v, first, n):
        m = v.shape[0] // n
        return [pltpu.make_async_copy(h.at[k * m:(k + 1) * m, :], v.at[k * m:(k + 1) * m, :], ws.at[first + k]) for k in range(n)]
    early = parts(o_h, o_ref, 0, 2) + parts(wo_h, wo, 2, 1) + parts(x_h, x_ref, 3, 2)
    load1 = parts(fc1_h, fc1, 5, 6)
    load2 = parts(g_h, g_ref, 11, 2) + parts(fc2_h, fc2, 13, 6)
    outs = [pltpu.make_async_copy(v, h, ws.at[19 + k]) for k, (h, v) in enumerate(
        ((dy_h, dy_ref), (do_h, do_ref), (gwo_h, gwo)))]
    sg, sb, fg, fb = [vec[k:k + 1, :] for k in range(2, 6)]
    tiles = [slice(t * T, (t + 1) * T) for t in range(NT)]
    subs = [slice(r * SR, (r + 1) * SR) for r in range(T // SR)]
    cols = [slice(c * K, (c + 1) * K) for c in range(NC)]
    def fold(v):
        r = v[:, :128]
        for k in range(1, v.shape[1] // 128): r = r + v[:, k * 128:(k + 1) * 128]
        return r
    @pl.when(step == 0)
    def _():
        for l in early + load1 + load2: l.start()
        gvec[...] = jnp.zeros_like(gvec); gmid[...] = jnp.zeros_like(gmid)
        for l in early: l.wait()
        bs = []
        for sl in tiles:
            oh, _r = stats(o_ref[sl, :].astype(f32))
            b_s[sl, :] = (oh * sg + sb).astype(bf16)
        for sl in tiles:
            y_s[sl, :] = x_ref[sl, :].astype(f32) + nn(b_s[sl, :], wo[...])
        for sl in tiles:
            yh, _r = stats(y_s[sl, :])
            c_s[sl, :] = (yh * fg + fb).astype(bf16)
        for l in load1: l.wait()
    base = jnp.minimum(step, NS - 1) * T
    rs = pl.ds(pl.multiple_of(base, T), T)
    sub_rows = lambda s: pl.ds(pl.multiple_of(base + s.start, SR), SR)
    total = lambda k: jnp.sum(jnp.sum(st_s[k], axis=0), axis=1, keepdims=True) * (1.0 / ff)
    def moments():
        mu = total(0)
        return mu, lax.rsqrt(total(1) - mu * mu + EPS)
    @pl.when(step < NS)
    def _():
        h_s[0] = nt(c_s[rs, :], fc1[cols[0], :])
        for c in range(NC):
            for s in subs:
                h = h_s[c % 2, s, :]
                phi, den = gelu_parts(h)
                u = h * phi
                u_s[s, cols[c]] = u
                d_s[s, cols[c]] = phi + h * den
                st_s[0, c, s, :] = fold(u); st_s[1, c, s, :] = fold(u * u)
            if c + 1 < NC: h_s[(c + 1) % 2] = nt(c_s[rs, :], fc1[cols[c + 1], :])
    @pl.when(step == 0)
    def _():
        for l in load2: l.wait()
    @pl.when(step < NS)
    def _():
        mu, R = moments()
        dm_s[:, cols[0]] = nt(g_ref[rs, :], fc2[cols[0], :])
        for c in range(NC):
            gain = mid[0:1, cols[c]]; shift = mid[1:2, cols[c]]
            g6 = jnp.zeros((8, K), f32); g7 = jnp.zeros((8, K), f32)
            for s in subs:
                uh = (u_s[s, cols[c]] - mu[s]) * R[s]
                u_s[s, cols[c]] = uh
                m_s[sub_rows(s), cols[c]] = (uh * gain + shift).astype(bf16)
                dm = dm_s[s, cols[c]]
                e = dm * gain
                dm_s[s, cols[c]] = e
                q = dm * uh
                g6 += jnp.sum(q.reshape(SR // 8, 8, K), axis=0); g7 += jnp.sum(dm.reshape(SR // 8, 8, K), axis=0)
                st_s[2, c, s, :] = fold(e); st_s[3, c, s, :] = fold(e * uh)
            gmid[6:7, cols[c]] += colsum(g6)
            gmid[7:8, cols[c]] += colsum(g7)
            if c + 1 < NC: dm_s[:, cols[c + 1]] = nt(g_ref[rs, :], fc2[cols[c + 1], :])
    @pl.when(step < NS)
    def _():
        R = moments()[1]
        se = total(2); seu = total(3)
        for c in range(NC):
            for s in subs:
                dh = (dm_s[s, cols[c]] - se[s] - u_s[s, cols[c]] * seu[s]) * R[s] * d_s[s, cols[c]]
                dh_s[sub_rows(s), cols[c]] = dh.astype(bf16)
            if c == 0:
                out_ref[rs, :] = (y_s[rs, :] + nn(m_s[rs, :], fc2[...])).astype(bf16)
    @pl.when(step < NS)
    def _():
        dc_s[rs, :] = nn(dh_s[rs, :], fc1[...])
    def grads(lanes):
        gfc2[0] = tn(m_s[:, lanes], g_ref[...]).astype(bf16)
        gfc1[0] = tn(dh_s[:, lanes], c_s[...]).astype(bf16)
    @pl.when(step == NS)
    def _():
        hs = []
        for sl in tiles:
            yh, yr = stats(y_s[sl, :])
            dc = dc_s[sl, :]
            gvec[4:5, :] += colsum(dc * yh)
            gvec[5:6, :] += colsum(dc)
            dy_ref[sl, :] = (g_ref[sl, :].astype(f32) + ln_back(dc, yh, yr, fg)).astype(bf16)
        for sl in tiles:
            dc_s[sl, :] = nt(dy_ref[sl, :], wo[...])
        for sl in tiles:
            dbn = dc_s[sl, :]
            o = o_ref[sl, :].astype(f32)
            oh, orr = stats(o)
            gvec[2:3, :] += colsum(dbn * oh)
            gvec[3:4, :] += colsum(dbn)
            do = ln_back(dbn, oh, orr, sg).astype(bf16)
            do_ref[sl, :] = do
            pr = do.astype(f32) * o
            hi = pr.astype(bf16)
            lo = (pr - hi.astype(f32)).astype(bf16)
            delta_ref[:, sl] = nt(sel[...], hi) + nt(sel[...], lo)
        grads(cols[0])
        gwo[...] = tn(b_s[...], dy_ref[...]).astype(bf16)
        for c in outs: c.start()
    @pl.when(step > NS)
    def _():
        grads(pl.ds(pl.multiple_of((step - NS) * K, K), K))
    @pl.when(step == NS + NC - 1)
    def _():
        for c in outs: c.wait()

def ffn(o, x, g, wo, fc1, fc2, vec, mid, T=256, K=512, dt=f32, SR=16, UT=1):
    rows, D = x.shape; ff = fc1.shape[0]; NC = ff // K; NT = rows // T; NS = NT // UT
    head = np.arange(D)[None] // 64
    sel = jnp.asarray((np.arange(16)[:, None] == head // (D // 128) * 8 + head % (D // 128)).astype(np.float32), bf16)
    one = dict(pipeline_mode=pl.Buffered(1))
    full = lambda *s: pl.BlockSpec(s, lambda i: (0,) * len(s), **one)
    A = pl.BlockSpec(memory_space=pl.ANY)
    chunk = pl.BlockSpec((1, K, D), lambda s: (jnp.maximum(s - NS, 0), 0, 0))
    sds = jax.ShapeDtypeStruct
    M = pltpu.VMEM
    act = sds((rows, D), bf16)
    delta, gvec, gmid, g1, g2, out, dy, do, gwo = pl.pallas_call(functools.partial(ffn_kernel, T=T, NT=NT, NC=NC, SR=SR, UT=UT), name="ffn",
        grid=(NS + NC,),
        in_specs=[full(8, D), full(8, ff), full(16, D)] + [A] * 6,
        out_specs=[full(16, rows), full(8, D), full(8, ff), chunk, chunk, full(rows, D)] + [A] * 3,
        out_shape=[sds((16, rows), f32), sds((8, D), f32), sds((8, ff), f32), sds((NC, K, D), bf16), sds((NC, K, D), bf16),
                   act, act, act, sds((D, D), bf16)],
        scratch_shapes=[M((rows, D), bf16), M((D, D), bf16), M((rows, D), bf16)][:0] + [M((rows, D), bf16), M((rows, D), bf16), M((rows, D), bf16),
                        M((D, D), bf16), M((ff, D), bf16), M((ff, D), bf16), M((rows, D), bf16), M((rows, D), bf16), M((D, D), bf16),
                        M((2, T, K), f32), M((T, ff), f32), M((T, ff), f32), M((T, ff), f32),
                        M((rows, ff), bf16), M((rows, ff), bf16), M((rows, D), bf16), M((rows, D), bf16), M((rows, D), f32), M((rows, D), f32),
                        M((4, NC, T, 128), f32), pltpu.SemaphoreType.DMA((22,))],
        compiler_params=pltpu.CompilerParams(vmem_limit_bytes=63 << 20, dimension_semantics=("arbitrary",)))(
            vec, mid, sel, o, x, g, wo, fc1, fc2)
    return out, dy, do, delta, gwo, g1, g2, gvec, gmid

MESH = pl.DeviceIdType.MESH

def place():
    dp, tp = lax.axis_index("dp"), lax.axis_index("tp")
    q, z = dp % 4, dp // 4
    dx = 1 - 2 * (dp % 2)
    dy = 2 - 4 * ((dp // 2) % 2)
    a, b = (1 - tp) * dx + tp * dy, tp * dx + (1 - tp) * dy
    return dict(dp=dp, tp=tp, z=z, q=q, qa=q + a, qb=q + b, qab=q + a + b,
                a=(dp + a, tp), b=(dp + b, tp), peer=(dp, 1 - tp),
                zs=[((dp + 4 * k) % 16, tp) for k in (1, 2, 3)], zi=[(z + k) % 4 for k in (1, 2, 3)])

def enter(w):
    bar = pltpu.get_barrier_semaphore()
    for d in [w["a"], w["b"], w["peer"]] + w["zs"]:
        pl.semaphore_signal(bar, inc=1, device_id=d, device_id_type=MESH)
    pl.semaphore_wait(bar, 6)

class Copy:
    def __init__(self, ss, rs):
        self.ss, self.rs, self.n, self.all = ss, rs, 0, []
    def __call__(self, src, dst, dev):
        c = pltpu.make_async_remote_copy(src_ref=src, dst_ref=dst, send_sem=self.ss.at[self.n], recv_sem=self.rs.at[self.n],
                                         device_id=dev, device_id_type=MESH)
        self.n += 1
        self.all.append(c)
        return c

def go_all(cs):
    for c in cs: c.start()

def got(cs):
    for c in cs: c.wait_recv()

class Gather:
    def __init__(self, copy, w, src, slot, view, peer):
        q, qa, qb, qab = w["q"], w["qa"], w["qb"], w["qab"]
        own = slot(w["z"], q)
        far = [slot(z, q) for z in w["zi"]]
        self.z = [copy(src, own, d) for d in w["zs"]]
        self.a = [copy(src, own, w["a"])] + [copy(s, s, w["a"]) for s in far]
        self.b = [copy(src, own, w["b"])] + [copy(s, s, w["b"]) for s in far]
        self.ab = [copy(view(qa), view(qa), w["b"])]
        self.p = [copy(view(c), view(c), w["peer"]) for c in (q, qa, qb, qab)] if peer else []
    def start(self):
        go_all(self.z + self.a[:1] + self.b[:1])
    def after_z(self):
        got(self.z)
        for k in (1, 2, 3): go_all([self.a[k], self.b[k]])
        go_all(self.p[:1])
    def after_a(self):
        got(self.a)
        go_all(self.ab + self.p[1:2])
    def after_b(self):
        got(self.b + self.ab)
        go_all(self.p[2:])
    def finish(self):
        got(self.p)

N_COPIES = 112

def k12_kernel(len_ref, tok, wq, wos, vpk, e24, e96, rsel, fc1s, fc2s,
               o_out, lse_ref, vec, mid, xh_h, qkv_h, wown_h, wo_h, fc1_h, fc2_h,
               xh16, qkv, wown, afull, xp, vbuf, sb, rb, woc, o_loc, fq, fk, q2, m_s, l_s, acc, ss, rs, ls, *, B, pairs, stage=9):
    w = place()
    tp = w["tp"]
    rows, D = tok.shape
    W = pairs * 128
    send = Copy(ss, rs)
    first = tp == 0
    sb[...] = jnp.zeros_like(sb)
    pick = lambda c0, n: (jnp.where(first, wq[:, c0:c0 + W], wq[:, c0 + W:c0 + 2 * W]).astype(bf16),
                          jnp.where(first, wq[:, c0 + W:c0 + 2 * W], wq[:, c0:c0 + W]).astype(bf16))
    mine = []
    for k in range(3):
        own, oth = pick(k * D, W)
        mine.append(own); sb[0:24, k * W:(k + 1) * W] = oth
    own_o = jnp.where(first, wos[:, :W], wos[:, W:])
    sb[0:24, 3 * W:4 * W] = jnp.where(first, wos[:, W:], wos[:, :W])
    vbuf[w["z"], w["q"], tp] = vpk[...]
    loc = [pltpu.make_async_copy(fc1s, fc1_h.at[w["z"], w["q"], tp], ls.at[0]),
           pltpu.make_async_copy(fc2s, fc2_h.at[w["z"], w["q"], tp], ls.at[1])]
    for c in loc: c.start()
    enter(w)
    cpre = send(sb, rb, w["peer"])
    gv = Gather(send, w, vbuf.at[w["z"], w["q"], tp], lambda z, q: vbuf.at[z, q, tp], lambda q: vbuf.at[:, q, tp], True)
    cx = send(tok, xp, w["peer"])
    gq = [Gather(send, w, wown.at[p, w["z"], w["q"]], lambda z, q, p=p: wown.at[p, z, q], lambda q, p=p: wown.at[p, :, q], False)
          for p in range(pairs)]
    keep = [pltpu.make_async_copy(v, h, ls.at[3 + k]) for k, (v, h) in enumerate(((xh16, xh_h), (qkv, qkv_h), (wown, wown_h)))]
    cols = pl.ds(pl.multiple_of(tp * W, 128), W)
    go = Gather(send, w, woc, lambda z, q: wo_h.at[z, q, :, cols], lambda q: wo_h.at[:, q, :, cols], True)
    g1 = Gather(send, w, fc1s, lambda z, q: fc1_h.at[z, q, tp], lambda q: fc1_h.at[:, q, tp], True)
    g2 = Gather(send, w, fc2s, lambda z, q: fc2_h.at[z, q, tp], lambda q: fc2_h.at[:, q, tp], True)
    peer_rows = pl.ds(pl.multiple_of((1 - tp) * rows, rows), rows)
    co = [send(o_loc.at[peer_rows, p * 128:(p + 1) * 128],
               o_out.at[:, pl.ds(pl.multiple_of(tp * W + p * 128, 128), 128)], w["peer"]) for p in range(pairs)]
    cpre.start()
    gv.start()
    cx.start()
    cpre.wait_recv()
    other = rb[0:24, :].astype(f32)
    me = jnp.concatenate(mine + [own_o], axis=1).astype(f32)
    both = jnp.concatenate([jnp.where(first, me, other), jnp.where(first, other, me)], axis=0).astype(bf16)
    for p in range(pairs):
        for k in range(3):
            wown[p, w["z"], w["q"], :, k * 128:(k + 1) * 128] = both[:, k * W + p * 128:k * W + (p + 1) * 128]
    woc[...] = both[:, 3 * W:]
    gq[0].start()
    lw = pltpu.make_async_copy(woc, wo_h.at[w["z"], w["q"], :, cols], ls.at[2])
    lw.start()
    gv.after_z(); gv.after_a()
    gq[0].after_z()
    gq[1].start()
    gv.after_b(); gv.finish()
    small = nn(rsel[...], vbuf[...].reshape(512, 128)).astype(bf16)
    dev = lax.broadcasted_iota(jnp.int32, (32, 1), 0)
    def spread(v, e, n):
        lane = lax.broadcasted_iota(jnp.int32, (1, e.shape[1]), 1)
        hit = (lane >= dev * n) & (lane < dev * n + n)
        return colsum(jnp.where(hit, nn(small[v * 32:(v + 1) * 32], e[...]), 0.0))
    for v in range(2): vec[v:v + 1, :] = spread(v, e24, 24)
    gq[0].after_a()
    def normed(src, base):
        def body(r, _):
            sl = pl.ds(pl.multiple_of(r * 256, 256), 256)
            xh, _r = stats(src[sl, :].astype(f32))
            to = pl.ds(pl.multiple_of(base + r * 256, 256), 256)
            xh16[to, :] = xh.astype(bf16)
            afull[to, :] = (xh * vec[0:1, :] + vec[1:2, :]).astype(bf16)
            return 0
        lax.fori_loop(0, rows // 256, body, 0)
    normed(tok, tp * rows)
    gq[0].after_b()
    gq[1].after_z()
    gq[2].start()
    for c in loc: c.wait()
    lw.wait()
    go.start(); g1.start()
    cx.wait_recv()
    normed(xp, (1 - tp) * rows)
    keep[0].start()
    doc_features(len_ref, 2 * rows, fq, fk)
    def proj(p):
        def body(r, _):
            sl = pl.ds(pl.multiple_of(r * 512, 512), 512)
            qkv[sl, p * 3 * 128:(p + 1) * 3 * 128] = nn(afull[sl, :], wown[p].reshape(D, 3 * 128)).astype(bf16)
            return 0
        lax.fori_loop(0, 2 * rows // 512, body, 0)
    proj(0)
    gq[1].after_a(); gq[2].after_z()
    g2.start()
    for v in range(2, 6): vec[v:v + 1, :] = spread(v, e24, 24)
    vec[6:8, :] = jnp.zeros((2, D), f32)
    for v in range(2): mid[v:v + 1, :] = spread(6 + v, e96, 96)
    mid[2:8, :] = jnp.zeros((6, 4 * D), f32)
    nb = 2 * rows // B
    half = lax.broadcasted_iota(jnp.int32, (1, 128), 1) < 64
    causal = lax.broadcasted_iota(jnp.int32, (B, B), 0) <= lax.broadcasted_iota(jnp.int32, (B, B), 1)
    causal = jnp.concatenate([causal, causal], axis=1)
    def unit(u, _):
        p, i = u // nb, u % nb
        def at(k):
            def deco(f): pl.when(u == k)(f)
            return deco
        @at(1)
        def _():
            gq[1].after_b(); gq[2].after_a()
        @at(3)
        def _():
            gq[2].after_b()
            keep[2].start()
        @at(4)
        def _():
            co[0].start()
            go.after_z(); g1.after_z()
            proj(1)
        @at(6)
        def _():
            go.after_a(); g1.after_a(); g2.after_z()
        @at(7)
        def _():
            go.after_b()
        @at(8)
        def _():
            co[1].start()
            proj(2)
            keep[1].start()
            g1.after_b()
        @at(10)
        def _():
            g2.after_a()
        qs = pl.ds(pl.multiple_of(i * B, B), B)
        lanes = lambda k: pl.ds(pl.multiple_of(p * 384 + k * 128, 128), 128)
        q = qkv[qs, lanes(0)] * bf16(0.125)
        fqb = fq[qs, :]
        z = jnp.zeros_like(q)
        q2[...] = jnp.concatenate([
            jnp.concatenate([jnp.where(half, q, z), fqb], axis=1),
            jnp.concatenate([jnp.where(half, z, q), fqb], axis=1)], axis=0)
        def block(j, diag):
            ks = pl.ds(pl.multiple_of(j * B, B), B)
            s = nt(jnp.concatenate([qkv[ks, lanes(1)], fk[ks, :]], axis=1), q2[...])
            if diag: s = jnp.where(causal, s, -BIG)
            mn = jnp.max(s, axis=0, keepdims=True)
            if not diag:
                mo = m_s[...]
                mn = jnp.maximum(mo, mn); al = jnp.exp(mo - mn)
            e = jnp.exp(s - mn)
            su = jnp.sum(e, axis=0, keepdims=True)
            pv = tn(qkv[ks, lanes(2)], e.astype(bf16))
            if diag: l_s[...] = su; acc[...] = pv
            else: l_s[...] = l_s[...] * al + su; acc[...] = acc[...] * al + pv
            m_s[...] = mn
        block(i, True)
        def kstep(j, _):
            block(j, False); return 0
        lax.fori_loop(0, i, kstep, 0)
        l = l_s[...]
        a = acc[...] * (1.0 / l)
        ot = jnp.concatenate([a[:64, :B], a[64:, B:]], axis=0)
        o_loc[qs, pl.ds(pl.multiple_of(p * 128, 128), 128)] = ot.T.astype(bf16)
        lse = m_s[...] + jnp.log(l)
        lse_ref[p, 0:1, qs] = lse[:, :B]
        lse_ref[p, 1:2, qs] = lse[:, B:]
        return 0
    lax.fori_loop(0, pairs * nb, unit, 0)
    co[2].start()
    o_out[:, cols] = o_loc[pl.ds(pl.multiple_of(tp * rows, rows), rows), :]
    g2.after_b()
    got(co)
    go.finish(); g1.finish(); g2.finish()
    for c in send.all: c.wait_send()
    for c in keep: c.wait()

def consts_np(D):
    k = np.arange(128)[:, None]
    e24 = (np.arange(D)[None] % 24 == k).astype(np.float32)
    e96 = (np.arange(4 * D)[None] % 96 == k).astype(np.float32)
    r = np.arange(256)[:, None]
    rsel = (np.arange(512)[None] == (r % 32) * 16 + r // 32).astype(np.float32)
    return e24, e96, rsel

def consts(D):
    return [jnp.asarray(c, bf16) for c in consts_np(D)]

def k12(lengths, tok, wq, wos, vpk, fc1s, fc2s, B=512):
    rows, D = tok.shape
    W = D // 2; pairs = W // 128
    V, A = pl.BlockSpec(memory_space=pltpu.VMEM), pl.BlockSpec(memory_space=pl.ANY)
    sds = jax.ShapeDtypeStruct
    hid = fc1s.shape[0]
    return pl.pallas_call(functools.partial(k12_kernel, B=B, pairs=pairs), name="forward",
        out_shape=(sds((rows, D), bf16), sds((pairs, 2, 2 * rows), f32), sds((8, D), f32), sds((8, 4 * D), f32),
                   sds((2 * rows, D), bf16), sds((2 * rows, 3 * W), bf16), sds((pairs, 4, 4, 48, 3 * 128), bf16),
                   sds((4, 4, 48, D), bf16), sds((4, 4, 2, hid, D), bf16), sds((4, 4, 2, hid, D), bf16)),
        in_specs=[pl.BlockSpec(memory_space=pltpu.SMEM)] + [V] * 7 + [A] * 2,
        out_specs=(V,) * 4 + (A,) * 6,
        scratch_shapes=[pltpu.VMEM((2 * rows, D), bf16), pltpu.VMEM((2 * rows, 3 * W), bf16), pltpu.VMEM((pairs, 4, 4, 48, 3 * 128), bf16), pltpu.VMEM((2 * rows, D), bf16), pltpu.VMEM((rows, D), bf16), pltpu.VMEM((4, 4, 2, 16, 128), bf16), pltpu.VMEM((32, 4 * W), bf16), pltpu.VMEM((32, 4 * W), bf16),
                        pltpu.VMEM((48, W), bf16), pltpu.VMEM((2 * rows, W), bf16), pltpu.VMEM((2 * rows, 128), bf16), pltpu.VMEM((2 * rows, 128), bf16),
                        pltpu.VMEM((2 * B, 256), bf16), pltpu.VMEM((1, 2 * B), f32), pltpu.VMEM((1, 2 * B), f32), pltpu.VMEM((128, 2 * B), f32),
                        pltpu.SemaphoreType.DMA((N_COPIES,)), pltpu.SemaphoreType.DMA((N_COPIES,)), pltpu.SemaphoreType.DMA((6,))],
        compiler_params=pltpu.CompilerParams(vmem_limit_bytes=60 << 20, collective_id=0, has_side_effects=True))(
            lengths, tok, wq, wos, vpk, *consts(D), fc1s, fc2s)

def pack_vectors(six, two):
    n6 = jnp.pad(jnp.stack(six), ((0, 0), (0, 128 - six[0].shape[0])))
    n2 = jnp.pad(jnp.stack(two), ((0, 8), (0, 128 - two[0].shape[0])))
    return jnp.concatenate([n6, n2], axis=0)


def add(x, y):
    return (x.astype(f32) + y.astype(f32)).astype(x.dtype)

class Scatter:
    def __init__(self, copy, w, s, bb, ab, zb):
        self.w, self.s, self.bb, self.ab, self.zb = w, s, bb, ab, zb
        self.b = [copy(s.at[:, w["qb"]], bb.at[0], w["b"]), copy(s.at[:, w["qab"]], bb.at[1], w["b"])]
        self.a = [copy(s.at[:, w["qa"]], ab, w["a"])]
        self.z = [copy(s.at[w["zi"][k], w["q"]], zb.at[k], w["zs"][k]) for k in range(3)]
    def go(self, cs):
        for c in cs: c.start()
    def start(self):
        self.go(self.b)
    def after_b(self):
        for c in self.b: c.wait_recv()
        for z in range(4):
            self.s[z, self.w["qa"]] = add(self.s[z, self.w["qa"]], self.bb[1, z])
        self.go(self.a)
        for z in range(4):
            self.s[z, self.w["q"]] = add(self.s[z, self.w["q"]], self.bb[0, z])
    def after_a(self):
        for c in self.a: c.wait_recv()
        for z in range(4):
            self.s[z, self.w["q"]] = add(self.s[z, self.w["q"]], self.ab[z])
        self.go(self.z)
    def result(self):
        for c in self.z: c.wait_recv()
        r = self.s[self.w["z"], self.w["q"]].astype(f32)
        for k in range(3): r = r + self.zb[k].astype(f32)
        return r

def k45_kernel(len_ref, do, delta, lse_ref, vec, gvec, gmid, e24t, e96t, qkv_h, xh_h, wown_h, gwo_h, tok_h, dy_h, g1_h, g2_h,
               gtok, gq_o, gwo_o, g1_o, g2_o, small_o, pre_o,
               qkv, xh16, wown, gwo, tok, dy, do_own, dl_own, fq, fk, q2, do2, dq, dk, dv,
               s1, r1, b1, a1, z1, s2, r2, b2, a2, z2, so, ro, bo, ao, zo, *rest, B, pairs):
    flows, rest = rest[:4 * pairs], rest[4 * pairs:]
    (sm, pm, s4, bm, am, zm, da, dsend, drecv, fo, xo, fqk, xq, gcol, bcol, vacc, uacc, ss, rs, ls) = rest
    w = place()
    tp = w["tp"]
    rows, D = tok.shape
    W = pairs * 128
    nb = 2 * rows // B
    first = tp == 0
    other = 1 - tp
    mine_rows = pl.ds(pl.multiple_of(tp * rows, rows), rows)
    mine_cols = pl.ds(pl.multiple_of(tp * W, 128), W)
    other_cols = pl.ds(pl.multiple_of(other * W, 128), W)
    copy = Copy(ss, rs)
    c_do = copy(do.at[:, other_cols], do_own.at[mine_rows, :], w["peer"])
    c_dl = copy(delta.at[pl.ds(pl.multiple_of(other * 8, 8), 8), :], dl_own.at[:, mine_rows], w["peer"])
    c_r2 = copy(g2_h.at[:, :, other], r2, w["peer"])
    c_r1 = copy(g1_h.at[:, :, other], r1, w["peer"])
    c_ro = copy(gwo_h.at[:, other_cols], ro, w["peer"])
    f1, f2 = Scatter(copy, w, s1, b1, a1, z1), Scatter(copy, w, s2, b2, a2, z2)
    fo_ = Scatter(copy, w, so, bo, ao, zo)
    fqs = [Scatter(copy, w, *flows[4 * p:4 * p + 4]) for p in range(pairs)]
    fm = Scatter(copy, w, s4, bm, am, zm)
    c_pm = copy(sm.at[:, :, other], pm, w["peer"])
    hr = rows // 2
    c_da = [copy(dsend.at[pl.ds(k * hr, hr), :], drecv.at[pl.ds(k * hr, hr), :], w["peer"]) for k in range(2)]
    n = gq_o.shape[0]
    other_n = pl.ds(pl.multiple_of(other * n, 8), n)
    mine_n = pl.ds(pl.multiple_of(tp * n, 8), n)
    c_xo = copy(fo.at[other_n, :], xo, w["peer"])
    c_xq = copy(fqk.at[other_n, :], xq, w["peer"])
    l_q = pltpu.make_async_copy(qkv_h, qkv, ls.at[0])
    l_2 = pltpu.make_async_copy(g2_h.at[:, :, tp], s2, ls.at[1])
    l_1 = pltpu.make_async_copy(g1_h.at[:, :, tp], s1, ls.at[2])
    l_t = pltpu.make_async_copy(tok_h, tok, ls.at[3])
    l_y = pltpu.make_async_copy(dy_h, dy, ls.at[4])
    l_o = pltpu.make_async_copy(gwo_h, gwo, ls.at[5])
    l_x = pltpu.make_async_copy(xh_h, xh16, ls.at[6])
    l_w = [pltpu.make_async_copy(wown_h.at[p], wown.at[:, p * 384:(p + 1) * 384], ls.at[7 + p]) for p in range(pairs)]
    for l in [l_q, l_2, l_o, l_1, l_x] + l_w + [l_t, l_y]: l.start()
    enter(w)
    for c in (c_do, c_dl): c.start()
    do_own[mine_rows, :] = do[:, mine_cols]
    dl_own[:, mine_rows] = delta[pl.ds(pl.multiple_of(tp * 8, 8), 8), :]
    doc_features(len_ref, 2 * rows, fq, fk)
    dev = lax.broadcasted_iota(jnp.int32, (32, 1, 1), 0)
    def pieces(v, e, n):
        lane = lax.broadcasted_iota(jnp.int32, (1, 1, v.shape[1]), 2)
        hit = (lane >= dev * n) & (lane < dev * n + n)
        t = jnp.where(hit, v[None], 0.0).reshape(256, v.shape[1])
        hi = t.astype(bf16)
        return nn(hi, e) + nn((t - hi.astype(f32)).astype(bf16), e)
    early = pieces(gmid[...], e96t[...], 4 * D // 32) + pieces(gvec[...], e24t[...], D // 32)
    sm[...] = early.reshape(4, 4, 2, 8, 128)
    c_pm.start()
    gcol[...] = jnp.broadcast_to(vec[0:1, :], (128, D)).T
    bcol[...] = jnp.broadcast_to(vec[1:2, :], (128, D)).T
    vacc[...] = jnp.zeros_like(vacc); uacc[...] = jnp.zeros_like(uacc)
    l_q.wait()
    c_do.wait_recv(); c_dl.wait_recv()
    c_r2.start(); c_ro.start()

    half = lax.broadcasted_iota(jnp.int32, (1, 128), 1) < 64
    causal = lax.broadcasted_iota(jnp.int32, (B, B), 0) <= lax.broadcasted_iota(jnp.int32, (B, B), 1)
    causal = jnp.concatenate([causal, causal], axis=1)
    def grads(p):
        out = flows[4 * p]
        cs = [slice(p * 384 + k * 128, p * 384 + (k + 1) * 128) for k in range(3)]
        g = qkv[:, p * 384:(p + 1) * 384]
        t = tn(xh16[...], g)
        gsum = jnp.sum(g.astype(f32), axis=0, keepdims=True)
        for k in range(3):
            sl = slice(k * 128, (k + 1) * 128)
            wk = wown[:, cs[k]].astype(f32)
            tk, sk = t[:, sl], gsum[:, sl]
            out[:, :, :, sl] = (gcol[...] * tk + bcol[...] * sk).astype(bf16).reshape(4, 4, 48, 128)
            vacc[...] += tk * wk
            uacc[...] += sk * wk
        if p == pairs - 1:
            lane = lax.broadcasted_iota(jnp.int32, (1, 128), 1)
            e = jnp.where(lane == 0, jnp.sum(vacc[...], axis=1, keepdims=True), 0.0)
            e = jnp.where(lane == 1, jnp.sum(uacc[...], axis=1, keepdims=True), e)
            out[:, :, :, 384:512] = e.astype(bf16).reshape(4, 4, 48, 128)
    def unit(u, _):
        p, j = u // nb, u % nb
        lanes = lambda k: pl.ds(pl.multiple_of(p * 384 + k * 128, 128), 128)
        def at(k):
            def deco(f): pl.when(u == k)(f)
            return deco
        @at(1)
        def _():
            c_pm.wait_recv()
            for z in range(4):
                for k in range(4): s4[z, k] = sm[z, k, tp] + pm[z, k]
            fm.start()
            c_r2.wait_recv(); l_2.wait()
            c_r1.start()
            for z in range(4):
                for k in range(4): s2[z, k] = add(s2[z, k], r2[z, k])
            f2.start()
            c_ro.wait_recv(); l_o.wait()
            so[...] = add(gwo[:, mine_cols], ro[...]).reshape(so.shape)
            fo_.start()
        @at(2)
        def _():
            fm.after_b()
            c_r1.wait_recv(); l_1.wait()
            for z in range(4):
                for k in range(4): s1[z, k] = add(s1[z, k], r1[z, k])
        @at(3)
        def _():
            fm.after_a()
        @at(4)
        def _():
            l_x.wait()
            for l in l_w: l.wait()
            grads(0)
            f2.after_b(); fo_.after_b(); f1.start()
            small_o[...] = fm.result()
        @at(5)
        def _():
            fqs[0].start()
        @at(6)
        def _():
            fo_.after_a()
        @at(7)
        def _():
            f2.after_a(); fqs[0].after_b()
        @at(8)
        def _():
            grads(1)
            f1.after_b(); fqs[1].start()
        @at(9)
        def _():
            f1.after_a(); fqs[0].after_a()
            fo[...] = fo_.result()
            c_xo.start()
        @at(10)
        def _():
            fqs[1].after_b()
        @at(11)
        def _():
            fqs[1].after_a()
            g2_o[...] = f2.result()
        @pl.when(j == 0)
        def _():
            def prep(i, _):
                qs = pl.ds(pl.multiple_of(i * B, B), B)
                q = qkv[qs, lanes(0)] * bf16(0.125)
                d = do_own[qs, pl.ds(pl.multiple_of(p * 128, 128), 128)]
                fqb = fq[qs, :]
                z = jnp.zeros_like(q)
                q2[i] = jnp.concatenate([
                    jnp.concatenate([jnp.where(half, q, z), fqb], axis=1),
                    jnp.concatenate([jnp.where(half, z, q), fqb], axis=1)], axis=0)
                do2[i] = jnp.concatenate([jnp.where(half, d, z), jnp.where(half, z, d)], axis=0)
                dq[i] = jnp.zeros(dq.shape[1:], f32)
                return 0
            lax.fori_loop(0, nb, prep, 0)
        ks = pl.ds(pl.multiple_of(j * B, B), B)
        kt = qkv[ks, lanes(1)]
        v = qkv[ks, lanes(2)]
        k2 = jnp.concatenate([kt, fk[ks, :]], axis=1)
        def block(i, diag):
            qs = pl.ds(pl.multiple_of(i * B, B), B)
            lse = jnp.concatenate([lse_ref[p, 0:1, qs], lse_ref[p, 1:2, qs]], axis=1)
            d0 = pl.ds(2 * p, 1); d1 = pl.ds(2 * p + 1, 1)
            dl = jnp.concatenate([dl_own[d0, qs], dl_own[d1, qs]], axis=1)
            qq = q2[i]; dd = do2[i]
            pt = jnp.exp(nt(k2, qq) - lse)
            if diag: pt = jnp.where(causal, pt, 0.0)
            ds = (pt * (nt(v, dd) - dl)).astype(bf16)
            dvp = nn(pt.astype(bf16), dd)
            dkp = nn(ds, qq[:, :128])
            if diag: dv[...] = dvp; dk[...] = dkp
            else: dv[...] += dvp; dk[...] += dkp
            dq[i] += tn(ds, kt)
        block(j, True)
        def qstep(i, _):
            block(i, False); return 0
        lax.fori_loop(j + 1, nb, qstep, 0)
        qkv[ks, lanes(1)] = dk[...].astype(bf16)
        qkv[ks, lanes(2)] = dv[...].astype(bf16)
        @pl.when(j == nb - 1)
        def _():
            def fin(i, _):
                qs = pl.ds(pl.multiple_of(i * B, B), B)
                d = dq[i]
                qkv[qs, lanes(0)] = (jnp.where(half, d[:B], d[B:]) * 0.125).astype(bf16)
                return 0
            lax.fori_loop(0, nb, fin, 0)
        return 0
    lax.fori_loop(0, pairs * nb, unit, 0)
    grads(2)
    fqs[2].start()
    for k in range(2):
        sl = pl.ds(pl.multiple_of(other * rows + k * hr, hr), hr)
        dsend[k * hr:(k + 1) * hr, :] = nt(qkv[sl, :], wown[...]).astype(bf16)
        c_da[k].start()
    fqs[2].after_b()
    g1_o[...] = f1.result()
    for k in range(2):
        sl = pl.ds(pl.multiple_of(tp * rows + k * hr, hr), hr)
        da[k * hr:(k + 1) * hr, :] = nt(qkv[sl, :], wown[...])
        if k == 0: fqs[2].after_a()
    l_t.wait(); l_y.wait()
    for c in c_da: c.wait_recv()
    gain = vec[0:1, :]
    def fin(r, _):
        sl = pl.ds(pl.multiple_of(r * 256, 256), 256)
        d = da[sl, :] + drecv[sl, :].astype(f32)
        xh, xr = stats(tok[sl, :].astype(f32))
        gtok[sl, :] = (dy[sl, :].astype(f32) + ln_back(d, xh, xr, gain)).astype(bf16)
        return 0
    def collect(p):
        r = fqs[p].result()
        fqk[:, p * 384:(p + 1) * 384] = r[:, :384]
        if p == pairs - 1: fqk[:, pairs * 384:] = r[:, 384:]
    for p in range(pairs - 1): collect(p)
    lax.fori_loop(0, rows // 256, fin, 0)
    collect(pairs - 1)
    c_xq.start()
    c_xo.wait_recv()
    mine = fo[mine_n, :]
    gwo_o[:, :W] = jnp.where(first, mine, xo[...])
    gwo_o[:, W:] = jnp.where(first, xo[...], mine)
    c_xq.wait_recv()
    for p in range(pairs):
        for k in range(3):
            src = p * 384 + k * 128
            mine = fqk[mine_n, src:src + 128]
            oth = xq[:, src:src + 128]
            c0 = k * D + p * 128
            gq_o[:, c0:c0 + 128] = jnp.where(first, mine, oth)
            gq_o[:, c0 + W:c0 + W + 128] = jnp.where(first, oth, mine)
    pre_o[...] = fqk[mine_n, 3 * W:] + xq[:, 3 * W:]
    for c in copy.all: c.wait_send()

def k45(lengths, xh, wown, do, delta, lse, vec, gvec, gmid, gwo, qkv, tok, dy, g1, g2, B=512):
    rows, D = tok.shape
    W = D // 2; pairs = W // 128; nb = 2 * rows // B
    V, A = pl.BlockSpec(memory_space=pltpu.VMEM), pl.BlockSpec(memory_space=pl.ANY)
    sds = jax.ShapeDtypeStruct
    hid = g1.shape[3]
    M = pltpu.VMEM
    e24t, e96t = [c.T for c in consts_np(D)[:2]]
    def flow(r, c, t, lead=()):
        return [M(lead + (4, 4, r, c), t), M(lead + (2, 4, r, c), t), M(lead + (4, r, c), t), M(lead + (3, r, c), t)]
    fc = flow(hid, D, bf16)
    fc = [fc[0], M((4, 4, hid, D), bf16)] + fc[1:]
    wo = flow(48, W, bf16)
    wo = [wo[0], M((D, W), bf16)] + wo[1:]
    sm = flow(8, 128, f32)
    return pl.pallas_call(functools.partial(k45_kernel, B=B, pairs=pairs), name="backward",
        out_shape=(sds((rows, D), bf16), sds((D // 32, 3 * D), f32), sds((D // 32, D), f32), sds((hid, D), f32), sds((hid, D), f32), sds((8, 128), f32), sds((D // 32, 128), f32)),
        in_specs=[pl.BlockSpec(memory_space=pltpu.SMEM)] + [V] * 8 + [A] * 8,
        out_specs=(V,) * 7,
        scratch_shapes=[M((2 * rows, 3 * W), bf16), M((2 * rows, D), bf16), M((D, 3 * W), bf16), M((D, D), bf16), M((rows, D), bf16), M((rows, D), dy.dtype), M((2 * rows, W), bf16), M((8, 2 * rows), f32),
                        M((2 * rows, 128), bf16), M((2 * rows, 128), bf16), M((nb, 2 * B, 256), bf16), M((nb, 2 * B, 128), bf16), M((nb, 2 * B, 128), f32),
                        M((B, 128), f32), M((B, 128), f32)] + fc + fc + wo + flow(48, W, bf16) * (pairs - 1) + flow(48, W + 128, bf16) +
                       [M((4, 4, 2, 8, 128), f32), M((4, 4, 8, 128), f32)] + sm +
                       [M((rows, D), f32), M((rows, D), bf16), M((rows, D), bf16), M((48, W), f32), M((24, W), f32), M((48, 3 * W + 128), f32), M((24, 3 * W + 128), f32),
                        M((D, 128), f32), M((D, 128), f32), M((D, 128), f32), M((D, 128), f32),
                        pltpu.SemaphoreType.DMA((64,)), pltpu.SemaphoreType.DMA((64,)), pltpu.SemaphoreType.DMA((10,))],
        compiler_params=pltpu.CompilerParams(vmem_limit_bytes=63 << 20, collective_id=1, has_side_effects=True))(
            lengths, do, delta, lse, vec, gvec, gmid, jnp.asarray(e24t, bf16), jnp.asarray(e96t, bf16), qkv, xh, wown, gwo, tok, dy, g1, g2)

def local_fast(tokens, cotangent, lengths, qkv_weight, out_weight, pre_gain, pre_shift, sub_gain, sub_shift,
          ffn_gain, ffn_shift, fc1_weight, mid_gain, mid_shift, fc2_weight):
    rows, D = tokens.shape
    vpk = pack_vectors([pre_gain, pre_shift, sub_gain, sub_shift, ffn_gain, ffn_shift], [mid_gain, mid_shift])
    o, lse, vec, mid, xh16, qkv, wown, wo, fc1, fc2 = k12(lengths, tokens, qkv_weight, out_weight, vpk, fc1_weight, fc2_weight)
    block_out, dy, do, delta, gwo, g1, g2, gvec, gmid = ffn(o, tokens, cotangent, wo.reshape(D, D), fc1.reshape(4 * D, D), fc2.reshape(4 * D, D), vec, mid)
    shape = (4, 4, 2, fc1_weight.shape[0], D)
    gtok, gq, gwo, g1, g2, small, pre = k45(lengths, xh16, wown.reshape(3, D, 384), do, delta, lse, vec, gvec, gmid, gwo, qkv, tokens, dy, g1.reshape(shape), g2.reshape(shape))
    n, m = pre_gain.shape[0], mid_gain.shape[0]
    return (block_out, gtok, gq, gwo, pre[:, 0], pre[:, 1], small[2, :n], small[3, :n], small[4, :n], small[5, :n],
            g1, small[6, :m], small[7, :m], g2)

def norm(v):
    return stats(v)


def local_any(tokens, cotangent, lengths, qkv_weight, out_weight, pre_gain, pre_shift, sub_gain, sub_shift,
          ffn_gain, ffn_shift, fc1_weight, mid_gain, mid_shift, fc2_weight):
    rows, D = tokens.shape
    W = D // 2
    tp = lax.axis_index("tp")
    both = ("dp", "tp")
    gather = lambda a: lax.all_gather(a, both, axis=0, tiled=True)
    small = gather(jnp.stack([pre_gain, pre_shift, sub_gain, sub_shift, ffn_gain, ffn_shift], axis=1)).astype(f32).T
    mid = gather(jnp.stack([mid_gain, mid_shift], axis=1)).astype(f32).T
    wq = gather(qkv_weight)
    wo, fc1, fc2 = gather(out_weight), gather(fc1_weight), gather(fc2_weight)
    wown = lax.dynamic_index_in_dim(wq.reshape(D, 3, 2, W), tp, 2, keepdims=False).reshape(D, 3 * W)
    x = tokens.astype(f32)
    xh, xr = norm(x)
    a = (xh * small[0] + small[1]).astype(bf16)
    afull = lax.all_gather(a, "tp", axis=0, tiled=True)
    qkv = nn(afull, wown).astype(bf16)
    o_own, lse = attn_fwd(lengths, qkv, B=512)
    o = lax.all_to_all(o_own, "tp", 0, 1, tiled=True)
    vec = jnp.concatenate([small, jnp.zeros((2, D), f32)], axis=0)
    block_out, dy, do, delta, gwo, gfc1, gfc2, gvec, gmid = ffn(
        o, tokens, cotangent, wo, fc1, fc2, vec, jnp.concatenate([mid, jnp.zeros((6, 4 * D), f32)], axis=0))
    do_own = lax.all_to_all(do, "tp", 1, 0, tiled=True)
    dl_own = lax.all_to_all(delta, "tp", 0, 1, tiled=True)
    dqkv = attn_bwd(lengths, qkv, do_own, lse, dl_own, B=512)
    gq = tn(afull, dqkv)
    da = lax.psum_scatter(nt(dqkv, wown), "tp", scatter_dimension=0, tiled=True)
    grad_tokens = (dy.astype(f32) + ln_back(da, xh, xr, small[0])).astype(bf16)
    scatter = lambda v: lax.psum_scatter(v, both, scatter_dimension=0, tiled=True)
    gq = lax.psum_scatter(gq, "dp", scatter_dimension=0, tiled=True)
    n = gq.shape[0] // 2
    gq = lax.all_to_all(gq.reshape(2, n, 3, 1, W), "tp", 0, 3, tiled=True).reshape(n, 3 * D)
    small_grads = scatter(jnp.concatenate([jnp.stack([colsum(da * xh)[0], colsum(da)[0]]), gvec[2:6]], axis=0).T).T
    mid_grads = scatter(gmid[6:8].T).T
    gwo = scatter(gwo.astype(f32))
    gfc1 = scatter(gfc1.reshape(-1, D).astype(f32))
    gfc2 = scatter(gfc2.reshape(-1, D).astype(f32))
    return (block_out, grad_tokens, gq, gwo, small_grads[0], small_grads[1], small_grads[2], small_grads[3],
            small_grads[4], small_grads[5], gfc1, mid_grads[0], mid_grads[1], gfc2)


def local(*arrays):
    fits = lax.axis_size("dp") == 16 and lax.axis_size("tp") == 2
    return (local_fast if fits else local_any)(*arrays)


def solution(mesh):
    two, one = P(("dp", "tp"), None), P(("dp", "tp"))
    return jax.shard_map(
        local,
        mesh=mesh,
        in_specs=(two, two, P("dp", None), two, two, one, one, one, one, one, one, two, one, one, two),
        out_specs=(two, two, two, two, one, one, one, one, one, one, two, one, one, two),
        check_vma=False,
    )
```
